32 devices in a mesh: wide: 4 (over x, core), narrow: 8 (over z, y).
Axes of the slice: x: 2, y: 2, z: 4, core: 2. Of those that a mesh axis runs over, the one named last changes fastest.
Arguments:
- tokens: bfloat16 [4096, 1024], P('wide'), may hold values from -6 to 6
- scene_ids: int32 [4096], P('wide'), may hold values from 0 to 1, as said below
- norm1_gain: float32 [1024], replicated, may hold values from 0.25 to 1.75
- norm1_shift: float32 [1024], replicated, may hold values from -1.75 to 1.75
- qkv_weight: bfloat16 [1024, 3072], P(None, 'narrow'), may hold values from -0.1875 to 0.1875
- qv_bias: float32 [2048], P('narrow'), may hold values from -0.3125 to 0.3125
- out_weight: bfloat16 [1024, 1024], P('narrow'), may hold values from -4 to 4
- out_bias: float32 [1024], replicated, may hold values from -1.75 to 1.75
- norm2_gain: float32 [1024], replicated, may hold values from 0.25 to 1.75
- norm2_shift: float32 [1024], replicated, may hold values from -1.75 to 1.75
- up_weight: bfloat16 [1024, 4096], P(None, 'narrow'), may hold values from -0.1875 to 0.1875
- up_bias: float32 [4096], P('narrow'), may hold values from -1.75 to 1.75
- down_weight: bfloat16 [4096, 1024], P('narrow'), may hold values from -0.1875 to 0.1875
- down_bias: float32 [1024], replicated, may hold values from -1.75 to 1.75
- cotangent: bfloat16 [4096, 1024], P('wide'), may hold values from -6 to 6
Outputs:
- layer_output: bfloat16 [4096, 1024], P('wide')
- grad_tokens: bfloat16 [4096, 1024], P('wide')
- grad_norm1_gain: float32 [1024], P('wide')
- grad_norm1_shift: float32 [1024], P('wide')
- grad_qkv_weight: float32 [1024, 3072], P('wide', 'narrow')
- grad_qv_bias: float32 [8, 256], P('narrow', 'wide')
- grad_out_weight: float32 [1024, 1024], P('narrow', 'wide')
- grad_out_bias: float32 [1024], P('wide')
- grad_norm2_gain: float32 [1024], P('wide')
- grad_norm2_shift: float32 [1024], P('wide')
- grad_up_weight: float32 [1024, 4096], P('wide', 'narrow')
- grad_up_bias: float32 [8, 512], P('narrow', 'wide')
- grad_down_weight: float32 [4096, 1024], P('narrow', 'wide')
- grad_down_bias: float32 [1024], P('wide')
The draws below stay inside these ranges and needn't reach their ends.
Inputs may be any that keep to these rules, and one draw needn't show every extreme that they name: `scene_ids`: two scenes, 0 and 1, each of 2 * (512) tokens or more.
All inputs are finite; a program needn't handle non-finite values.
Results may differ from the reference program's by a relative error of at most 0.023.
Values may be sent and summed in bfloat16 or wider, within the bound.
No kernel may reach another device: no remote copies, remote signals or barrier semaphores. Data moves between devices by JAX's collectives and lax.ppermute only.
A program may use at most 128 MiB of HBM per device.

```python
import math
from functools import partial
import jax
import jax.numpy as jnp
from jax import lax

HEADS = 16
HEAD_DIM = 64
D = 1024
FF = 4096
TOKENS = 4096
N_NARROW = 8


def draw_scene_ids(key, part):
    key = jax.random.fold_in(key, 11)
    first_key, second_key, label_key = jax.random.split(key, 3)
    eighth = TOKENS // 8
    first_cut = jax.random.randint(first_key, (), eighth, 3 * eighth)
    second_cut = jax.random.randint(second_key, (), 5 * eighth, 7 * eighth + 1)
    spanning = jax.random.randint(label_key, (), 0, 2)
    places = jnp.arange(TOKENS, dtype=jnp.int32)
    inner = (places >= first_cut) & (places < second_cut)
    return jnp.where(inner, 1 - spanning, spanning).astype(jnp.int32)


def levels(key, dims, cuts, smallest, largest):
    loudness = 1.0
    for dim, shards_of in cuts:
        heights = jax.random.uniform(jax.random.fold_in(jax.random.fold_in(key, 6), dim), (shards_of,), jnp.float32, smallest / len(cuts), largest / len(cuts))
        loudness = loudness * jnp.repeat(jnp.exp(heights), dims[dim] // shards_of).reshape((-1,) + (1,) * (len(dims) - 1 - dim))
    return loudness


def noise(stream_key, extent, scale, bound, cuts=(), held_as=jnp.bfloat16):
    array = jax.random.normal(stream_key, extent, jnp.float32) * scale
    if len(cuts) > 0:
        array = levels(stream_key, extent, cuts, -0.22, 0.18) * array
    return jnp.clip(array, min=-bound, max=bound).astype(held_as)


def setup_inputs(seed: int = 0) -> dict:
    splits = jax.random.split(jax.random.key(seed), 16)
    tokens = noise(splits[0], (TOKENS, D), 1.0, 6.0, ((0, 4),))
    scene_ids = draw_scene_ids(jax.random.fold_in(splits[15], 71), 0)
    norm1_gain = jnp.clip(1.0 + 0.15 * jax.random.normal(splits[2], (D,), jnp.float32), 0.25, 1.75)
    norm1_shift = noise(splits[3], (D,), 0.3, 1.75, (), jnp.float32)
    qkv_weight = noise(splits[4], (D, 3 * D), D ** -0.5, 0.1875, ((1, 8),))
    qv_bias = noise(splits[5], (2 * D,), 0.05, 0.3125, ((0, 8),), jnp.float32)
    out_weight = noise(splits[6], (D, D), (max(1, 8 * D // TOKENS)) ** -0.5, 4.0, ((0, 8),))
    out_bias = noise(splits[7], (D,), 0.3, 1.75, (), jnp.float32)
    norm2_gain = jnp.clip(1.0 + 0.15 * jax.random.normal(splits[8], (D,), jnp.float32), 0.25, 1.75)
    norm2_shift = noise(splits[9], (D,), 0.3, 1.75, (), jnp.float32)
    up_weight = noise(splits[10], (D, FF), D ** -0.5, 0.1875, ((1, 8),))
    up_bias = noise(splits[11], (FF,), 0.3, 1.75, ((0, 8),), jnp.float32)
    down_weight = noise(splits[12], (FF, D), (FF // 4) ** -0.5, 0.1875, ((0, 8),))
    down_bias = noise(splits[13], (D,), 0.3, 1.75, (), jnp.float32)
    cotangent = noise(splits[14], (TOKENS, D), 1.0, 6.0, ((0, 4),))
    return {"tokens": tokens, "scene_ids": scene_ids, "norm1_gain": norm1_gain, "norm1_shift": norm1_shift, "qkv_weight": qkv_weight, "qv_bias": qv_bias, "out_weight": out_weight, "out_bias": out_bias, "norm2_gain": norm2_gain, "norm2_shift": norm2_shift, "up_weight": up_weight, "up_bias": up_bias, "down_weight": down_weight, "down_bias": down_bias, "cotangent": cotangent}


@jax.custom_vjp
def low(v):
    return lax.optimization_barrier(v.astype(jnp.bfloat16)).astype(jnp.float32)

@jax.custom_vjp
def low_back(v):
    return v

def low_keep(v):
    return (low(v), None)

def low_pass(kept, grad):
    return (grad,)

def back_keep(v):
    return (v, None)

def back_low(kept, grad):
    return (low(grad),)
low.defvjp(low_keep, low_pass)
low_back.defvjp(back_keep, back_low)
EPSILON = 1e-05
MASKED = -1e+30
HIGHEST = lax.Precision.HIGHEST

def norm_rows(values, gain_vector, offset):
    centre = lax.optimization_barrier(jnp.mean(values, axis=-1, keepdims=True))
    centred = values - centre
    spread = lax.optimization_barrier(jnp.mean(centred * centred, axis=-1, keepdims=True))
    return centred * lax.rsqrt(spread + EPSILON) * gain_vector + offset

def layer(scene_ids, tokens, norm1_gain, norm1_shift, qkv_weight, qv_bias, out_weight, out_bias, norm2_gain, norm2_shift, up_weight, up_bias, down_weight, down_bias):
    total_rows = tokens.shape[0]
    factor = HEAD_DIM ** (-0.5)
    normed = low(norm_rows(tokens, norm1_gain, norm1_shift))
    projected = jnp.dot(normed, qkv_weight, precision=HIGHEST).reshape(total_rows, HEADS, 3, HEAD_DIM)
    bias_pair = qv_bias.reshape(HEADS, 2, HEAD_DIM)
    queries = low_back(low(projected[:, :, 0] + bias_pair[:, 0]))
    keys_all = low_back(low(projected[:, :, 1]))
    values_all = low_back(low(projected[:, :, 2] + bias_pair[:, 1]))
    block_rows = math.gcd(total_rows, 256)

    def attend(pieces):
        query_block, id_block = pieces
        logits = low_back(jnp.einsum('qhd,khd->hqk', query_block, keys_all, precision=HIGHEST) * factor)
        same_scene = (id_block[:, None] == scene_ids[None, :])[None]
        weights = low(jax.nn.softmax(jnp.where(same_scene, logits, MASKED), axis=-1))
        return jnp.einsum('hqk,khd->qhd', weights, values_all, precision=HIGHEST)
    mixed = lax.map(jax.checkpoint(attend), (queries.reshape(-1, block_rows, HEADS, HEAD_DIM), scene_ids.reshape(-1, block_rows)))
    mixed = low_back(low(mixed.reshape(total_rows, HEADS * HEAD_DIM)))
    residual = tokens + low_back(jnp.dot(mixed, out_weight, precision=HIGHEST)) + out_bias
    normed2 = low(norm_rows(residual, norm2_gain, norm2_shift))
    hidden = low_back(jnp.dot(normed2, up_weight, precision=HIGHEST) + up_bias)
    active = low(jax.nn.gelu(hidden))
    return residual + jnp.dot(active, down_weight, precision=HIGHEST) + down_bias

def reference(tokens, scene_ids, norm1_gain, norm1_shift, qkv_weight, qv_bias, out_weight, out_bias, norm2_gain, norm2_shift, up_weight, up_bias, down_weight, down_bias, cotangent):
    floats = tuple((item.astype(jnp.float32) for item in (tokens, norm1_gain, norm1_shift, qkv_weight, qv_bias, out_weight, out_bias, norm2_gain, norm2_shift, up_weight, up_bias, down_weight, down_bias)))
    output, pull = jax.vjp(partial(layer, scene_ids), *floats)
    grads = pull(cotangent.astype(jnp.float32))
    return (output.astype(jnp.bfloat16), grads[0].astype(jnp.bfloat16), grads[1], grads[2], grads[3], grads[4].reshape(N_NARROW, -1), grads[5], grads[6], grads[7], grads[8], grads[9], grads[10].reshape(N_NARROW, -1), grads[11], grads[12])
```

```python
import functools

import jax
import jax.numpy as jnp
from jax import lax
from jax.experimental import pallas as pl
from jax.experimental.pallas import tpu as pltpu
from jax.sharding import PartitionSpec as P

HEAD_DIM = 64
EPSILON = 1e-05
BIG = 2.0**100
SAFE = 40.0
ONE = 2
NT = (((1,), (1,)), ((), ()))
NN = (((1,), (0,)), ((), ()))
TN = (((0,), (0,)), ((), ()))
VMEM = pl.BlockSpec(memory_space=pltpu.VMEM)
PARAMS = pltpu.CompilerParams(vmem_limit_bytes=56 * 1024 * 1024)
F32 = jnp.float32
BF16 = jnp.bfloat16


def mm(a, b, dims=NN):
    return lax.dot_general(a, b, dims, preferred_element_type=F32)


def slot(at, size):
    return pl.ds(pl.multiple_of(at, size), size)


def shape(dims, dtype):
    return jax.ShapeDtypeStruct(dims, dtype)


def unit_rows(values):
    centre = jnp.mean(values, axis=-1, keepdims=True)
    centred = values - centre
    spread = jnp.mean(centred * centred, axis=-1, keepdims=True)
    scale = lax.rsqrt(spread + EPSILON)
    return centred * scale, scale


def norm_back(grad, unit, scale):
    first = jnp.mean(grad, axis=-1, keepdims=True)
    second = jnp.mean(grad * unit, axis=-1, keepdims=True)
    return (grad - first - unit * second) * scale


def gelu_parts(v):
    c = 0.7978845608028654
    square = v * v
    t = jnp.tanh(c * (v + 0.044715 * (v * square)))
    value = 0.5 * v * (1.0 + t)
    slope = 0.5 * (1.0 + t) + 0.5 * v * (1.0 - t * t) * (c * (1.0 + 3 * 0.044715 * square))
    return value, slope


def split3(v):
    a = v.astype(BF16)
    rest = v - a.astype(F32)
    b = rest.astype(BF16)
    return a, b, (rest - b.astype(F32)).astype(BF16)


def id_features(id_rows, start, change):
    n = id_rows.shape[0]
    row = lax.broadcasted_iota(jnp.int32, (128, 128), 0)
    lane = lax.broadcasted_iota(jnp.int32, (128, 128), 1)
    ones = jnp.ones((128, 128), BF16)
    out = []
    for c in range(n):
        spread = jnp.broadcast_to(id_rows[c : c + 1], (128, 128))
        own = jnp.where(row == lane, spread, 0.0).astype(BF16)
        ids = mm(own, ones)
        first, second = start
        up, down = change
        rest = 1.0 if first != 0.0 else 0.0
        feature = jnp.where(
            lane == 0, first + up * ids, jnp.where(lane == 1, second + down * ids, rest)
        )
        out.append(feature.astype(BF16))
    return jnp.concatenate(out, axis=0)


def key_features(id_rows):
    return id_features(id_rows, (-BIG, 0.0), (BIG, -BIG))


def query_features(id_rows):
    return id_features(id_rows, (0.0, 1.0), (1.0, -1.0))


def project_kernel(hh, T, blk, tok, gain, shift, w, bias, idr, normed, q_out, kvx, most):
    i = pl.program_id(0)

    @pl.when(i == 0)
    def _():
        most[...] = jnp.zeros_like(most)
        kvx[hh * T :, :] = idr[...]

    unit, _ = unit_rows(tok[...].astype(F32))
    low = (unit * gain[...] + shift[...]).astype(BF16)
    normed[...] = low
    proj = mm(low, w[...]) + bias[...]
    for h in range(hh):
        part = proj[:, h * 192 : h * 192 + 192].astype(BF16)
        q = part[:, :64] * BF16(0.125)
        kv = part[:, 64:]
        q_out[h] = jnp.concatenate([q, jnp.zeros((blk, 64), BF16)], axis=1)
        kvx[slot(h * T + i * blk, blk), :] = kv
        k32 = part[:, 64:128].astype(F32)
        q32 = q.astype(F32)
        most[0:1] = jnp.maximum(most[0:1], jnp.max(jnp.sum(k32 * k32, axis=1)))
        most[1:2] = jnp.maximum(most[1:2], jnp.max(jnp.sum(q32 * q32, axis=1)))

    @pl.when(i == T // blk - 1)
    def _():
        rows = hh * T + idr.shape[0]
        row = lax.broadcasted_iota(jnp.int32, (16, 128), 0)
        tops = jnp.where(row == 0, most[0:1], jnp.where(row == 1, most[1:2], 0.0))
        kvx[rows - 16 :, :] = (tops * 1.02).astype(BF16)


def project(tokens, gain, shift, w, bias, id_rows, hh):
    T, D = tokens.shape
    blk = min(256, T)
    extra = id_rows.shape[0]
    whole = lambda *dims: pl.BlockSpec(dims, lambda i: (0,) * len(dims))
    return pl.pallas_call(
        functools.partial(project_kernel, hh, T, blk),
        grid=(T // blk,),
        in_specs=[
            pl.BlockSpec((blk, D), lambda i: (i, 0)),
            whole(1, D),
            whole(1, D),
            whole(D, 192 * hh),
            whole(1, 192 * hh),
            whole(extra, 128),
        ],
        out_specs=[
            pl.BlockSpec((blk, D), lambda i: (i, 0)),
            pl.BlockSpec((hh, blk, 128), lambda i: (0, i, 0)),
            whole(hh * T + extra, 128),
        ],
        out_shape=[
            shape((T, D), BF16),
            shape((hh, T, 128), BF16),
            shape((hh * T + extra, 128), BF16),
        ],
        scratch_shapes=[pltpu.VMEM((8, 128), F32)],
        compiler_params=PARAMS,
        name="project",
    )(tokens, gain, shift, w, bias, id_rows)


def scene_rows(ref, tail, count):
    return ref[tail : tail + count + -count % 16, :].astype(F32)[:count]


def ranges(ids, per, out, at):
    for j in range(ids.shape[0] // per):
        part = ids[j * per : (j + 1) * per]
        out[at + 2 * j] = jnp.min(part)
        out[at + 2 * j + 1] = jnp.max(part)


def attend_kernel(hh, T, nb, bq, bk, first, last, mine, q_ref, *refs):
    kvs = refs[:nb]
    refs = refs[nb:]
    if not first:
        acc_in, m_in = refs[:2]
        refs = refs[2:]
    if last:
        mixed, mix32, feat = refs[:3]
        refs = refs[3:]
    else:
        acc_out, m_out = refs[:2]
        refs = refs[2:]
    acc_sc, m_sc, qf_sc, kf_sc, spans, qspans = refs
    trows = T // 128
    tail = hh * T
    ids = scene_rows(mine, tail, trows)
    ranges(ids, bq // 128, qspans, 0)
    qf_sc[...] = query_features(ids)
    top_q = jnp.max(mine[-16:, :].astype(F32)[1:2])
    top_k = 0.0
    for b in range(nb):
        ids = scene_rows(kvs[b], tail, trows)
        ranges(ids, bk // 128, spans, b * 2 * (T // bk))
        kf_sc[b] = key_features(ids)
        top_k = jnp.maximum(top_k, jnp.max(kvs[b][-16:, :].astype(F32)[0:1]))
    calm = top_q * top_k < SAFE * SAFE
    if not first:
        acc_sc[...] = acc_in[...]
        calm = calm & (jnp.max(m_in[...]) == 0.0) & (jnp.min(m_in[...]) == 0.0)
    else:
        acc_sc[...] = jnp.zeros_like(acc_sc)

    def hit(i, b, j):
        s = (b * (T // bk) + j) * 2
        return (qspans[2 * i] <= spans[s + 1]) & (spans[s] <= qspans[2 * i + 1])

    m_sc[...] = jnp.zeros_like(m_sc)

    def block(b, h, j):
        rows = slot(h * T + j * bk, bk)
        return jnp.concatenate([kvs[b][rows, :], kf_sc[b, slot(j * bk, bk), :]], axis=1)

    @pl.when(jnp.logical_not(calm))
    def _():
        m_sc[...] = jnp.full(m_sc.shape, -2.0 * BIG, F32)

        def step(n, carry):
            i, j = n // (T // bk), n % (T // bk)
            qr = slot(i * bq, bq)
            for b in range(nb):
                for h in range(hh):
                    q = jnp.concatenate([q_ref[h, qr, :], qf_sc[qr, :]], axis=1)
                    s = mm(q, block(b, h, j), NT)
                    m = jnp.max(s, axis=1, keepdims=True).astype(BF16).astype(F32)
                    m_sc[h, qr, :] = jnp.maximum(m_sc[h, qr, :], m)
            return carry

        lax.fori_loop(0, (T // bq) * (T // bk), step, 0)
        if not first:
            m_new = jnp.maximum(m_sc[...], m_in[...])
            keep = jnp.exp(m_in[...] - m_new)
            for h in range(hh):
                acc_sc[h] = acc_sc[h] * jnp.concatenate([keep[h], keep[h]], axis=1)
            m_sc[...] = m_new

    lane = lax.broadcasted_iota(jnp.int32, (bq, 128), 1)

    def per_query(i, carry):
        qr = slot(i * bq, bq)
        qs = []
        for h in range(hh):
            feature = jnp.where(lane == ONE, (-m_sc[h, qr, :]).astype(BF16), qf_sc[qr, :])
            qs.append(jnp.concatenate([q_ref[h, qr, :], feature], axis=1))
        for b in range(nb):

            def per_key(j, carry):
                @pl.when(hit(i, b, j))
                def _():
                    for h in range(hh):
                        kv = block(b, h, j)
                        p = jnp.exp(mm(qs[h], kv, NT)).astype(BF16)
                        acc_sc[h, qr, :] += mm(p, kv)

                return carry

            lax.fori_loop(0, T // bk, per_key, 0)
        return carry

    lax.fori_loop(0, T // bq, per_query, 0)
    if not last:
        acc_out[...] = acc_sc[...]
        m_out[...] = m_sc[...]
        return
    lanes = lax.broadcasted_iota(jnp.int32, (T, 128), 1)
    parts = []
    for h in range(hh):
        acc = acc_sc[h]
        total = acc[:, 128 + ONE : 129 + ONE]
        mix = acc[:, :128] / total
        mix32[h] = mix
        parts.append(mix[:, 64:])
        a, b, c = split3(-(m_sc[h] + jnp.log(total)))
        feat[h] = jnp.where(
            lanes == 2, a, jnp.where(lanes == 3, b, jnp.where(lanes == 4, c, qf_sc[...]))
        )
    whole = jnp.concatenate(parts, axis=1) if hh > 1 else parts[0]
    mixed[...] = whole.astype(BF16)


def attend(hh, mine, q, kvs, before, last):
    T = q.shape[1]
    nb = len(kvs)
    bq = min(512, T)
    bk = min(1024, T)
    first = before is None
    if last:
        outs = [
            shape((T, hh * 64), BF16),
            shape((hh, T, 128), F32),
            shape((hh, T, 128), BF16),
        ]
    else:
        outs = [shape((hh, T, 256), F32), shape((hh, T, 128), F32)]
    return pl.pallas_call(
        functools.partial(attend_kernel, hh, T, nb, bq, bk, first, last),
        in_specs=[VMEM] * (2 + nb + (0 if first else 2)),
        out_specs=[VMEM] * len(outs),
        out_shape=outs,
        scratch_shapes=[
            pltpu.VMEM((hh, T, 256), F32),
            pltpu.VMEM((hh, T, 128), F32),
            pltpu.VMEM((T, 128), BF16),
            pltpu.VMEM((nb, T, 128), BF16),
            pltpu.SMEM((nb * 2 * (T // bk),), F32),
            pltpu.SMEM((2 * (T // bq),), F32),
        ],
        compiler_params=PARAMS,
        name="attend",
    )(mine, q, *kvs, *(before or ()))


def middle_kernel(
    hidden_here, zb, mix, tok, cot, wo, up_own, dn_own, b_own, far, near, bo, g2, s2,
    a_out, rff, normed2, res, sums,
):
    i = pl.program_id(0)
    n = mix.shape[0]
    D = tok.shape[-1]
    rows = tok.shape[0] * tok.shape[2]
    mixed = jnp.concatenate([mix[s].reshape(rows, mix.shape[-1]) for s in range(n)], axis=1)
    x = tok[...].reshape(rows, D).astype(F32)
    g = cot[...].reshape(rows, D)
    residual = x + mm(mixed, wo[...]) + bo[...]
    unit, scale = unit_rows(residual)
    low = (unit * g2[...] + s2[...]).astype(BF16)
    res[...] = residual.reshape(res.shape)
    normed2[...] = low.reshape(normed2.shape)
    half = hidden_here // 2
    ff = jnp.zeros((rows, D), F32)
    gn = jnp.zeros((rows, D), F32)
    for piece in range(3):
        if piece == 0:
            up, up_dims, back_dims = up_own[...], NN, NT
            dn = dn_own[...]
            bias = b_own[...]
        else:
            pack = (far, near)[piece - 1]
            up, up_dims, back_dims = pack[:half, :], NT, NN
            dn = pack[half : 2 * half, :]
            tail = pack[2 * half :, :].astype(F32)
            bias = tail[0:1, :half] + tail[1:2, :half]
        value, slope = gelu_parts(mm(low, up, up_dims) + bias)
        grad = (mm(g, dn, NT) * slope).astype(BF16)
        ff += mm(value.astype(BF16), dn)
        gn += mm(grad, up, back_dims)
    back = norm_back(gn * g2[...], unit, scale)
    back_low = back.astype(BF16)
    rff[:, :, :D] = back_low.reshape(rff.shape[0], rff.shape[1], D)
    rff[:, :, D:] = ff.astype(BF16).reshape(rff.shape[0], rff.shape[1], D)
    a = mm(back_low, wo[...], NT).astype(BF16)
    c = a_out.shape[-1]
    for s in range(n):
        a_out[s] = a[:, s * c : (s + 1) * c].reshape(a_out.shape[1:])

    @pl.when(i == 0)
    def _():
        sums[...] = jnp.zeros_like(sums)

    sums[0:1] += jnp.sum(gn * unit, axis=0, keepdims=True)
    sums[1:2] += jnp.sum(gn, axis=0, keepdims=True)


def middle(mix, tok, cot, wo, up_own, dn_own, b_own, far, near, bo, g2, s2, half):
    n, zs, tn, c = mix.shape
    D = wo.shape[1]
    U = up_own.shape[1]
    zb = max(1, zs // 2)
    const = lambda a: pl.BlockSpec(a.shape, lambda i, y: (0,) * a.ndim)
    rows = pl.BlockSpec((zb, tn, D), lambda i, y: (i, 0, 0))
    split = pl.BlockSpec((zb, None, tn, D), lambda i, y: (i, y[0], 0, 0))

    def kernel(y_ref, mix, tok, cot, *rest):
        middle_kernel(U, zb, mix, _Row(tok), _Row(cot), *rest)

    return pl.pallas_call(
        kernel,
        grid_spec=pltpu.PrefetchScalarGridSpec(
            num_scalar_prefetch=1,
            grid=(zs // zb,),
            in_specs=[
                pl.BlockSpec((n, zb, tn, c), lambda i, y: (0, i, 0, 0)),
                split,
                split,
            ]
            + [const(a) for a in (wo, up_own, dn_own, b_own, far, near, bo, g2, s2)],
            out_specs=[
                pl.BlockSpec((n, zb, tn, c), lambda i, y: (0, i, 0, 0)),
                pl.BlockSpec((zb, tn, 2 * D), lambda i, y: (i, 0, 0)),
                rows,
                rows,
                pl.BlockSpec((8, D), lambda i, y: (0, 0)),
            ],
        ),
        out_shape=[
            shape((n, zs, tn, c), BF16),
            shape((zs, tn, 2 * D), BF16),
            shape((zs, tn, D), BF16),
            shape((zs, tn, D), F32),
            shape((8, D), F32),
        ],
        compiler_params=PARAMS,
        name="middle",
    )(half, mix, tok, cot, wo, up_own, dn_own, b_own, far, near, bo, g2, s2)


class _Row:
    def __init__(self, ref):
        self.ref = ref
        self.shape = (ref.shape[0], 1, ref.shape[1], ref.shape[2])

    def __getitem__(self, at):
        return self.ref[at]


def gather_kernel(hh, parts, direct, mix32, do, dof):
    rows = direct.shape[0] * direct.shape[2]
    c = direct.shape[-1]
    total = direct[...].reshape(rows, c)
    for s in range(parts.shape[0]):
        total += parts[s].reshape(rows, c).astype(F32)
    low = total.astype(BF16)
    lane = lax.broadcasted_iota(jnp.int32, (rows, 128), 1)
    for h in range(hh):
        grad = jnp.concatenate(
            [jnp.zeros((rows, 64), BF16), low[:, h * 64 : h * 64 + 64]], axis=1
        )
        mix = mix32[h].reshape(rows, 128)
        delta = jnp.sum(grad.astype(F32) * mix, axis=1, keepdims=True)
        a, b, e = split3(jnp.broadcast_to(-delta, (rows, 128)))
        zero = BF16(0)
        feature = jnp.where(lane == 2, a, jnp.where(lane == 3, b, jnp.where(lane == 4, e, zero)))
        do[h] = grad.reshape(do.shape[1:])
        dof[h] = feature.reshape(dof.shape[1:])


def gather_grad(hh, parts, direct, mix32):
    zs, _, _, tn, c = parts.shape
    T = 2 * zs * tn
    m4 = mix32.reshape(hh, zs, 2, tn, 128)
    wide = pl.BlockSpec((hh, zs, None, tn, 128), lambda y: (0, 0, y, 0, 0))

    def kernel(parts, direct, mix32, do, dof):
        gather_kernel(hh, parts, _Row(direct), mix32, do, dof)

    do, dof = pl.pallas_call(
        kernel,
        grid=(2,),
        in_specs=[
            pl.BlockSpec((zs, None, zs, tn, c), lambda y: (0, y, 0, 0, 0)),
            pl.BlockSpec((zs, None, tn, c), lambda y: (0, y, 0, 0)),
            wide,
        ],
        out_specs=[wide, wide],
        out_shape=[shape((hh, zs, 2, tn, 128), BF16)] * 2,
        compiler_params=PARAMS,
        name="gather_grad",
    )(parts, direct, m4)
    return do.reshape(hh, T, 128), dof.reshape(hh, T, 128)


def back_kernel(hh, T, bq, bk, first, mine, kv, q, qf, do, dof, *refs):
    if first:
        dq_out, dkv, dkv_sc, kf_sc, spans, qspans = refs
        dq_out[...] = jnp.zeros_like(dq_out)
    else:
        dq_in, dq_out, dkv, dkv_sc, kf_sc, spans, qspans = refs
        dq_out[...] = dq_in[...]
    trows = T // 128
    tail = hh * T
    ranges(scene_rows(mine, tail, trows), bq // 128, qspans, 0)
    ids = scene_rows(kv, tail, trows)
    ranges(ids, bk // 128, spans, 0)
    kf_sc[...] = key_features(ids)

    def per_key(j, carry):
        dkv_sc[...] = jnp.zeros_like(dkv_sc)

        def per_query(i, carry):
            @pl.when((qspans[2 * i] <= spans[2 * j + 1]) & (spans[2 * j] <= qspans[2 * i + 1]))
            def _():
                qr = slot(i * bq, bq)
                kf = kf_sc[slot(j * bk, bk), :]
                for h in range(hh):
                    keys = kv[slot(h * T + j * bk, bk), :]
                    ka = jnp.concatenate([keys, kf], axis=1)
                    qh = q[h, qr, :]
                    dh = do[h, qr, :]
                    p = jnp.exp(mm(ka, jnp.concatenate([qh, qf[h, qr, :]], axis=1), NT))
                    dp = mm(ka, jnp.concatenate([dh, dof[h, qr, :]], axis=1), NT)
                    ds = (p * dp).astype(BF16)
                    dkv_sc[h] += mm(ds, qh) + mm(p.astype(BF16), dh)
                    dq_out[h, qr, :] += mm(ds, keys, TN)

            return carry

        lax.fori_loop(0, T // bq, per_query, 0)
        for h in range(hh):
            dkv[slot(h * T + j * bk, bk), :] = dkv_sc[h].astype(BF16)
        return carry

    lax.fori_loop(0, T // bk, per_key, 0)


def attend_back(hh, mine, kv, q, qf, do, dof, dq):
    T = q.shape[1]
    bq = min(256, T)
    bk = min(1024, T)
    first = dq is None
    return pl.pallas_call(
        functools.partial(back_kernel, hh, T, bq, bk, first),
        in_specs=[VMEM] * (6 if first else 7),
        out_specs=[VMEM] * 2,
        out_shape=[shape((hh, T, 128), F32), shape((hh * T, 128), BF16)],
        scratch_shapes=[
            pltpu.VMEM((hh, bk, 128), F32),
            pltpu.VMEM((T, 128), BF16),
            pltpu.SMEM((2 * (T // bk),), F32),
            pltpu.SMEM((2 * (T // bq),), F32),
        ],
        compiler_params=PARAMS,
        name="attend_back",
    )(mine, kv, q, qf, do, dof, *(() if first else (dq,)))


def tail_kernel(hh, dq, dkv, tok, w, out, gp, sums):
    i = pl.program_id(0)
    parts = []
    for h in range(hh):
        q = (dq[h] * 0.125)[:, :64].astype(BF16)
        parts += [q, dkv[h]]
    grads = jnp.concatenate(parts, axis=1)
    gp[...] = grads
    grad = mm(grads, w[...], NT)
    out[...] = grad.astype(BF16)
    unit, _ = unit_rows(tok[...].astype(F32))

    @pl.when(i == 0)
    def _():
        sums[...] = jnp.zeros_like(sums)

    sums[0:1] += jnp.sum(grad * unit, axis=0, keepdims=True)
    sums[1:2] += jnp.sum(grad, axis=0, keepdims=True)


def tail(hh, dq, dkv, tokens, w):
    T, D = tokens.shape
    blk = min(256, T)
    return pl.pallas_call(
        functools.partial(tail_kernel, hh),
        grid=(T // blk,),
        in_specs=[
            pl.BlockSpec((hh, blk, 128), lambda i: (0, i, 0)),
            pl.BlockSpec((hh, blk, 128), lambda i: (0, i, 0)),
            pl.BlockSpec((blk, D), lambda i: (i, 0)),
            pl.BlockSpec(w.shape, lambda i: (0, 0)),
        ],
        out_specs=[
            pl.BlockSpec((blk, D), lambda i: (i, 0)),
            pl.BlockSpec((blk, 192 * hh), lambda i: (i, 0)),
            pl.BlockSpec((8, D), lambda i: (0, 0)),
        ],
        out_shape=[shape((T, D), BF16), shape((T, 192 * hh), BF16), shape((8, D), F32)],
        compiler_params=PARAMS,
        name="tail",
    )(dq, dkv.reshape(hh, T, 128), tokens, w)


def finish_kernel(parts, tok, cot, back, gain, out):
    total = parts[0].astype(F32)
    for s in range(1, parts.shape[0]):
        total += parts[s].astype(F32)
    unit, scale = unit_rows(tok[...].astype(F32))
    grad = norm_back(total * gain[...], unit, scale)
    out[...] = (cot[...].astype(F32) + back[...].astype(F32) + grad).astype(BF16)


def finish(parts, tok, cot, back, gain):
    return pl.pallas_call(
        finish_kernel,
        in_specs=[VMEM] * 5,
        out_specs=VMEM,
        out_shape=shape(tok.shape, BF16),
        compiler_params=PARAMS,
        name="finish",
    )(parts, tok, cot, back, gain)


def local(
    tokens,
    scene_ids,
    norm1_gain,
    norm1_shift,
    qkv_weight,
    qv_bias,
    out_weight,
    out_bias,
    norm2_gain,
    norm2_shift,
    up_weight,
    up_bias,
    down_weight,
    down_bias,
    cotangent,
):
    T, D = tokens.shape
    NW = lax.axis_size("wide")
    N = lax.axis_size("narrow")
    C = out_weight.shape[0]
    hh = C // HEAD_DIM
    U = up_weight.shape[1]
    zs = N // 2
    tn = T // N
    wid = lax.axis_index("wide")
    nid = lax.axis_index("narrow")
    core = wid % 2
    ybit = nid % 2
    zgroups = [list(range(0, N, 2)), list(range(1, N, 2))]
    row = lambda v: v.reshape(1, -1)

    def swap(v, axis, bit):
        size = lax.axis_size(axis)
        return lax.ppermute(v, axis, [(i, i ^ bit) for i in range(size)])

    def wide_scatter(v):
        bit = 1
        live = v.reshape((1, NW) + v.shape[1:])
        blocks = [None]
        order = jnp.arange(NW) ^ wid
        rel = [lax.dynamic_index_in_dim(v, order[k], 0, keepdims=False) for k in range(NW)]
        while bit < NW:
            send = [rel[k] for k in range(len(rel)) if k & 1]
            keep = [rel[k] for k in range(len(rel)) if not k & 1]
            got = swap(jnp.stack(send), "wide", bit)
            rel = [
                (keep[k].astype(F32) + got[k].astype(F32)).astype(v.dtype)
                for k in range(len(keep))
            ]
            bit *= 2
        return rel[0]

    half = U // 2
    up_half = lax.dynamic_slice_in_dim(up_weight, core * half, half, 1)
    dn_half = lax.dynamic_slice_in_dim(down_weight, core * half, half, 0)
    b_half = lax.dynamic_slice_in_dim(up_bias, core * half, half, 0)
    b_high = lax.reduce_precision(b_half, 8, 7)
    b_rows = jnp.zeros((16, D), BF16)
    b_rows = b_rows.at[0, :half].set(b_high.astype(BF16))
    b_rows = b_rows.at[1, :half].set((b_half - b_high).astype(BF16))
    pack = jnp.concatenate([up_half.T, dn_half, b_rows], axis=0)
    near = swap(pack, "narrow", 1)
    wo_all = lax.all_gather(out_weight, "narrow", axis=0, tiled=True)

    bias3 = jnp.concatenate(
        [
            qv_bias.reshape(hh, 2, 64)[:, 0],
            jnp.zeros((hh, 64), F32),
            qv_bias.reshape(hh, 2, 64)[:, 1],
        ],
        axis=1,
    )
    id_rows = scene_ids.astype(BF16).reshape(T // 128, 128)
    id_rows = jnp.pad(id_rows, ((0, -(T // 128) % 16 + 16), (0, 0)))
    normed, q, mine = project(
        tokens, row(norm1_gain), row(norm1_shift), qkv_weight, row(bias3), id_rows, hh
    )

    kv = {0: mine}
    bit = 2
    while bit < NW:
        for k in list(kv):
            kv[k + bit] = swap(kv[k], "wide", bit)
        bit *= 2
    for k in list(kv):
        kv[k + 1] = swap(kv[k], "wide", 1)
    far = swap(near, "wide", 1)

    direct = mm(cotangent, out_weight, NT)
    before = None
    for k in range(0, NW, 2):
        before = attend(hh, mine, q, [kv[k], kv[k + 1]], before, k + 2 == NW)
    mixed, mix32, qf = before

    blocks = jnp.transpose(mixed.reshape(zs, 2, tn, C), (1, 0, 2, 3))
    sends = jnp.broadcast_to(blocks[None], (zs, 2, zs, tn, C)).reshape(N, zs, tn, C)
    mix_half = lax.all_to_all(sends, "narrow", split_axis=0, concat_axis=0, tiled=True)
    tok4 = tokens.reshape(zs, 2, tn, D)
    cot4 = cotangent.reshape(zs, 2, tn, D)
    a_parts, rff, normed2, residual, sums2 = middle(
        mix_half, tok4, cot4, wo_all, up_weight, down_weight, row(up_bias), far, near,
        row(out_bias), row(norm2_gain), row(norm2_shift), ybit.reshape(1),
    )
    arrived = lax.all_to_all(a_parts, "narrow", split_axis=0, concat_axis=0, tiled=True)
    summed = lax.psum_scatter(
        rff, "narrow", scatter_dimension=0, tiled=True, axis_index_groups=zgroups
    ).reshape(tn, 2 * D)
    normed2_other = swap(normed2, "narrow", 1)

    do, dof = gather_grad(hh, arrived.reshape(zs, 2, zs, tn, C), direct.reshape(zs, 2, tn, C), mix32)

    dq = None
    come = {k: [] for k in range(0, NW, 2)}
    for k in range(NW - 2, -1, -2):
        dq, other = attend_back(hh, mine, kv[k + 1], q, qf, do, dof, dq)
        home = swap(other, "wide", 1)
        dq, own = attend_back(hh, mine, kv[k], q, qf, do, dof, dq)
        total = own.astype(F32) + home.astype(F32)
        for part in come[k]:
            total += part.astype(F32)
        dkv = total.astype(BF16)
        if k:
            top = 1 << (k.bit_length() - 1)
            come[k ^ top].append(swap(dkv, "wide", top))
    grad_part, grads, sums1 = tail(hh, dq, dkv, tokens, qkv_weight)
    back_all = lax.all_to_all(
        grad_part.reshape(N, tn, D), "narrow", split_axis=0, concat_axis=0, tiled=True
    )

    mine_rows = lambda v: lax.dynamic_slice_in_dim(v, nid * tn, tn, 0)
    back_rows = summed[:, :D]
    tok_rows = mine_rows(tokens)
    cot_rows = mine_rows(cotangent)
    zpos = nid // 2
    res_rows = lax.dynamic_index_in_dim(residual, zpos, 0, keepdims=False)
    output_rows = (res_rows + summed[:, D:].astype(F32) + down_bias).astype(BF16)
    output = lax.all_gather(output_rows, "narrow", axis=0, tiled=True)
    token_rows = finish(back_all, tok_rows, cot_rows, back_rows, row(norm1_gain))

    n2 = jnp.where(
        (jnp.arange(2) == ybit)[None, :, None, None], normed2[:, None], normed2_other[:, None]
    ).reshape(T, D)
    hidden = mm(n2, up_weight) + up_bias
    value, slope = gelu_parts(hidden)
    active = value.astype(BF16)
    grad_hidden = (mm(cotangent, down_weight, NT) * slope).astype(BF16)
    grad_down = mm(active, cotangent, TN)
    grad_up = mm(n2, grad_hidden, TN)
    grad_up_bias = jnp.sum(grad_hidden, axis=0, dtype=F32)
    r_rows = (cot_rows.astype(F32) + back_rows.astype(F32)).astype(BF16)
    r_all = lax.all_gather(r_rows, "narrow", axis=0, tiled=True)
    grad_out = mm(mixed, r_all, TN)
    grad_qkv = mm(normed, grads, TN)

    cols = lambda v: v.astype(BF16).reshape(v.shape[0], NW, D // NW).transpose(1, 0, 2)
    grad_down_w = wide_scatter(cols(grad_down)).astype(F32)
    grad_out_w = wide_scatter(cols(grad_out)).astype(F32)
    grad_up_w = wide_scatter(grad_up.astype(BF16).reshape(NW, D // NW, U)).astype(F32)
    grad_qkv_w = wide_scatter(grad_qkv.astype(BF16).reshape(NW, D // NW, 3 * C)).astype(F32)

    r32 = cot_rows.astype(F32) + back_rows.astype(F32)
    vectors = jnp.stack(
        [sums1[0], sums1[1], sums2[0], sums2[1], r32.sum(0), cot_rows.astype(F32).sum(0)]
    ).reshape(6, NW, D // NW)
    bias_sums = jnp.sum(grads, axis=0, dtype=F32).reshape(hh, 3, 64)
    grad_qv = jnp.concatenate([bias_sums[:, 0], bias_sums[:, 2]], axis=1).reshape(NW, -1)
    packed = jnp.concatenate(
        [
            jnp.transpose(vectors, (1, 0, 2)).reshape(NW, -1),
            grad_up_bias.reshape(NW, -1),
            grad_qv,
        ],
        axis=1,
    )
    packed = wide_scatter(packed)
    width = 6 * (D // NW)
    feature_sums = packed[:width]
    up_bias_out = packed[width : width + U // NW].reshape(1, -1)
    qv_out = packed[width + U // NW :].reshape(1, -1)
    vec_rows = jnp.zeros((16 * D,), BF16)
    vec_rows = lax.dynamic_update_slice_in_dim(vec_rows, feature_sums.astype(BF16), 0, 0)
    ending = jnp.concatenate([token_rows, vec_rows.reshape(16, D)], axis=0)
    ended = lax.all_gather(ending, "narrow", axis=0, tiled=True).reshape(N, tn + 16, D)
    grad_tokens = ended[:, :tn].reshape(T, D)
    final = ended[:, tn:].reshape(N, -1)[:, :width].astype(F32).sum(0).reshape(6, D // NW)
    return (
        output,
        grad_tokens,
        final[0],
        final[1],
        grad_qkv_w,
        qv_out,
        grad_out_w,
        final[4],
        final[2],
        final[3],
        grad_up_w,
        up_bias_out,
        grad_down_w,
        final[5],
    )


def solution(mesh):
    in_specs = (
        P("wide", None),
        P("wide"),
        P(),
        P(),
        P(None, "narrow"),
        P("narrow"),
        P("narrow", None),
        P(),
        P(),
        P(),
        P(None, "narrow"),
        P("narrow"),
        P("narrow", None),
        P(),
        P("wide", None),
    )
    out_specs = (
        P("wide", None),
        P("wide", None),
        P("wide"),
        P("wide"),
        P("wide", "narrow"),
        P("narrow", "wide"),
        P("narrow", "wide"),
        P("wide"),
        P("wide"),
        P("wide"),
        P("wide", "narrow"),
        P("narrow", "wide"),
        P("narrow", "wide"),
        P("wide"),
    )
    return jax.shard_map(local, mesh=mesh, in_specs=in_specs, out_specs=out_specs, check_vma=False)
```

```python
import functools

import jax
import jax.numpy as jnp
from jax import lax
from jax.experimental import pallas as pl
from jax.experimental.pallas import tpu as pltpu
from jax.sharding import PartitionSpec as P

HEAD_DIM = 64
EPSILON = 1e-05
BIG = 2.0**100
SAFE = 40.0
ONE = 2
NT = (((1,), (1,)), ((), ()))
NN = (((1,), (0,)), ((), ()))
TN = (((0,), (0,)), ((), ()))
VMEM = pl.BlockSpec(memory_space=pltpu.VMEM)
F32 = jnp.float32
BF16 = jnp.bfloat16


PARAMS = pltpu.CompilerParams(vmem_limit_bytes=56 * 1024 * 1024)


def cost(us, size=0):
    return pl.CostEstimate(flops=int(us * 1e6), bytes_accessed=size, transcendentals=0)


def mm(a, b, dims=NN):
    return lax.dot_general(a, b, dims, preferred_element_type=F32)


def slot(at, size):
    return pl.ds(pl.multiple_of(at, size), size)


def shape(dims, dtype):
    return jax.ShapeDtypeStruct(dims, dtype)


def unit_rows(values):
    centre = jnp.mean(values, axis=-1, keepdims=True)
    centred = values - centre
    spread = jnp.mean(centred * centred, axis=-1, keepdims=True)
    scale = lax.rsqrt(spread + EPSILON)
    return centred * scale, scale


def norm_back(grad, unit, scale):
    first = jnp.mean(grad, axis=-1, keepdims=True)
    second = jnp.mean(grad * unit, axis=-1, keepdims=True)
    return (grad - first - unit * second) * scale


def gelu_parts(v):
    c = 0.7978845608028654
    square = v * v
    t = jnp.tanh(c * (v + 0.044715 * (v * square)))
    value = 0.5 * v * (1.0 + t)
    slope = 0.5 * (1.0 + t) + 0.5 * v * (1.0 - t * t) * (c * (1.0 + 3 * 0.044715 * square))
    return value, slope


def split3(v):
    a = v.astype(BF16)
    rest = v - a.astype(F32)
    b = rest.astype(BF16)
    return a, b, (rest - b.astype(F32)).astype(BF16)


def id_features(ids, start, change):
    n = ids.shape[0]
    row = lax.broadcasted_iota(jnp.int32, (128, 128), 0)
    lane = lax.broadcasted_iota(jnp.int32, (128, 128), 1)
    pick = lambda v: jnp.where(lane == 0, v[0], jnp.where(lane == 1, v[1], v[2]))
    spread = [
        jnp.where(row == lane, jnp.broadcast_to(ids[c : c + 1], (128, 128)), 0.0) for c in range(n)
    ]
    own = jnp.concatenate(spread, axis=0).astype(BF16)
    moved = mm(own, pick((change[0], change[1], 0.0)).astype(BF16))
    return (moved + pick(start)[0:1]).astype(BF16)


def key_features(ids):
    return id_features(ids, (-BIG, 0.0, 1.0), (BIG, -BIG))


def query_features(ids):
    return id_features(ids, (0.0, 1.0, 0.0), (1.0, -1.0))


def project_kernel(hh, T, blk, tok, gain, shift, w, bias, ids, normed, q_out, kvx, most):
    i = pl.program_id(0)
    extra = kvx.shape[0] - hh * T

    @pl.when(i == 0)
    def _():
        most[...] = jnp.zeros_like(most)
        rows = ids[...].astype(F32)
        rows = jnp.concatenate([rows, jnp.zeros((extra - rows.shape[0], 128), F32)], axis=0)
        kvx[hh * T :, :] = rows.astype(BF16)

    unit, _ = unit_rows(tok[...].astype(F32))
    low = (unit * gain[...] + shift[...]).astype(BF16)
    normed[...] = low
    proj = mm(low, w[...])
    for h in range(hh):
        part = proj[:, h * 192 : h * 192 + 192]
        at = h * 128
        q = ((part[:, :64] + bias[:, at : at + 64]).astype(BF16) * BF16(0.125)).astype(F32)
        k = part[:, 64:128]
        v = part[:, 128:] + bias[:, at + 64 : at + 128]
        q_out[h] = jnp.concatenate([q, jnp.zeros((blk, 64), F32)], axis=1).astype(BF16)
        kvx[slot(h * T + i * blk, blk), :] = jnp.concatenate([k, v], axis=1).astype(BF16)
        for r, vec in ((0, k), (1, q)):
            top = jnp.max(jnp.sum(vec * vec, axis=1, keepdims=True), axis=0, keepdims=True)
            most[r : r + 1] = jnp.maximum(most[r : r + 1], top)

    @pl.when(i == T // blk - 1)
    def _():
        row = lax.broadcasted_iota(jnp.int32, (16, 128), 0)
        tops = jnp.where(row == 0, most[0:1], jnp.where(row == 1, most[1:2], 0.0))
        kvx[hh * T + extra - 16 :, :] = (tops * 1.02).astype(BF16)


def project(tokens, gain, shift, w, bias, ids, hh):
    T, D = tokens.shape
    blk = min(256, T)
    extra = ids.shape[0] + -ids.shape[0] % 16 + 16
    whole = lambda *dims: pl.BlockSpec(dims, lambda i: (0,) * len(dims))
    return pl.pallas_call(
        functools.partial(project_kernel, hh, T, blk),
        grid=(T // blk,),
        in_specs=[
            pl.BlockSpec((blk, D), lambda i: (i, 0)),
            whole(1, D),
            whole(1, D),
            whole(D, 192 * hh),
            whole(*bias.shape),
            whole(*ids.shape),
        ],
        out_specs=[
            pl.BlockSpec((blk, D), lambda i: (i, 0)),
            pl.BlockSpec((hh, blk, 128), lambda i: (0, i, 0)),
            whole(hh * T + extra, 128),
        ],
        out_shape=[
            shape((T, D), BF16),
            shape((hh, T, 128), BF16),
            shape((hh * T + extra, 128), BF16),
        ],
        scratch_shapes=[pltpu.VMEM((8, 128), F32)],
        compiler_params=PARAMS,
        cost_estimate=cost(7),
        name="project",
    )(tokens, gain, shift, w, bias, ids)


def scene_rows(ref, tail, count):
    return ref[tail : tail + count + -count % 16, :].astype(F32)[:count]


def counts(ids, per, out, at):
    for j in range(ids.shape[0] // per):
        out[at + j] = jnp.sum(ids[j * per : (j + 1) * per])


def meets(a, na, b, nb):
    apart = ((a == 0) & (b == nb)) | ((a == na) & (b == 0))
    return jnp.logical_not(apart)


def attend_kernel(hh, T, nb, bq, bk, first, last, mine, q_ref, *refs):
    kvs = refs[:nb]
    refs = refs[nb:]
    if not first:
        acc_in = refs[0]
        refs = refs[1:]
    if last:
        sends, mix32, feat = refs[:3]
        refs = refs[3:]
    else:
        acc_out = refs[0]
        refs = refs[1:]
    acc_sc, m_sc, qf_sc, kf_sc, spans, qspans = refs
    trows = T // 128
    tail = hh * T
    ids = scene_rows(mine, tail, trows)
    counts(ids, bq // 128, qspans, 0)
    qf_sc[...] = query_features(ids)
    top_q = jnp.max(mine[-16:, :].astype(F32)[1:2])
    tops = kvs[0][-16:, :].astype(F32)
    for b in range(nb):
        ids = scene_rows(kvs[b], tail, trows)
        counts(ids, bk // 128, spans, b * (T // bk))
        kf_sc[b] = key_features(ids)
        tops = jnp.maximum(tops, kvs[b][-16:, :].astype(F32))
    calm = top_q * jnp.max(tops[0:1]) < SAFE * SAFE
    if first:
        acc_sc[...] = jnp.zeros_like(acc_sc)
    else:
        acc_sc[...] = acc_in[...]
        shift = acc_in[:, :, 255:]
        calm = calm & (jnp.max(jnp.abs(shift)) == 0.0)
    m_sc[...] = jnp.zeros_like(m_sc)

    def block(b, h, j):
        rows = slot(h * T + j * bk, bk)
        return jnp.concatenate([kvs[b][rows, :], kf_sc[b, slot(j * bk, bk), :]], axis=1)

    @pl.when(jnp.logical_not(calm))
    def _():
        m_sc[...] = jnp.full(m_sc.shape, -2.0 * BIG, F32)

        def step(n, carry):
            i, j = n // (T // bk), n % (T // bk)
            qr = slot(i * bq, bq)
            for b in range(nb):
                for h in range(hh):
                    q = jnp.concatenate([q_ref[h, qr, :], qf_sc[qr, :]], axis=1)
                    s = mm(q, block(b, h, j), NT)
                    m = jnp.max(s, axis=1, keepdims=True).astype(BF16).astype(F32)
                    m_sc[h, qr, :] = jnp.maximum(m_sc[h, qr, :], m)
            return carry

        lax.fori_loop(0, (T // bq) * (T // bk), step, 0)
        if not first:
            for h in range(hh):
                old = jnp.broadcast_to(acc_in[h, :, 255:], (T, 128))
                new = jnp.maximum(m_sc[h], old)
                keep = jnp.exp(old - new)
                acc_sc[h] = acc_sc[h] * jnp.concatenate([keep, keep], axis=1)
                m_sc[h] = new

    lane = lax.broadcasted_iota(jnp.int32, (bq, 128), 1)

    def per_query(i, carry):
        qr = slot(i * bq, bq)
        qs = []
        for h in range(hh):
            feature = jnp.where(lane == ONE, (-m_sc[h, qr, :]).astype(BF16), qf_sc[qr, :])
            qs.append(jnp.concatenate([q_ref[h, qr, :], feature], axis=1))
        for b in range(nb):

            def per_key(j, carry):
                @pl.when(meets(qspans[i], bq, spans[b * (T // bk) + j], bk))
                def _():
                    for h in range(hh):
                        kv = block(b, h, j)
                        p = jnp.exp(mm(qs[h], kv, NT)).astype(BF16)
                        acc_sc[h, qr, :] += mm(p, kv)

                return carry

            lax.fori_loop(0, T // bk, per_key, 0)
        return carry

    lax.fori_loop(0, T // bq, per_query, 0)
    lanes = lax.broadcasted_iota(jnp.int32, (T, 128), 1)
    if not last:
        for h in range(hh):
            acc_out[h, :, :128] = acc_sc[h, :, :128]
            acc_out[h, :, 128:] = jnp.where(lanes == 127, m_sc[h], acc_sc[h, :, 128:])
        return
    parts = []
    for h in range(hh):
        acc = acc_sc[h]
        total = acc[:, 128 + ONE : 129 + ONE]
        mix = acc[:, :128] / total
        mix32[h] = mix
        parts.append(mix[:, 64:])
        a, b, c = split3(-(m_sc[h] + jnp.log(total)))
        feat[h] = jnp.where(
            lanes == 2, a, jnp.where(lanes == 3, b, jnp.where(lanes == 4, c, qf_sc[...]))
        )
    whole = jnp.concatenate(parts, axis=1) if hh > 1 else parts[0]
    count, zs, tn, c = sends.shape
    halves = whole.astype(BF16).reshape(zs, 2, tn, c)
    for n in range(count):
        sends[n] = halves[:, n % 2]


def attend(hh, devices, mine, q, kvs, before, last):
    T = q.shape[1]
    nb = len(kvs)
    bq = min(512, T)
    bk = min(1024, T)
    first = before is None
    if last:
        outs = [
            shape((devices, devices // 2, T // devices, hh * 64), BF16),
            shape((hh, T, 128), F32),
            shape((hh, T, 128), BF16),
        ]
    else:
        outs = [shape((hh, T, 256), F32)]
    return pl.pallas_call(
        functools.partial(attend_kernel, hh, T, nb, bq, bk, first, last),
        in_specs=[VMEM] * (2 + nb + (0 if first else 1)),
        out_specs=[VMEM] * len(outs),
        out_shape=outs,
        scratch_shapes=[
            pltpu.VMEM((hh, T, 256), F32),
            pltpu.VMEM((hh, T, 128), F32),
            pltpu.VMEM((T, 128), BF16),
            pltpu.VMEM((nb, T, 128), BF16),
            pltpu.SMEM((nb * (T // bk),), F32),
            pltpu.SMEM((T // bq,), F32),
        ],
        compiler_params=PARAMS,
        cost_estimate=cost(8),
        name="attend",
    )(mine, q, *kvs, *(() if first else (before,)))


def pack_kernel(c_ref, up, dn, bias, out):
    half = dn.shape[0]
    D = dn.shape[1]
    for a in range(D // half):
        out[:half, a * half : (a + 1) * half] = up[a * half : (a + 1) * half, :]
    out[half : 2 * half, :] = dn[...]
    a, b, c = split3(bias[...])
    zero = jnp.zeros((1, D - 3 * half), F32)
    parts = [v.astype(F32) for v in (a, b, c)] + ([zero] if D > 3 * half else [])
    row = jnp.concatenate(parts, axis=1)
    out[2 * half :, :] = jnp.broadcast_to(row, (16, D)).astype(BF16)


def pack_half(core, up, dn, bias):
    D, U = up.shape
    half = U // 2
    return pl.pallas_call(
        pack_kernel,
        grid_spec=pltpu.PrefetchScalarGridSpec(
            num_scalar_prefetch=1,
            grid=(1,),
            in_specs=[
                pl.BlockSpec((D, half), lambda i, c: (0, c[0])),
                pl.BlockSpec((half, D), lambda i, c: (c[0], 0)),
                pl.BlockSpec((1, half), lambda i, c: (0, c[0])),
            ],
            out_specs=pl.BlockSpec((2 * half + 16, D), lambda i, c: (0, 0)),
        ),
        out_shape=shape((2 * half + 16, D), BF16),
        compiler_params=PARAMS,
        cost_estimate=cost(3),
        name="pack_half",
    )(core, up, dn, bias)


def pieces(own, far, near, half, units):
    up, dn, bias = own
    ahead = lambda v: mm(v, up[...])
    back = lambda v: mm(v, up[...], NT)
    yield slice(0, units), ahead, back, dn, bias
    for at, pack in enumerate((far, near)):
        D = pack.shape[1]
        tail = pack[2 * half :, :].astype(F32)
        bias = tail[0:1, :half] + tail[0:1, half : 2 * half] + tail[0:1, 2 * half : 3 * half]
        spans = [slice(a, a + half) for a in range(0, D, half)]

        def ahead(v, pack=pack):
            total = mm(v[:, spans[0]], pack[:half, spans[0]])
            for span in spans[1:]:
                total += mm(v[:, span], pack[:half, span])
            return total

        def back(v, pack=pack):
            return jnp.concatenate([mm(v, pack[:half, span], NT) for span in spans], axis=1)

        yield slice(units + at * half, units + (at + 1) * half), ahead, back, _Rows(
            pack, half, 2 * half
        ), bias


class _Rows:
    def __init__(self, ref, start, stop):
        self.ref, self.start, self.stop = ref, start, stop

    def __getitem__(self, at):
        return self.ref[self.start : self.stop, :]


def before_kernel(units, cot, dn_own, far, near, out):
    rows = cot.shape[0] * cot.shape[1]
    g = cot[...].reshape(rows, cot.shape[2])
    for cols, _, _, dn, _ in pieces((None, dn_own, None), far, near, units // 2, units):
        out[:, cols] = mm(g, dn[...], NT).astype(BF16)


def before_middle(cot, dn_own, far, near, half):
    zs, _, tn, D = cot.shape
    U = dn_own.shape[0]
    const = lambda a: pl.BlockSpec(a.shape, lambda i, y: (0,) * a.ndim)

    def kernel(y_ref, *refs):
        before_kernel(U, *refs)

    return pl.pallas_call(
        kernel,
        grid_spec=pltpu.PrefetchScalarGridSpec(
            num_scalar_prefetch=1,
            grid=(1,),
            in_specs=[pl.BlockSpec((zs, None, tn, D), lambda i, y: (0, y[0], 0, 0))]
            + [const(a) for a in (dn_own, far, near)],
            out_specs=pl.BlockSpec((zs * tn, 2 * U), lambda i, y: (0, 0)),
        ),
        out_shape=shape((zs * tn, 2 * U), BF16),
        compiler_params=PARAMS,
        cost_estimate=cost(3),
        name="before_middle",
    )(half, cot, dn_own, far, near)


def middle_kernel(
    units, wid, count, mix, tok, ga, *refs,
):
    wos = refs[:count]
    middle_rest(units, wid, wos, mix, tok, ga, *refs[count:])


def middle_rest(
    units, wid, wos, mix, tok, ga, up_own, b_own, far, near, bo, g2, s2,
    a_out, active, back_out, normed2, res, sums, wo_sc,
):
    i = pl.program_id(0)

    @pl.when(i == 0)
    def _():
        sums[...] = jnp.zeros_like(sums)
        for k, part in enumerate(wos):
            wo_sc[wid ^ k] = part[...].reshape(wo_sc.shape[1:])

    wo = jnp.concatenate([wo_sc[k] for k in range(len(wos))], axis=1)
    n = mix.shape[0]
    D = tok.shape[-1]
    rows = tok.shape[0] * tok.shape[1]
    mixed = jnp.concatenate([mix[s].reshape(rows, mix.shape[-1]) for s in range(n)], axis=1)
    x = tok[...].reshape(rows, D).astype(F32)
    residual = x + mm(mixed, wo) + bo[...]
    unit, scale = unit_rows(residual)
    low = (unit * g2[...] + s2[...]).astype(BF16)
    res[...] = residual.reshape(res.shape)
    normed2[...] = low.reshape(normed2.shape)
    gn = jnp.zeros((rows, D), F32)
    for cols, ahead, back, _, bias in pieces(
        (up_own, None, b_own[...]), far, near, units // 2, units
    ):
        value, slope = gelu_parts(ahead(low) + bias)
        active[:, cols] = value.astype(BF16)
        gn += back((ga[:, cols].astype(F32) * slope).astype(BF16))
    back_low = norm_back(gn * g2[...], unit, scale).astype(BF16)
    back_out[...] = back_low.reshape(back_out.shape)
    a = mm(back_low, wo, NT).astype(BF16)
    c = a_out.shape[-1]
    for s in range(n):
        a_out[s] = a[:, s * c : (s + 1) * c].reshape(a_out.shape[1:])

    sums[0:1] += jnp.sum(gn * unit, axis=0, keepdims=True)
    sums[1:2] += jnp.sum(gn, axis=0, keepdims=True)


def middle(mix, tok, ga, wos, up_own, b_own, far, near, bo, g2, s2, half, wid):
    n, zs, tn, c = mix.shape
    D = up_own.shape[0]
    U = up_own.shape[1]
    zb = max(1, zs // 2)
    const = lambda a: pl.BlockSpec(a.shape, lambda i, y, e: (0,) * a.ndim)
    rows = pl.BlockSpec((zb, tn, D), lambda i, y, e: (i, 0, 0))
    flat = pl.BlockSpec((zb * tn, 2 * U), lambda i, y, e: (i, 0))
    heads = pl.BlockSpec((n, zb, tn, c), lambda i, y, e: (0, i, 0, 0))

    def kernel(y_ref, e_ref, *refs):
        middle_kernel(U, e_ref[0], len(wos), *refs)

    return pl.pallas_call(
        kernel,
        grid_spec=pltpu.PrefetchScalarGridSpec(
            num_scalar_prefetch=2,
            grid=(zs // zb,),
            in_specs=[
                heads,
                pl.BlockSpec((zb, None, tn, D), lambda i, y, e: (i, y[0], 0, 0)),
                flat,
            ]
            + [const(a) for a in (*wos, up_own, b_own, far, near, bo, g2, s2)],
            out_specs=[heads, flat, rows, rows, rows, pl.BlockSpec((8, D), lambda i, y, e: (0, 0))],
            scratch_shapes=[pltpu.VMEM((len(wos), n * c, D // len(wos)), BF16)],
        ),
        out_shape=[
            shape((n, zs, tn, c), BF16),
            shape((zs * tn, 2 * U), BF16),
            shape((zs, tn, D), BF16),
            shape((zs, tn, D), BF16),
            shape((zs, tn, D), F32),
            shape((8, D), F32),
        ],
        compiler_params=PARAMS,
        cost_estimate=cost(12),
        name="middle",
    )(half, wid, mix, tok, ga, *wos, up_own, b_own, far, near, bo, g2, s2)


def after_kernel(units, y_ref, lead, active, back, mix, cot, dn_own, far, near, rff, go):
    rows = active.shape[0]
    D = back.shape[-1]
    ff = jnp.zeros((rows, D), F32)
    for cols, _, _, dn, _ in pieces((None, dn_own, None), far, near, units // 2, units):
        ff += mm(active[:, cols], dn[...])
    rff[:, :, :D] = back[...]
    rff[:, :, D:] = ff.astype(BF16).reshape(back.shape)
    r = back[...].reshape(rows, D)
    g = jnp.where(lead[0] == 0, cot[...].reshape(rows, D), jnp.zeros((), BF16))
    c = mix.shape[-1]
    size = go.shape[2]
    for s in range(mix.shape[0]):
        heads = mix[s].reshape(rows, c)
        total = (mm(heads, r, TN) + mm(heads, g, TN)).astype(BF16)
        for k in range(go.shape[0]):
            go[k, s * c : (s + 1) * c, :] = total[:, k * size : (k + 1) * size]


def after_middle(active, back, mix, cot, dn_own, far, near, half, lead, wides):
    n, zs, tn, c = mix.shape
    U, D = dn_own.shape
    const = lambda a: pl.BlockSpec(a.shape, lambda i, y, z: (0,) * a.ndim)
    return pl.pallas_call(
        functools.partial(after_kernel, U),
        grid_spec=pltpu.PrefetchScalarGridSpec(
            num_scalar_prefetch=2,
            grid=(1,),
            in_specs=[
                const(active),
                const(back),
                const(mix),
                pl.BlockSpec((zs, None, tn, D), lambda i, y, z: (0, y[0], 0, 0)),
            ]
            + [const(a) for a in (dn_own, far, near)],
            out_specs=[
                pl.BlockSpec((zs, tn, 2 * D), lambda i, y, z: (0, 0, 0)),
                pl.BlockSpec((wides, n * c, D // wides), lambda i, y, z: (0, 0, 0)),
            ],
        ),
        out_shape=[shape((zs, tn, 2 * D), BF16), shape((wides, n * c, D // wides), BF16)],
        compiler_params=PARAMS,
        cost_estimate=cost(6),
        name="after_middle",
    )(half, lead, active, back, mix, cot, dn_own, far, near)


class _Row:
    def __init__(self, ref):
        self.ref = ref
        self.shape = (ref.shape[0], 1, ref.shape[1], ref.shape[2])

    def __getitem__(self, at):
        return self.ref[at]


def gather_kernel(hh, parts, direct, mix32, do, dof):
    rows = direct.shape[0] * direct.shape[2]
    c = direct.shape[-1]
    total = direct[...].reshape(rows, c)
    for s in range(parts.shape[0]):
        total += parts[s].reshape(rows, c).astype(F32)
    low = total.astype(BF16)
    lane = lax.broadcasted_iota(jnp.int32, (rows, 128), 1)
    for h in range(hh):
        grad = jnp.concatenate(
            [jnp.zeros((rows, 64), BF16), low[:, h * 64 : h * 64 + 64]], axis=1
        )
        mix = mix32[h].reshape(rows, 128)
        delta = jnp.sum(grad.astype(F32) * mix, axis=1, keepdims=True)
        a, b, e = split3(jnp.broadcast_to(-delta, (rows, 128)))
        zero = BF16(0)
        feature = jnp.where(lane == 2, a, jnp.where(lane == 3, b, jnp.where(lane == 4, e, zero)))
        do[h] = grad.reshape(do.shape[1:])
        dof[h] = feature.reshape(dof.shape[1:])


def gather_grad(hh, parts, direct, mix32):
    zs, _, _, tn, c = parts.shape
    T = 2 * zs * tn
    m4 = mix32.reshape(hh, zs, 2, tn, 128)
    wide = pl.BlockSpec((hh, zs, None, tn, 128), lambda y: (0, 0, y, 0, 0))

    def kernel(parts, direct, mix32, do, dof):
        gather_kernel(hh, parts, _Row(direct), mix32, do, dof)

    do, dof = pl.pallas_call(
        kernel,
        grid=(2,),
        in_specs=[
            pl.BlockSpec((zs, None, zs, tn, c), lambda y: (0, y, 0, 0, 0)),
            pl.BlockSpec((zs, None, tn, c), lambda y: (0, y, 0, 0)),
            wide,
        ],
        out_specs=[wide, wide],
        out_shape=[shape((hh, zs, 2, tn, 128), BF16)] * 2,
        compiler_params=PARAMS,
        cost_estimate=cost(3),
        name="gather_grad",
    )(parts, direct, m4)
    return do.reshape(hh, T, 128), dof.reshape(hh, T, 128)


def back_kernel(hh, T, bq, bk, first, last, mine, kv, q, qf, do, dof, *refs):
    if first:
        dq_out, dkv, dkv_sc, dq_sc, kf_sc, spans, qspans = refs
        dq_sc[...] = jnp.zeros_like(dq_sc)
    else:
        dq_in, dq_out, dkv, dkv_sc, dq_sc, kf_sc, spans, qspans = refs
        dq_sc[...] = dq_in[...]
    trows = T // 128
    tail = hh * T
    counts(scene_rows(mine, tail, trows), bq // 128, qspans, 0)
    ids = scene_rows(kv, tail, trows)
    counts(ids, bk // 128, spans, 0)
    kf_sc[...] = key_features(ids)

    def per_key(j, carry):
        dkv_sc[...] = jnp.zeros_like(dkv_sc)

        def per_query(i, carry):
            @pl.when(meets(qspans[i], bq, spans[j], bk))
            def _():
                qr = slot(i * bq, bq)
                kf = kf_sc[slot(j * bk, bk), :]
                for h in range(hh):
                    keys = kv[slot(h * T + j * bk, bk), :]
                    ka = jnp.concatenate([keys, kf], axis=1)
                    qh = q[h, qr, :]
                    dh = do[h, qr, :]
                    p = jnp.exp(mm(ka, jnp.concatenate([qh, qf[h, qr, :]], axis=1), NT))
                    dp = mm(ka, jnp.concatenate([dh, dof[h, qr, :]], axis=1), NT)
                    ds = (p * dp).astype(BF16)
                    dkv_sc[h] += mm(ds, qh) + mm(p.astype(BF16), dh)
                    dq_sc[h, qr, :] += mm(ds, keys, TN)

            return carry

        lax.fori_loop(0, T // bq, per_query, 0)
        for h in range(hh):
            dkv[slot(h * T + j * bk, bk), :] = dkv_sc[h].astype(BF16)
        return carry

    lax.fori_loop(0, T // bk, per_key, 0)
    if last:
        parts = [dq_sc[h][:, :64] * 0.125 for h in range(hh)]
        whole = jnp.concatenate(parts, axis=1) if hh > 1 else parts[0]
        dq_out[...] = whole.astype(BF16)
    else:
        dq_out[...] = dq_sc[...]


def attend_back(hh, mine, kv, q, qf, do, dof, dq, last):
    T = q.shape[1]
    bq = min(256, T)
    bk = min(1024, T)
    first = dq is None
    sums = shape((T, hh * 64), BF16) if last else shape((hh, T, 128), F32)
    return pl.pallas_call(
        functools.partial(back_kernel, hh, T, bq, bk, first, last),
        in_specs=[VMEM] * (6 if first else 7),
        out_specs=[VMEM] * 2,
        out_shape=[sums, shape((hh * T, 128), BF16)],
        scratch_shapes=[
            pltpu.VMEM((hh, bk, 128), F32),
            pltpu.VMEM((hh, T, 128), F32),
            pltpu.VMEM((T, 128), BF16),
            pltpu.SMEM((T // bk,), F32),
            pltpu.SMEM((T // bq,), F32),
        ],
        compiler_params=PARAMS,
        cost_estimate=cost(9),
        name="attend_back",
    )(mine, kv, q, qf, do, dof, *(() if first else (dq,)))


def collect_kernel(hh, y_ref, gq, *refs):
    parts = refs[:-3]
    grads, send, sums = refs[-3:]
    zs, _, tn, width = grads.shape
    T = 2 * zs * tn
    cols = []
    for h in range(hh):
        total = parts[0][h * T : (h + 1) * T, :].astype(F32)
        for part in parts[1:]:
            total += part[h * T : (h + 1) * T, :].astype(F32)
        low = total.astype(BF16).astype(F32)
        cols += [gq[:, h * 64 : (h + 1) * 64].astype(F32), low]
    whole = jnp.concatenate(cols, axis=1)
    row = lax.broadcasted_iota(jnp.int32, (8, width), 0)
    sums[...] = jnp.where(row == 0, jnp.sum(whole, axis=0, keepdims=True), 0.0)
    halves = whole.astype(BF16).reshape(zs, 2, tn, width)
    grads[...] = halves
    send[...] = jnp.where(y_ref[0] == 0, halves[:, 1], halves[:, 0])


def collect(hh, half, gq, parts, zs):
    T = gq.shape[0]
    tn = T // zs // 2
    width = 192 * hh
    return pl.pallas_call(
        functools.partial(collect_kernel, hh),
        in_specs=[pl.BlockSpec(memory_space=pltpu.SMEM)] + [VMEM] * (1 + len(parts)),
        out_specs=[VMEM] * 3,
        out_shape=[
            shape((zs, 2, tn, width), BF16),
            shape((zs, tn, width), BF16),
            shape((8, width), F32),
        ],
        compiler_params=PARAMS,
        cost_estimate=cost(3),
        name="collect",
    )(half, gq, *parts)


def project_back(grads, other, w, w_near, w_far, half, core):
    zs, _, tn, width = grads.shape
    D = w.shape[0]
    zb = max(1, zs // 2)

    def kernel(y_ref, c_ref, own, other, w, w_near, w_far, out, w_sc):
        rows = zb * tn

        @pl.when(pl.program_id(0) == 0)
        def _():
            w_sc[c_ref[0]] = w_near[...]
            w_sc[1 - c_ref[0]] = w_far[...]

        total = mm(own[...].reshape(rows, width), w[...], NT)
        total += mm(other[...].reshape(rows, width), w_sc[...].reshape(D, width), NT)
        out[...] = total.astype(BF16).reshape(out.shape)

    const = lambda a: pl.BlockSpec(a.shape, lambda i, y, c: (0,) * a.ndim)
    return pl.pallas_call(
        kernel,
        grid_spec=pltpu.PrefetchScalarGridSpec(
            num_scalar_prefetch=2,
            grid=(zs // zb,),
            in_specs=[
                pl.BlockSpec((zb, None, tn, width), lambda i, y, c: (i, y[0], 0, 0)),
                pl.BlockSpec((zb, tn, width), lambda i, y, c: (i, 0, 0)),
                const(w),
                const(w_near),
                const(w_far),
            ],
            out_specs=pl.BlockSpec((zb, tn, D), lambda i, y, c: (i, 0, 0)),
            scratch_shapes=[pltpu.VMEM((2, D // 2, width), BF16)],
        ),
        out_shape=shape((zs, tn, D), BF16),
        compiler_params=PARAMS,
        cost_estimate=cost(3),
        name="project_back",
    )(half, core, grads, other, w, w_near, w_far)


def vector_sums(hh, wides, part, tok, sums2, summed, cot, unit_sums, grad_sums, half, at):
    zs, tn, D = part.shape
    size = D // wides

    def kernel(y_ref, n_ref, part, tok, sums2, summed, cot, unit_sums, grad_sums, out, sc):
        i = pl.program_id(0)
        unit, _ = unit_rows(tok[...].astype(F32))
        grad = part[...].astype(F32)

        @pl.when(i == 0)
        def _():
            sc[...] = jnp.zeros_like(sc)

        sc[0:1] += jnp.sum(grad * unit, axis=0, keepdims=True)
        sc[1:2] += jnp.sum(grad, axis=0, keepdims=True)

        @pl.when(i == zs - 1)
        def _():
            g = cot[...].astype(F32)
            sc[2:4] = sums2[0:2]
            sc[4:5] = jnp.sum(g + summed[...].astype(F32), axis=0, keepdims=True)
            sc[5:6] = jnp.sum(g, axis=0, keepdims=True)
            pairs = []
            for h in range(hh):
                first = h * 192
                pairs += [grad_sums[0:1, first : first + 64], grad_sums[0:1, first + 128 : first + 192]]
            heads = jnp.concatenate(pairs, axis=1)
            for k in range(wides):
                out[k] = sc[:, k * size : (k + 1) * size]
                for row, v in ((6, unit_sums[0:1]), (7, heads)):
                    n = v.shape[1] // wides
                    mine = v[:, k * n : (k + 1) * n]
                    if n < size:
                        mine = jnp.concatenate([mine, jnp.zeros((1, size - n), F32)], axis=1)
                    out[k, row : row + 1] = mine

    whole = lambda a: pl.BlockSpec(a.shape, lambda i, y, n: (0,) * a.ndim)
    return pl.pallas_call(
        kernel,
        grid_spec=pltpu.PrefetchScalarGridSpec(
            num_scalar_prefetch=2,
            grid=(zs,),
            in_specs=[
                pl.BlockSpec((None, tn, D), lambda i, y, n: (i, 0, 0)),
                pl.BlockSpec((None, None, tn, D), lambda i, y, n: (i, y[0], 0, 0)),
                whole(sums2),
                pl.BlockSpec((tn, D), lambda i, y, n: (0, 0)),
                pl.BlockSpec((tn, D), lambda i, y, n: (n[0], 0)),
                whole(unit_sums),
                whole(grad_sums),
            ],
            out_specs=pl.BlockSpec((wides, 8, size), lambda i, y, n: (0, 0, 0)),
            scratch_shapes=[pltpu.VMEM((8, D), F32)],
        ),
        out_shape=shape((wides, 8, size), F32),
        compiler_params=PARAMS,
        cost_estimate=cost(3),
        name="vector_sums",
    )(half, at, part, tok, sums2, summed, cot, unit_sums, grad_sums)


def finish_kernel(at, *refs):
    tok, cot, back, gain, vec, out = refs[-6:]
    total = refs[0][...].astype(F32)
    for part in refs[1:-6]:
        total += part[...].astype(F32)
    unit, scale = unit_rows(tok[...].astype(F32))
    grad = norm_back(total * gain[...], unit, scale)
    r = cot[...].astype(F32) + back[...].astype(F32)
    out[: r.shape[0], :] = (r + grad).astype(BF16)
    tn, D = r.shape
    rows = jnp.concatenate([vec[...], jnp.zeros_like(vec)], axis=0).astype(BF16)
    out[tn:, :] = jnp.concatenate([rows, jnp.zeros((16, D - rows.shape[1]), BF16)], axis=1)


def finish(at, parts, tokens, cot, back, gain, vec):
    tn, D = parts[0].shape
    mine = pl.BlockSpec((tn, D), lambda i, n: (n[0], 0))
    first = pl.BlockSpec((tn, D), lambda i, n: (0, 0))
    return pl.pallas_call(
        finish_kernel,
        grid_spec=pltpu.PrefetchScalarGridSpec(
            num_scalar_prefetch=1,
            grid=(1,),
            in_specs=[first] * len(parts)
            + [
                mine,
                mine,
                first,
                pl.BlockSpec((1, D), lambda i, n: (0, 0)),
                pl.BlockSpec(vec.shape, lambda i, n: (0, 0)),
            ],
            out_specs=pl.BlockSpec((tn + 16, D), lambda i, n: (0, 0)),
        ),
        out_shape=shape((tn + 16, D), BF16),
        compiler_params=PARAMS,
        cost_estimate=cost(2),
        name="finish",
    )(at, *parts, tokens, cot, back, gain, vec)


def place(nid, mine, theirs, tail):
    moves = [move for _, move in mine]
    rows, D = theirs[0].shape
    tn = rows - tail
    zs = len(moves)

    def kernel(n_ref, *refs):
        out, total = refs[-2:]
        z, y = n_ref[0] // 2, n_ref[0] % 2
        total[...] = jnp.zeros_like(total)
        for k, move in enumerate(moves):
            to = lax.rem(z + move + zs, zs)
            out[to, y] = refs[k][:tn, :]
            out[to, 1 - y] = refs[zs + k][:tn, :]
            total[...] += refs[k][tn:, :].astype(F32) + refs[zs + k][tn:, :].astype(F32)

    return pl.pallas_call(
        kernel,
        in_specs=[pl.BlockSpec(memory_space=pltpu.SMEM)] + [VMEM] * (2 * zs),
        out_specs=[VMEM] * 2,
        out_shape=[shape((zs, 2, tn, D), BF16), shape((tail, D), F32)],
        compiler_params=PARAMS,
        cost_estimate=cost(2),
        name="place",
    )(nid, *[v for v, _ in mine], *theirs)


def join(y, mine, theirs):
    zs, tn, D = mine.shape

    def kernel(y_ref, mine, theirs, out):
        out[:, y_ref[0]] = mine[...]
        out[:, 1 - y_ref[0]] = theirs[...]

    return pl.pallas_call(
        kernel,
        in_specs=[pl.BlockSpec(memory_space=pltpu.SMEM)] + [VMEM] * 2,
        out_specs=VMEM,
        out_shape=shape((zs, 2, tn, D), BF16),
        compiler_params=PARAMS,
        cost_estimate=cost(2),
        name="join",
    )(y, mine, theirs)


def units_kernel(y_ref, n2, n2_other, cot, up, dn, bias, both, sums, act_sc, grad_sc):
    zs, _, tn, D = cot.shape
    rows = zs * tn
    U = up.shape[1]
    halves = cot[...]
    swap = y_ref[0] == 1
    g = [
        jnp.where(swap, halves[:, 1], halves[:, 0]).reshape(rows, D),
        jnp.where(swap, halves[:, 0], halves[:, 1]).reshape(rows, D),
    ]
    lows = [n2[...].reshape(rows, D), n2_other[...].reshape(rows, D)]
    total = jnp.zeros((1, U), F32)
    for k in range(2):
        value, slope = gelu_parts(mm(lows[k], up[...]) + bias[...])
        act_sc[k] = value.astype(BF16)
        grad = (mm(g[k], dn[...], NT) * slope).astype(BF16)
        grad_sc[k] = grad
        total += jnp.sum(grad.astype(F32), axis=0, keepdims=True)
    row = lax.broadcasted_iota(jnp.int32, (8, U), 0)
    sums[...] = jnp.where(row == 0, total, 0.0)
    size = both.shape[2]
    for w in range(both.shape[0]):
        cols = slice(w * size, (w + 1) * size)
        for at, left, right in ((0, g, act_sc), (1, lows, grad_sc)):
            part = mm(left[0][:, cols], right[0], TN) + mm(left[1][:, cols], right[1], TN)
            both[w, at] = part.astype(BF16)


def unit_grads(half, n2, n2_other, cot, up, dn, bias, wides):
    zs, tn, D = n2.shape
    U = up.shape[1]
    return pl.pallas_call(
        units_kernel,
        in_specs=[pl.BlockSpec(memory_space=pltpu.SMEM)] + [VMEM] * 6,
        out_specs=[VMEM] * 2,
        out_shape=[shape((wides, 2, D // wides, U), BF16), shape((8, U), F32)],
        scratch_shapes=[pltpu.VMEM((2, zs * tn, U), BF16)] * 2,
        compiler_params=PARAMS,
        cost_estimate=cost(9),
        name="unit_grads",
    )(half, n2, n2_other, cot, up, dn, bias)


def local(
    tokens,
    scene_ids,
    norm1_gain,
    norm1_shift,
    qkv_weight,
    qv_bias,
    out_weight,
    out_bias,
    norm2_gain,
    norm2_shift,
    up_weight,
    up_bias,
    down_weight,
    down_bias,
    cotangent,
):
    T, D = tokens.shape
    NW = lax.axis_size("wide")
    N = lax.axis_size("narrow")
    C = out_weight.shape[0]
    hh = C // HEAD_DIM
    U = up_weight.shape[1]
    zs = N // 2
    tn = T // N
    wid = lax.axis_index("wide")
    nid = lax.axis_index("narrow")
    core = wid % 2
    ybit = nid % 2
    zgroups = [list(range(0, N, 2)), list(range(1, N, 2))]
    row = lambda v: v.reshape(1, -1)

    def swap(v, axis, bit):
        size = lax.axis_size(axis)
        return lax.ppermute(v, axis, [(i, i ^ bit) for i in range(size)])

    def wide_scatter(v):
        bit = 1
        while bit < NW:
            pairs = v.reshape((v.shape[0] // 2, 2) + v.shape[1:])
            here = (wid // bit) % 2
            send = lax.dynamic_index_in_dim(pairs, 1 - here, 1, keepdims=False)
            keep = lax.dynamic_index_in_dim(pairs, here, 1, keepdims=False)
            got = swap(send, "wide", bit)
            v = (keep.astype(F32) + got.astype(F32)).astype(v.dtype)
            bit *= 2
        return v[0]

    def gather_rows(v):
        turn = lambda v, by: lax.ppermute(v, "narrow", [(i, (i + by) % N) for i in range(N)])
        blocks = [(v, 0)]
        theirs = [swap(v, "narrow", 1)]
        up, down = v, v
        for k in range(1, zs // 2 + 1):
            up = turn(up, 2)
            blocks.append((up, -k))
            theirs.append(swap(up, "narrow", 1))
            if 2 * k < zs:
                down = turn(down, -2)
                blocks.append((down, k))
                theirs.append(swap(down, "narrow", 1))
        out, total = place(nid.reshape(1), blocks, theirs, v.shape[0] - tn)
        return out.reshape(T, D), total

    def after(v, *done):
        return lax.optimization_barrier((v,) + done)[0]

    half_at = ybit.reshape(1)
    pack = pack_half(core.reshape(1), up_weight, down_weight, row(up_bias))
    near = swap(pack, "narrow", 1)
    tokens = after(tokens, pack)
    normed, q, mine = project(
        tokens, row(norm1_gain), row(norm1_shift), qkv_weight,
        row(qv_bias), scene_ids.reshape(T // 128, 128), hh,
    )

    kv = {0: mine}
    bit = 2
    while bit < NW:
        for k in list(kv):
            kv[k + bit] = swap(kv[k], "wide", bit)
        bit *= 2
    kv[1] = swap(mine, "wide", 1)

    w_near = swap(
        lax.dynamic_slice_in_dim(after(qkv_weight, mine), core * (D // 2), D // 2, 0), "narrow", 1
    )

    wo_cols = lax.dynamic_slice_in_dim(after(out_weight, mine), wid * (D // NW), D // NW, 1)
    wos = {
        0: lax.all_to_all(
            jnp.broadcast_to(wo_cols[None], (N, C, D // NW)),
            "narrow", split_axis=0, concat_axis=0, tiled=True,
        )
    }
    sums = None
    for k in range(0, NW, 2):
        if k:
            kv[k + 1] = swap(after(kv[k], sums), "wide", 1)
        sums = attend(hh, N, mine, q, [kv[k], kv[k + 1]], sums, k + 2 == NW)
        if k + 2 < NW:
            sums = sums[0]
    sends, mix32, qf = sums

    mix_half = lax.all_to_all(
        after(sends, wos[0], near, w_near), "narrow", split_axis=0, concat_axis=0, tiled=True
    )
    wos[0] = after(wos[0], sends)
    bit = 2
    while bit < NW:
        for k in list(wos):
            wos[k + bit] = swap(wos[k], "wide", bit)
        bit *= 2
    for k in list(wos):
        wos[k + 1] = swap(wos[k], "wide", 1)
    far = swap(after(near, sends), "wide", 1)
    w_far = swap(after(w_near, sends), "wide", 1)
    tok4 = tokens.reshape(zs, 2, tn, D)
    cot4 = after(cotangent, sends).reshape(zs, 2, tn, D)
    ga = before_middle(cot4, down_weight, far, near, half_at)
    direct = mm(cot4.reshape(T, D), out_weight, NT)
    mix_half = after(mix_half, direct, ga)
    a_parts, active, back, normed2, residual, sums2 = middle(
        mix_half, tok4, ga, [wos[k] for k in range(NW)], up_weight, row(up_bias), far, near,
        row(out_bias), row(norm2_gain), row(norm2_shift), half_at, wid.reshape(1),
    )
    arrived = lax.all_to_all(a_parts, "narrow", split_axis=0, concat_axis=0, tiled=True)
    rff, grad_out = after_middle(
        active, back, mix_half, cot4, down_weight, far, near, half_at, (nid // 2).reshape(1), NW
    )
    rff = after(rff, arrived)
    summed = lax.psum_scatter(
        rff, "narrow", scatter_dimension=0, tiled=True, axis_index_groups=zgroups
    ).reshape(tn, 2 * D)
    normed2_other = swap(after(normed2, arrived), "narrow", 1)
    mine_rows = lambda v: lax.dynamic_slice_in_dim(v, nid * tn, tn, 0)
    res_rows = lax.dynamic_index_in_dim(residual, nid // 2, 0, keepdims=False)
    output_rows = (res_rows + summed[:, D:].astype(F32) + down_bias).astype(BF16)
    rows_here = lax.all_gather(output_rows, "narrow", axis=0, axis_index_groups=zgroups)

    do, dof = gather_grad(
        hh, arrived.reshape(zs, 2, zs, tn, C), direct.reshape(zs, 2, tn, C), mix32
    )

    dq = None
    come = {k: [] for k in range(0, NW, 2)}
    for k in range(NW - 2, -1, -2):
        dq, other = attend_back(hh, mine, kv[k + 1], q, qf, do, dof, dq, False)
        home = swap(other, "wide", 1)
        dq, own = attend_back(hh, mine, kv[k], q, qf, do, dof, dq, k == 0)
        parts = [own, home] + come[k]
        if k:
            total = parts[0].astype(F32)
            for part in parts[1:]:
                total += part.astype(F32)
            top = 1 << (k.bit_length() - 1)
            come[k ^ top].append(swap(total.astype(BF16), "wide", top))
    dq = after(dq, normed2_other, output_rows)
    grads, send, grad_sums = collect(hh, half_at, dq, parts, zs)
    other = swap(send, "narrow", 1)
    part = project_back(grads, other, qkv_weight, w_near, w_far, half_at, core.reshape(1))
    sums_z = []
    for k in range(zs):
        to = lax.dynamic_index_in_dim(part, (nid // 2) ^ k, 0, keepdims=False)
        sums_z.append(swap(to, "narrow", 2 * k) if k else to)

    both, unit_sums = unit_grads(
        half_at, after(normed2, part), normed2_other, cot4, up_weight, down_weight, row(up_bias), NW
    )
    rows_there = swap(after(rows_here, part), "narrow", 1)
    grad_out = wide_scatter(after(grad_out, part)).reshape(zs, 2, C, D // NW)
    keep = lax.dynamic_index_in_dim(grad_out, ybit, 1, keepdims=False)
    send = lax.dynamic_index_in_dim(grad_out, 1 - ybit, 1, keepdims=False)
    grad_out = (keep.astype(F32) + swap(send, "narrow", 1).astype(F32)).astype(BF16)
    vectors = vector_sums(
        hh, NW, part, tok4, sums2, summed, cotangent, unit_sums, grad_sums, half_at, nid.reshape(1)
    )
    vectors = wide_scatter(vectors)
    tied = lax.optimization_barrier((*sums_z, vectors, both, grad_out))
    sums_z, vectors = tied[:zs], tied[zs]
    token_rows = finish(
        nid.reshape(1), sums_z, tokens, cotangent, summed,
        row(norm1_gain), vectors,
    )
    grad_tokens, final = gather_rows(token_rows)
    output = join(half_at, rows_here, rows_there).reshape(T, D)
    grad_out_w = (
        lax.all_to_all(
            after(grad_out, token_rows),
            "narrow", split_axis=0, concat_axis=0, tiled=True, axis_index_groups=zgroups,
        )
        .astype(F32)
        .sum(0)
    )
    grad_qkv = mm(normed, after(grads, token_rows).reshape(T, 3 * C), TN)
    grad_down_w, grad_up_w = wide_scatter(both).astype(F32)
    grad_qkv_w = wide_scatter(grad_qkv.astype(BF16).reshape(NW, D // NW, 3 * C)).astype(F32)
    final = final[:6, : D // NW]
    up_bias_out = vectors[6, : U // NW].reshape(1, -1)
    qv_out = vectors[7, : 2 * C // NW].reshape(1, -1)
    return (
        output,
        grad_tokens,
        final[0],
        final[1],
        grad_qkv_w,
        qv_out,
        grad_out_w,
        final[4],
        final[2],
        final[3],
        grad_up_w,
        up_bias_out,
        grad_down_w.T,
        final[5],
    )


def solution(mesh):
    in_specs = (
        P("wide", None),
        P("wide"),
        P(),
        P(),
        P(None, "narrow"),
        P("narrow"),
        P("narrow", None),
        P(),
        P(),
        P(),
        P(None, "narrow"),
        P("narrow"),
        P("narrow", None),
        P(),
        P("wide", None),
    )
    out_specs = (
        P("wide", None),
        P("wide", None),
        P("wide"),
        P("wide"),
        P("wide", "narrow"),
        P("narrow", "wide"),
        P("narrow", "wide"),
        P("wide"),
        P("wide"),
        P("wide"),
        P("wide", "narrow"),
        P("narrow", "wide"),
        P("narrow", "wide"),
        P("wide"),
    )
    return jax.shard_map(local, mesh=mesh, in_specs=in_specs, out_specs=out_specs, check_vma=False)
```

```python
import functools

import jax
import jax.numpy as jnp
from jax import lax
from jax.experimental import pallas as pl
from jax.experimental.pallas import tpu as pltpu
from jax.sharding import PartitionSpec as P

HEAD_DIM = 64
EPSILON = 1e-05
BIG = 2.0**100
SAFE = 40.0
ONE = 2
NT = (((1,), (1,)), ((), ()))
NN = (((1,), (0,)), ((), ()))
TN = (((0,), (0,)), ((), ()))
VMEM = pl.BlockSpec(memory_space=pltpu.VMEM)
F32 = jnp.float32
BF16 = jnp.bfloat16


PARAMS = pltpu.CompilerParams(vmem_limit_bytes=56 * 1024 * 1024)


def cost(us, weight=0.0):
    return pl.CostEstimate(flops=int(us * weight * 1.15e9), bytes_accessed=0, transcendentals=0)


def mm(a, b, dims=NN):
    return lax.dot_general(a, b, dims, preferred_element_type=F32)


def slot(at, size):
    return pl.ds(pl.multiple_of(at, size), size)


def shape(dims, dtype):
    return jax.ShapeDtypeStruct(dims, dtype)


def unit_rows(values):
    centre = jnp.mean(values, axis=-1, keepdims=True)
    centred = values - centre
    spread = jnp.mean(centred * centred, axis=-1, keepdims=True)
    scale = lax.rsqrt(spread + EPSILON)
    return centred * scale, scale


def norm_back(grad, unit, scale):
    first = jnp.mean(grad, axis=-1, keepdims=True)
    second = jnp.mean(grad * unit, axis=-1, keepdims=True)
    return (grad - first - unit * second) * scale


def gelu_parts(v):
    c = 0.7978845608028654
    square = v * v
    t = jnp.tanh(c * (v + 0.044715 * (v * square)))
    value = 0.5 * v * (1.0 + t)
    slope = 0.5 * (1.0 + t) + 0.5 * v * (1.0 - t * t) * (c * (1.0 + 3 * 0.044715 * square))
    return value, slope


def split3(v):
    a = v.astype(BF16)
    rest = v - a.astype(F32)
    b = rest.astype(BF16)
    return a, b, (rest - b.astype(F32)).astype(BF16)


def id_features(ids, start, change):
    n = ids.shape[0]
    row = lax.broadcasted_iota(jnp.int32, (128, 128), 0)
    lane = lax.broadcasted_iota(jnp.int32, (128, 128), 1)
    pick = lambda v: jnp.where(lane == 0, v[0], jnp.where(lane == 1, v[1], v[2]))
    spread = [
        jnp.where(row == lane, jnp.broadcast_to(ids[c : c + 1], (128, 128)), 0.0) for c in range(n)
    ]
    own = jnp.concatenate(spread, axis=0).astype(BF16)
    moved = mm(own, pick((change[0], change[1], 0.0)).astype(BF16))
    return (moved + pick(start)[0:1]).astype(BF16)


def key_features(ids):
    return id_features(ids, (-BIG, 0.0, 1.0), (BIG, -BIG))


def query_features(ids):
    return id_features(ids, (0.0, 1.0, 0.0), (1.0, -1.0))


def project_kernel(hh, T, blk, tok, gain, shift, w, bias, ids, normed, q_out, kvx, most):
    i = pl.program_id(0)
    extra = kvx.shape[0] - hh * T

    @pl.when(i == 0)
    def _():
        most[...] = jnp.zeros_like(most)
        rows = ids[...].astype(F32)
        rows = jnp.concatenate([rows, jnp.zeros((extra - rows.shape[0], 128), F32)], axis=0)
        kvx[hh * T :, :] = rows.astype(BF16)

    unit, _ = unit_rows(tok[...].astype(F32))
    low = (unit * gain[...] + shift[...]).astype(BF16)
    normed[...] = low
    zero = jnp.zeros((1, 64), F32)
    shifts = []
    for h in range(hh):
        shifts += [bias[:, h * 128 : h * 128 + 64], zero, bias[:, h * 128 + 64 : h * 128 + 128]]
    proj = mm(low, w[...]) + jnp.concatenate(shifts, axis=1)
    for h in range(hh):
        part = proj[:, h * 192 : h * 192 + 192]
        q = jnp.concatenate([part[:, :64] * 0.125, jnp.zeros((blk, 64), F32)], axis=1)
        q_out[h] = q.astype(BF16)
        kvx[slot(h * T + i * blk, blk), :] = part[:, 64:].astype(BF16)
    row = lax.broadcasted_iota(jnp.int32, (192 * hh, 128), 0) % 192
    lane = lax.broadcasted_iota(jnp.int32, (192 * hh, 128), 1)
    is_q = (lane // 2 == lax.broadcasted_iota(jnp.int32, (192 * hh, 128), 0) // 192) & (
        lane % 2 == 1
    )
    is_k = (lane // 2 == lax.broadcasted_iota(jnp.int32, (192 * hh, 128), 0) // 192) & (
        lane % 2 == 0
    )
    pick = jnp.where(is_q & (row < 64), 1.0 / 64, 0.0)
    pick = jnp.where(is_k & (row >= 64) & (row < 128), 1.0, pick).astype(BF16)
    lengths = mm((proj * proj).astype(BF16), pick)
    most[0:1] = jnp.maximum(most[0:1], jnp.max(lengths, axis=0, keepdims=True))

    @pl.when(i == T // blk - 1)
    def _():
        row = lax.broadcasted_iota(jnp.int32, (16, 128), 0)
        odd = lax.broadcasted_iota(jnp.int32, (1, 128), 1) % 2 == 1
        tops = jnp.where(row == 0, jnp.where(odd, 0.0, most[0:1]), 0.0)
        tops = jnp.where(row == 1, jnp.where(odd, most[0:1], 0.0), tops)
        kvx[hh * T + extra - 16 :, :] = (tops * 1.05).astype(BF16)


def project(tokens, gain, shift, w, bias, ids, hh):
    T, D = tokens.shape
    blk = min(256, T)
    extra = ids.shape[0] + -ids.shape[0] % 16 + 16
    whole = lambda *dims: pl.BlockSpec(dims, lambda i: (0,) * len(dims))
    return pl.pallas_call(
        functools.partial(project_kernel, hh, T, blk),
        grid=(T // blk,),
        in_specs=[
            pl.BlockSpec((blk, D), lambda i: (i, 0)),
            whole(1, D),
            whole(1, D),
            whole(D, 192 * hh),
            whole(*bias.shape),
            whole(*ids.shape),
        ],
        out_specs=[
            pl.BlockSpec((blk, D), lambda i: (i, 0)),
            pl.BlockSpec((hh, blk, 128), lambda i: (0, i, 0)),
            whole(hh * T + extra, 128),
        ],
        out_shape=[
            shape((T, D), BF16),
            shape((hh, T, 128), BF16),
            shape((hh * T + extra, 128), BF16),
        ],
        scratch_shapes=[pltpu.VMEM((8, 128), F32)],
        compiler_params=PARAMS,
        cost_estimate=cost(7),
        name="project",
    )(tokens, gain, shift, w, bias, ids)


def scene_rows(ref, tail, count):
    return ref[tail : tail + count + -count % 16, :].astype(F32)[:count]


def counts(ids, per, out, at):
    for j in range(ids.shape[0] // per):
        out[at + j] = jnp.sum(ids[j * per : (j + 1) * per])


def meets(a, na, b, nb):
    apart = ((a == 0) & (b == nb)) | ((a == na) & (b == 0))
    return jnp.logical_not(apart)


def attend_kernel(hh, T, nb, bq, bk, first, last, mine, q_ref, *refs):
    kvs = refs[:nb]
    refs = refs[nb:]
    if not first:
        acc_in = refs[0]
        refs = refs[1:]
    if last:
        sends, mix32, feat = refs[:3]
        refs = refs[3:]
    else:
        acc_out = refs[0]
        refs = refs[1:]
    acc_sc, m_sc, v_sc, qf_sc, kf_sc, spans, qspans, tops_sc = refs
    i = pl.program_id(0)
    trows = T // 128
    tail = hh * T
    lane = lax.broadcasted_iota(jnp.int32, (bq, 128), 1)

    @pl.when(i == 0)
    def _():
        ids = scene_rows(mine, tail, trows)
        counts(ids, bq // 128, qspans, 0)
        qf_sc[...] = query_features(ids)
        tops = kvs[0][-16:, :].astype(F32)
        wide = lax.broadcasted_iota(jnp.int32, (T, 128), 1)
        for b in range(nb):
            ids = scene_rows(kvs[b], tail, trows)
            counts(ids, bk // 128, spans, b * (T // bk))
            kf_sc[b] = key_features(ids)
            tops = jnp.maximum(tops, kvs[b][-16:, :].astype(F32))
            for h in range(hh):
                kv = kvs[b][h * T : (h + 1) * T, :]
                v_sc[b, h] = jnp.where(wide < 64, jnp.ones((), BF16), kv)
        tops_sc[0] = jnp.max(mine[-16:, :].astype(F32)[1:2]) * jnp.max(tops[0:1])

    calm = tops_sc[0] < SAFE * SAFE
    if first:
        acc_sc[...] = jnp.zeros_like(acc_sc)
    else:
        acc_sc[...] = acc_in[...]
        shift = acc_in[:, :, :1]
        calm = calm & (jnp.max(jnp.abs(shift)) == 0.0)
    m_sc[...] = jnp.zeros_like(m_sc)
    qr = slot(i * bq, bq)

    def block(b, h, j):
        rows = slot(h * T + j * bk, bk)
        return jnp.concatenate([kvs[b][rows, :], kf_sc[b, slot(j * bk, bk), :]], axis=1)

    @pl.when(jnp.logical_not(calm))
    def _():
        m_sc[...] = jnp.full(m_sc.shape, -2.0 * BIG, F32)

        def step(j, carry):
            for b in range(nb):
                for h in range(hh):
                    q = jnp.concatenate([q_ref[h], qf_sc[qr, :]], axis=1)
                    s = mm(q, block(b, h, j), NT)
                    m = jnp.max(s, axis=1, keepdims=True).astype(BF16).astype(F32)
                    m_sc[h] = jnp.maximum(m_sc[h], m)
            return carry

        lax.fori_loop(0, T // bk, step, 0)
        if not first:
            for h in range(hh):
                old = jnp.broadcast_to(acc_in[h, :, :1], (bq, 128))
                new = jnp.maximum(m_sc[h], old)
                acc_sc[h] = acc_sc[h] * jnp.exp(old - new)
                m_sc[h] = new

    qs = []
    for h in range(hh):
        feature = jnp.where(lane == ONE, (-m_sc[h]).astype(BF16), qf_sc[qr, :])
        qs.append(jnp.concatenate([q_ref[h], feature], axis=1))
    for b in range(nb):
        for j in range(T // bk):

            @pl.when(meets(qspans[i], bq, spans[b * (T // bk) + j], bk))
            def _():
                for h in range(hh):
                    p = jnp.exp(mm(qs[h], block(b, h, j), NT)).astype(BF16)
                    acc_sc[h] += mm(p, v_sc[b, h, j * bk : (j + 1) * bk, :])

    if not last:
        for h in range(hh):
            acc_out[h] = jnp.where(lane == 0, m_sc[h], acc_sc[h])
        return
    parts = []
    for h in range(hh):
        acc = acc_sc[h]
        total = acc[:, 1:2]
        mix = acc / total
        mix32[h] = mix
        parts.append(mix[:, 64:])
        a, b, c = split3(-(m_sc[h] + jnp.log(total)))
        feat[h] = jnp.where(
            lane == 2, a, jnp.where(lane == 3, b, jnp.where(lane == 4, c, qf_sc[qr, :]))
        )
    whole = jnp.concatenate(parts, axis=1) if hh > 1 else parts[0]
    count, zb, tn, c = sends.shape
    halves = whole.astype(BF16).reshape(zb, 2, tn, c)
    for n in range(count):
        sends[n] = halves[:, n % 2]


def attend(hh, devices, mine, q, kvs, before, last):
    T = q.shape[1]
    nb = len(kvs)
    bq = min(512, T)
    bk = min(1024, T)
    first = before is None
    zs, tn = devices // 2, T // devices
    rows = pl.BlockSpec((hh, bq, 128), lambda i: (0, i, 0))
    whole = lambda a: pl.BlockSpec(a.shape, lambda i: (0,) * a.ndim)
    if last:
        outs = [
            shape((devices, zs, tn, hh * 64), BF16),
            shape((hh, T, 128), F32),
            shape((hh, T, 128), BF16),
        ]
        specs = [
            pl.BlockSpec((devices, zs * bq // T, tn, hh * 64), lambda i: (0, i, 0, 0)),
            rows,
            rows,
        ]
    else:
        outs = [shape((hh, T, 128), F32)]
        specs = [rows]
    return pl.pallas_call(
        functools.partial(attend_kernel, hh, T, nb, bq, bk, first, last),
        grid=(T // bq,),
        in_specs=[whole(mine), rows] + [whole(kv) for kv in kvs] + ([] if first else [rows]),
        out_specs=specs,
        out_shape=outs,
        scratch_shapes=[
            pltpu.VMEM((hh, bq, 128), F32),
            pltpu.VMEM((hh, bq, 128), F32),
            pltpu.VMEM((nb, hh, T, 128), BF16),
            pltpu.VMEM((T, 128), BF16),
            pltpu.VMEM((nb, T, 128), BF16),
            pltpu.SMEM((nb * (T // bk),), F32),
            pltpu.SMEM((T // bq,), F32),
            pltpu.SMEM((1,), F32),
        ],
        compiler_params=PARAMS,
        cost_estimate=cost(8),
        name="attend",
    )(mine, q, *kvs, *(() if first else (before,)))


def pack_kernel(c_ref, up, dn, bias, out):
    half = dn.shape[0]
    D = dn.shape[1]
    for a in range(D // half):
        out[:half, a * half : (a + 1) * half] = up[a * half : (a + 1) * half, :]
    out[half : 2 * half, :] = dn[...]
    a, b, c = split3(bias[...])
    zero = jnp.zeros((1, D - 3 * half), F32)
    parts = [v.astype(F32) for v in (a, b, c)] + ([zero] if D > 3 * half else [])
    row = jnp.concatenate(parts, axis=1)
    out[2 * half :, :] = jnp.broadcast_to(row, (16, D)).astype(BF16)


def pack_half(core, up, dn, bias):
    D, U = up.shape
    half = U // 2
    return pl.pallas_call(
        pack_kernel,
        grid_spec=pltpu.PrefetchScalarGridSpec(
            num_scalar_prefetch=1,
            grid=(1,),
            in_specs=[
                pl.BlockSpec((D, half), lambda i, c: (0, c[0])),
                pl.BlockSpec((half, D), lambda i, c: (c[0], 0)),
                pl.BlockSpec((1, half), lambda i, c: (0, c[0])),
            ],
            out_specs=pl.BlockSpec((2 * half + 16, D), lambda i, c: (0, 0)),
        ),
        out_shape=shape((2 * half + 16, D), BF16),
        compiler_params=PARAMS,
        cost_estimate=cost(3),
        name="pack_half",
    )(core, up, dn, bias)


def pieces(own, far, near, half, units):
    up, dn, bias = own
    ahead = lambda v: mm(v, up[...])
    back = lambda v: mm(v, up[...], NT)
    yield slice(0, units), ahead, back, dn, bias
    for at, pack in enumerate((far, near)):
        D = pack.shape[1]
        tail = pack[2 * half :, :].astype(F32)
        bias = tail[0:1, :half] + tail[0:1, half : 2 * half] + tail[0:1, 2 * half : 3 * half]
        spans = [slice(a, a + half) for a in range(0, D, half)]

        def ahead(v, pack=pack):
            total = mm(v[:, spans[0]], pack[:half, spans[0]])
            for span in spans[1:]:
                total += mm(v[:, span], pack[:half, span])
            return total

        def back(v, pack=pack):
            return jnp.concatenate([mm(v, pack[:half, span], NT) for span in spans], axis=1)

        yield slice(units + at * half, units + (at + 1) * half), ahead, back, _Rows(
            pack, half, 2 * half
        ), bias


class _Rows:
    def __init__(self, ref, start, stop):
        self.ref, self.start, self.stop = ref, start, stop

    def __getitem__(self, at):
        return self.ref[self.start : self.stop, :]


def before_kernel(units, cot, dn_own, far, near, out):
    rows = cot.shape[0] * cot.shape[1]
    g = cot[...].reshape(rows, cot.shape[2])
    for cols, _, _, dn, _ in pieces((None, dn_own, None), far, near, units // 2, units):
        out[:, cols] = mm(g, dn[...], NT).astype(BF16)


def before_middle(cot, dn_own, far, near, half):
    zs, _, tn, D = cot.shape
    U = dn_own.shape[0]
    const = lambda a: pl.BlockSpec(a.shape, lambda i, y: (0,) * a.ndim)

    def kernel(y_ref, *refs):
        before_kernel(U, *refs)

    return pl.pallas_call(
        kernel,
        grid_spec=pltpu.PrefetchScalarGridSpec(
            num_scalar_prefetch=1,
            grid=(1,),
            in_specs=[pl.BlockSpec((zs, None, tn, D), lambda i, y: (0, y[0], 0, 0))]
            + [const(a) for a in (dn_own, far, near)],
            out_specs=pl.BlockSpec((zs * tn, 2 * U), lambda i, y: (0, 0)),
        ),
        out_shape=shape((zs * tn, 2 * U), BF16),
        compiler_params=PARAMS,
        cost_estimate=cost(3, 1.0),
        name="before_middle",
    )(half, cot, dn_own, far, near)


def middle_kernel(
    units, wid, count, mix, tok, ga, *refs,
):
    wos = refs[:count]
    middle_rest(units, wid, wos, mix, tok, ga, *refs[count:])


def middle_rest(
    units, wid, wos, mix, tok, ga, up_own, b_own, far, near, bo, g2, s2,
    a_out, active, back_out, normed2, res, sums, wo_sc,
):
    i = pl.program_id(0)

    @pl.when(i == 0)
    def _():
        sums[...] = jnp.zeros_like(sums)
        for k, part in enumerate(wos):
            wo_sc[wid ^ k] = part[...].reshape(wo_sc.shape[1:])

    wo = jnp.concatenate([wo_sc[k] for k in range(len(wos))], axis=1)
    n = mix.shape[0]
    D = tok.shape[-1]
    rows = tok.shape[0] * tok.shape[1]
    mixed = jnp.concatenate([mix[s].reshape(rows, mix.shape[-1]) for s in range(n)], axis=1)
    x = tok[...].reshape(rows, D).astype(F32)
    residual = x + mm(mixed, wo) + bo[...]
    unit, scale = unit_rows(residual)
    low = (unit * g2[...] + s2[...]).astype(BF16)
    res[...] = residual.reshape(res.shape)
    normed2[...] = low.reshape(normed2.shape)
    gn = jnp.zeros((rows, D), F32)
    for cols, ahead, back, _, bias in pieces(
        (up_own, None, b_own[...]), far, near, units // 2, units
    ):
        value, slope = gelu_parts(ahead(low) + bias)
        active[:, cols] = value.astype(BF16)
        gn += back((ga[:, cols].astype(F32) * slope).astype(BF16))
    back_low = norm_back(gn * g2[...], unit, scale).astype(BF16)
    back_out[...] = back_low.reshape(back_out.shape)
    a = mm(back_low, wo, NT).astype(BF16)
    c = a_out.shape[-1]
    for s in range(n):
        a_out[s] = a[:, s * c : (s + 1) * c].reshape(a_out.shape[1:])

    sums[0:1] += jnp.sum(gn * unit, axis=0, keepdims=True)
    sums[1:2] += jnp.sum(gn, axis=0, keepdims=True)
    sums[2:3] += jnp.sum(back_low.astype(F32), axis=0, keepdims=True)


def middle(mix, tok, ga, wos, up_own, b_own, far, near, bo, g2, s2, half, wid):
    n, zs, tn, c = mix.shape
    D = up_own.shape[0]
    U = up_own.shape[1]
    zb = max(1, zs // 2)
    const = lambda a: pl.BlockSpec(a.shape, lambda i, y, e: (0,) * a.ndim)
    rows = pl.BlockSpec((zb, tn, D), lambda i, y, e: (i, 0, 0))
    flat = pl.BlockSpec((zb * tn, 2 * U), lambda i, y, e: (i, 0))
    heads = pl.BlockSpec((n, zb, tn, c), lambda i, y, e: (0, i, 0, 0))

    def kernel(y_ref, e_ref, *refs):
        middle_kernel(U, e_ref[0], len(wos), *refs)

    return pl.pallas_call(
        kernel,
        grid_spec=pltpu.PrefetchScalarGridSpec(
            num_scalar_prefetch=2,
            grid=(zs // zb,),
            in_specs=[
                heads,
                pl.BlockSpec((zb, None, tn, D), lambda i, y, e: (i, y[0], 0, 0)),
                flat,
            ]
            + [const(a) for a in (*wos, up_own, b_own, far, near, bo, g2, s2)],
            out_specs=[heads, flat, rows, rows, rows, pl.BlockSpec((8, D), lambda i, y, e: (0, 0))],
            scratch_shapes=[pltpu.VMEM((len(wos), n * c, D // len(wos)), BF16)],
        ),
        out_shape=[
            shape((n, zs, tn, c), BF16),
            shape((zs * tn, 2 * U), BF16),
            shape((zs, tn, D), BF16),
            shape((zs, tn, D), BF16),
            shape((zs, tn, D), F32),
            shape((8, D), F32),
        ],
        compiler_params=PARAMS,
        cost_estimate=cost(12),
        name="middle",
    )(half, wid, mix, tok, ga, *wos, up_own, b_own, far, near, bo, g2, s2)


def after_kernel(units, y_ref, z_ref, active, back, mix, cot, dn_own, far, near, go, out):
    rows = active.shape[0]
    zs, tn, D = back.shape
    ff = jnp.zeros((rows, D), F32)
    for cols, _, _, dn, _ in pieces((None, dn_own, None), far, near, units // 2, units):
        ff += mm(active[:, cols], dn[...])
    out[...] = ff.astype(BF16).reshape(zs, tn, D)
    r = back[...].reshape(rows, D)
    g = jnp.where(z_ref[0] == 0, cot[...].reshape(rows, D), jnp.zeros((), BF16))
    c = mix.shape[-1]
    size = go.shape[2]
    for s in range(mix.shape[0]):
        heads = mix[s].reshape(rows, c)
        total = (mm(heads, r, TN) + mm(heads, g, TN)).astype(BF16)
        for k in range(go.shape[0]):
            go[k, s * c : (s + 1) * c, :] = total[:, k * size : (k + 1) * size]


def after_middle(active, back, mix, cot, dn_own, far, near, half, z, wides):
    n, zs, tn, c = mix.shape
    U, D = dn_own.shape
    const = lambda a: pl.BlockSpec(a.shape, lambda i, y, z: (0,) * a.ndim)
    return pl.pallas_call(
        functools.partial(after_kernel, U),
        grid_spec=pltpu.PrefetchScalarGridSpec(
            num_scalar_prefetch=2,
            grid=(1,),
            in_specs=[
                const(active),
                const(back),
                const(mix),
                pl.BlockSpec((zs, None, tn, D), lambda i, y, z: (0, y[0], 0, 0)),
            ]
            + [const(a) for a in (dn_own, far, near)],
            out_specs=[pl.BlockSpec((wides, n * c, D // wides), lambda i, y, z: (0, 0, 0))]
            + [pl.BlockSpec((zs, tn, D), lambda i, y, z: (0, 0, 0))],
        ),
        out_shape=[shape((wides, n * c, D // wides), BF16), shape((zs, tn, D), BF16)],
        compiler_params=PARAMS,
        cost_estimate=cost(6, 1.0),
        name="after_middle",
    )(half, z, active, back, mix, cot, dn_own, far, near)


def rows_kernel(z_ref, *refs):
    res, bias, out = refs[-3:]
    total = res[...] + bias[...]
    parts = refs[0]
    for k in range(parts.shape[0]):
        total += parts[k].astype(F32)
    for k in range(out.shape[0]):
        out[k] = total.astype(BF16)


def output_rows(z, parts, residual, bias):
    zs, tn, D = residual.shape
    same = lambda a: pl.BlockSpec(a.shape, lambda i, z: (0,) * a.ndim)
    return pl.pallas_call(
        rows_kernel,
        grid_spec=pltpu.PrefetchScalarGridSpec(
            num_scalar_prefetch=1,
            grid=(1,),
            in_specs=[
                same(parts),
                pl.BlockSpec((None, tn, D), lambda i, z: (z[0], 0, 0)),
                same(bias),
            ],
            out_specs=pl.BlockSpec((zs, tn, D), lambda i, z: (0, 0, 0)),
        ),
        out_shape=shape((zs, tn, D), BF16),
        compiler_params=PARAMS,
        cost_estimate=cost(2),
        name="output_rows",
    )(z, parts, residual, bias)


class _Row:
    def __init__(self, ref):
        self.ref = ref
        self.shape = (ref.shape[0], 1, ref.shape[1], ref.shape[2])

    def __getitem__(self, at):
        return self.ref[at]


def gather_kernel(hh, parts, direct, mix32, do, dof):
    rows = direct.shape[0] * direct.shape[2]
    c = direct.shape[-1]
    total = direct[...].reshape(rows, c)
    for s in range(parts.shape[0]):
        total += parts[s].reshape(rows, c).astype(F32)
    low = total.astype(BF16)
    lane = lax.broadcasted_iota(jnp.int32, (rows, 128), 1)
    for h in range(hh):
        grad = jnp.concatenate(
            [jnp.zeros((rows, 64), BF16), low[:, h * 64 : h * 64 + 64]], axis=1
        )
        mix = mix32[h].reshape(rows, 128)
        delta = jnp.sum(grad.astype(F32) * mix, axis=1, keepdims=True)
        a, b, e = split3(jnp.broadcast_to(-delta, (rows, 128)))
        zero = BF16(0)
        feature = jnp.where(lane == 2, a, jnp.where(lane == 3, b, jnp.where(lane == 4, e, zero)))
        do[h] = grad.reshape(do.shape[1:])
        dof[h] = feature.reshape(dof.shape[1:])


def gather_grad(hh, parts, direct, mix32):
    zs, _, _, tn, c = parts.shape
    T = 2 * zs * tn
    m4 = mix32.reshape(hh, zs, 2, tn, 128)
    wide = pl.BlockSpec((hh, zs, None, tn, 128), lambda y: (0, 0, y, 0, 0))

    def kernel(parts, direct, mix32, do, dof):
        gather_kernel(hh, parts, _Row(direct), mix32, do, dof)

    do, dof = pl.pallas_call(
        kernel,
        grid=(2,),
        in_specs=[
            pl.BlockSpec((zs, None, zs, tn, c), lambda y: (0, y, 0, 0, 0)),
            pl.BlockSpec((zs, None, tn, c), lambda y: (0, y, 0, 0)),
            wide,
        ],
        out_specs=[wide, wide],
        out_shape=[shape((hh, zs, 2, tn, 128), BF16)] * 2,
        compiler_params=PARAMS,
        cost_estimate=cost(3),
        name="gather_grad",
    )(parts, direct, m4)
    return do.reshape(hh, T, 128), dof.reshape(hh, T, 128)


def back_kernel(hh, T, bq, bk, first, last, mine, kv, q, qf, do, dof, *refs):
    if first:
        dq_out, dkv, dkv_sc, dq_sc, kf_sc, spans, qspans = refs
        dq_sc[...] = jnp.zeros_like(dq_sc)
    else:
        dq_in, dq_out, dkv, dkv_sc, dq_sc, kf_sc, spans, qspans = refs
        dq_sc[...] = dq_in[...]
    i = pl.program_id(0)
    trows = T // 128
    tail = hh * T

    @pl.when(i == 0)
    def _():
        dkv_sc[...] = jnp.zeros_like(dkv_sc)
        counts(scene_rows(mine, tail, trows), bq // 128, qspans, 0)
        ids = scene_rows(kv, tail, trows)
        counts(ids, bk // 128, spans, 0)
        kf_sc[...] = key_features(ids)

    for j in range(T // bk):

        @pl.when(meets(qspans[i], bq, spans[j], bk))
        def _():
            keys_at = slice(j * bk, (j + 1) * bk)
            kf = kf_sc[keys_at, :]
            for h in range(hh):
                keys = kv[h * T + j * bk : h * T + (j + 1) * bk, :]
                ka = jnp.concatenate([keys, kf], axis=1)
                p = jnp.exp(mm(ka, jnp.concatenate([q[h], qf[h]], axis=1), NT))
                dp = mm(ka, jnp.concatenate([do[h], dof[h]], axis=1), NT)
                ds = (p * dp).astype(BF16)
                dkv_sc[h, keys_at, :] += mm(ds, q[h]) + mm(p.astype(BF16), do[h])
                dq_sc[h] += mm(ds, keys, TN)

    if last:
        parts = [dq_sc[h][:, :64] * 0.125 for h in range(hh)]
        whole = jnp.concatenate(parts, axis=1) if hh > 1 else parts[0]
        dq_out[...] = whole.astype(BF16)
    else:
        dq_out[...] = dq_sc[...]

    @pl.when(i == T // bq - 1)
    def _():
        for h in range(hh):
            dkv[h * T : (h + 1) * T, :] = dkv_sc[h].astype(BF16)


def attend_back(hh, mine, kv, q, qf, do, dof, dq, last):
    T = q.shape[1]
    bq = min(512, T)
    bk = min(1024, T)
    first = dq is None
    rows = pl.BlockSpec((hh, bq, 128), lambda i: (0, i, 0))
    whole = lambda a: pl.BlockSpec(a.shape, lambda i: (0,) * a.ndim)
    if last:
        sums, sums_spec = shape((T, hh * 64), BF16), pl.BlockSpec((bq, hh * 64), lambda i: (i, 0))
    else:
        sums, sums_spec = shape((hh, T, 128), F32), rows
    return pl.pallas_call(
        functools.partial(back_kernel, hh, T, bq, bk, first, last),
        grid=(T // bq,),
        in_specs=[whole(mine), whole(kv)] + [rows] * (4 if first else 5),
        out_specs=[sums_spec, pl.BlockSpec((hh * T, 128), lambda i: (0, 0))],
        out_shape=[sums, shape((hh * T, 128), BF16)],
        scratch_shapes=[
            pltpu.VMEM((hh, T, 128), F32),
            pltpu.VMEM((hh, bq, 128), F32),
            pltpu.VMEM((T, 128), BF16),
            pltpu.SMEM((T // bk,), F32),
            pltpu.SMEM((T // bq,), F32),
        ],
        compiler_params=PARAMS,
        cost_estimate=cost(9, 1.0),
        name="attend_back",
    )(mine, kv, q, qf, do, dof, *(() if first else (dq,)))


def collect_kernel(hh, y_ref, gq, *refs):
    parts = refs[:-3]
    grads, send, sums = refs[-3:]
    zs, _, tn, width = grads.shape
    T = 2 * zs * tn
    cols = []
    for h in range(hh):
        total = parts[0][h * T : (h + 1) * T, :].astype(F32)
        for part in parts[1:]:
            total += part[h * T : (h + 1) * T, :].astype(F32)
        low = total.astype(BF16).astype(F32)
        cols += [gq[:, h * 64 : (h + 1) * 64].astype(F32), low]
    whole = jnp.concatenate(cols, axis=1)
    row = lax.broadcasted_iota(jnp.int32, (8, width), 0)
    sums[...] = jnp.where(row == 0, jnp.sum(whole, axis=0, keepdims=True), 0.0)
    halves = whole.astype(BF16).reshape(zs, 2, tn, width)
    grads[...] = halves
    send[...] = jnp.where(y_ref[0] == 0, halves[:, 1], halves[:, 0])


def collect(hh, half, gq, parts, zs):
    T = gq.shape[0]
    tn = T // zs // 2
    width = 192 * hh
    return pl.pallas_call(
        functools.partial(collect_kernel, hh),
        in_specs=[pl.BlockSpec(memory_space=pltpu.SMEM)] + [VMEM] * (1 + len(parts)),
        out_specs=[VMEM] * 3,
        out_shape=[
            shape((zs, 2, tn, width), BF16),
            shape((zs, tn, width), BF16),
            shape((8, width), F32),
        ],
        compiler_params=PARAMS,
        cost_estimate=cost(3),
        name="collect",
    )(half, gq, *parts)


def project_back(grads, other, w, w_near, w_far, tok, back, gain, half, core):
    zs, _, tn, width = grads.shape
    D = w.shape[0]
    rows = zs * tn

    def kernel(
        y_ref, c_ref, own, other, w, w_near, w_far, tok, back, gain, grad_out, out, w_sc
    ):
        w_sc[c_ref[0]] = w_near[...]
        w_sc[1 - c_ref[0]] = w_far[...]
        unit, scale = unit_rows(tok[...].reshape(rows, D).astype(F32))
        grad = mm(own[...].reshape(rows, width), w[...], NT)
        grad += mm(other[...].reshape(rows, width), w_sc[...].reshape(D, width), NT)
        grad_out[...] = grad.astype(BF16).reshape(grad_out.shape)
        total = back[...].reshape(rows, D).astype(F32) + norm_back(grad * gain[...], unit, scale)
        out[...] = total.astype(BF16).reshape(out.shape)

    const = lambda a: pl.BlockSpec(a.shape, lambda i, y, c: (0,) * a.ndim)
    own = lambda n: pl.BlockSpec((zs, None, tn, n), lambda i, y, c: (0, y[0], 0, 0))
    all_rows = pl.BlockSpec((zs, tn, D), lambda i, y, c: (0, 0, 0))
    return pl.pallas_call(
        kernel,
        grid_spec=pltpu.PrefetchScalarGridSpec(
            num_scalar_prefetch=2,
            grid=(1,),
            in_specs=[own(width), const(other), const(w), const(w_near), const(w_far), own(D)]
            + [const(back), const(gain)],
            out_specs=[all_rows, all_rows],
            scratch_shapes=[pltpu.VMEM((2, D // 2, width), BF16)],
        ),
        out_shape=[shape((zs, tn, D), BF16)] * 2,
        compiler_params=PARAMS,
        cost_estimate=cost(3, 1.0),
        name="project_back",
    )(half, core, grads, other, w, w_near, w_far, tok, back, gain)


def vector_sums(hh, wides, part, tok, sums2, cot, unit_sums, grad_sums, half, at):
    zs, tn, D = part.shape
    size = D // wides

    def kernel(y_ref, n_ref, part, tok, sums2, cot, unit_sums, grad_sums, out, sc):
        i = pl.program_id(0)
        unit, _ = unit_rows(tok[...].astype(F32))
        grad = part[...].astype(F32)

        @pl.when(i == 0)
        def _():
            sc[...] = jnp.zeros_like(sc)

        sc[0:1] += jnp.sum(grad * unit, axis=0, keepdims=True)
        sc[1:2] += jnp.sum(grad, axis=0, keepdims=True)

        @pl.when(i == zs - 1)
        def _():
            g = jnp.sum(cot[...].astype(F32), axis=0, keepdims=True)
            sc[2:4] = sums2[0:2]
            sc[4:5] = sums2[2:3] + g
            sc[5:6] = g
            pairs = []
            for h in range(hh):
                first = h * 192
                pairs += [grad_sums[0:1, first : first + 64], grad_sums[0:1, first + 128 : first + 192]]
            heads = jnp.concatenate(pairs, axis=1)
            for k in range(wides):
                out[k] = sc[:, k * size : (k + 1) * size]
                for row, v in ((6, unit_sums[0:1]), (7, heads)):
                    n = v.shape[1] // wides
                    mine = v[:, k * n : (k + 1) * n]
                    if n < size:
                        mine = jnp.concatenate([mine, jnp.zeros((1, size - n), F32)], axis=1)
                    out[k, row : row + 1] = mine

    whole = lambda a: pl.BlockSpec(a.shape, lambda i, y, n: (0,) * a.ndim)
    return pl.pallas_call(
        kernel,
        grid_spec=pltpu.PrefetchScalarGridSpec(
            num_scalar_prefetch=2,
            grid=(zs,),
            in_specs=[
                pl.BlockSpec((None, tn, D), lambda i, y, n: (i, 0, 0)),
                pl.BlockSpec((None, None, tn, D), lambda i, y, n: (i, y[0], 0, 0)),
                whole(sums2),
                pl.BlockSpec((tn, D), lambda i, y, n: (n[0], 0)),
                whole(unit_sums),
                whole(grad_sums),
            ],
            out_specs=pl.BlockSpec((wides, 8, size), lambda i, y, n: (0, 0, 0)),
            scratch_shapes=[pltpu.VMEM((8, D), F32)],
        ),
        out_shape=shape((wides, 8, size), F32),
        compiler_params=PARAMS,
        cost_estimate=cost(3, 1.0),
        name="vector_sums",
    )(half, at, part, tok, sums2, cot, unit_sums, grad_sums)


def finish_kernel(at, *refs):
    cot, vec, out = refs[-3:]
    total = cot[...].astype(F32)
    for k in range(refs[0].shape[0]):
        total += refs[0][k].astype(F32)
    tn, D = total.shape
    out[:tn, :] = total.astype(BF16)
    rows = jnp.concatenate([vec[...], jnp.zeros_like(vec)], axis=0).astype(BF16)
    out[tn:, :] = jnp.concatenate([rows, jnp.zeros((16, D - rows.shape[1]), BF16)], axis=1)


def finish(at, parts, cot, vec):
    zs, tn, D = parts.shape
    return pl.pallas_call(
        finish_kernel,
        grid_spec=pltpu.PrefetchScalarGridSpec(
            num_scalar_prefetch=1,
            grid=(1,),
            in_specs=[
                pl.BlockSpec((zs, tn, D), lambda i, n: (0, 0, 0)),
                pl.BlockSpec((tn, D), lambda i, n: (n[0], 0)),
                pl.BlockSpec(vec.shape, lambda i, n: (0, 0)),
            ],
            out_specs=pl.BlockSpec((tn + 16, D), lambda i, n: (0, 0)),
        ),
        out_shape=shape((tn + 16, D), BF16),
        compiler_params=PARAMS,
        cost_estimate=cost(2),
        name="finish",
    )(at, parts, cot, vec)


def place(nid, mine, theirs, tail):
    moves = [move for _, move in mine]
    rows, D = theirs[0].shape
    tn = rows - tail
    zs = len(moves)

    def kernel(n_ref, *refs):
        out, total = refs[-2:]
        z, y = n_ref[0] // 2, n_ref[0] % 2
        total[...] = jnp.zeros_like(total)
        for k, move in enumerate(moves):
            to = lax.rem(z + move + zs, zs)
            out[to, y] = refs[k][:tn, :]
            out[to, 1 - y] = refs[zs + k][:tn, :]
            total[...] += refs[k][tn:, :].astype(F32) + refs[zs + k][tn:, :].astype(F32)

    return pl.pallas_call(
        kernel,
        in_specs=[pl.BlockSpec(memory_space=pltpu.SMEM)] + [VMEM] * (2 * zs),
        out_specs=[VMEM] * 2,
        out_shape=[shape((zs, 2, tn, D), BF16), shape((tail, D), F32)],
        compiler_params=PARAMS,
        cost_estimate=cost(2),
        name="place",
    )(nid, *[v for v, _ in mine], *theirs)


def join(y, mine, theirs):
    zs, tn, D = mine.shape

    def kernel(y_ref, mine, theirs, out):
        out[:, y_ref[0]] = mine[...]
        out[:, 1 - y_ref[0]] = theirs[...]

    return pl.pallas_call(
        kernel,
        in_specs=[pl.BlockSpec(memory_space=pltpu.SMEM)] + [VMEM] * 2,
        out_specs=VMEM,
        out_shape=shape((zs, 2, tn, D), BF16),
        compiler_params=PARAMS,
        cost_estimate=cost(2),
        name="join",
    )(y, mine, theirs)


def units_kernel(
    y_ref, n2, n2_other, cot, up, dn, bias, normed, grads, out, sums, act_sc, grad_sc
):
    zs, _, tn, D = cot.shape
    rows = zs * tn
    U = up.shape[1]
    halves = cot[...]
    swap = y_ref[0] == 1
    g = [
        jnp.where(swap, halves[:, 1], halves[:, 0]).reshape(rows, D),
        jnp.where(swap, halves[:, 0], halves[:, 1]).reshape(rows, D),
    ]
    lows = [n2[...].reshape(rows, D), n2_other[...].reshape(rows, D)]
    total = jnp.zeros((1, U), F32)
    for k in range(2):
        value, slope = gelu_parts(mm(lows[k], up[...]) + bias[...])
        act_sc[k] = value.astype(BF16)
        grad = (mm(g[k], dn[...], NT) * slope).astype(BF16)
        grad_sc[k] = grad
        total += jnp.sum(grad.astype(F32), axis=0, keepdims=True)
    row = lax.broadcasted_iota(jnp.int32, (8, U), 0)
    sums[...] = jnp.where(row == 0, total, 0.0)
    wides = out.shape[0]
    size = D // wides
    heads = grads[...].reshape(2 * rows, grads.shape[-1])
    blank = jnp.zeros((size, U - heads.shape[1]), F32)
    for w in range(wides):
        cols = slice(w * size, (w + 1) * size)
        for at, left, right in ((0, g, act_sc), (1, lows, grad_sc)):
            part = mm(left[0][:, cols], right[0], TN) + mm(left[1][:, cols], right[1], TN)
            out[w, at * size : (at + 1) * size, :] = part.astype(BF16)
        part = jnp.concatenate([mm(normed[:, cols], heads, TN), blank], axis=1)
        out[w, 2 * size :, :] = part.astype(BF16)


def unit_grads(half, n2, n2_other, cot, up, dn, bias, normed, grads, wides):
    zs, tn, D = n2.shape
    U = up.shape[1]
    return pl.pallas_call(
        units_kernel,
        in_specs=[pl.BlockSpec(memory_space=pltpu.SMEM)] + [VMEM] * 8,
        out_specs=[VMEM] * 2,
        out_shape=[shape((wides, 3 * (D // wides), U), BF16), shape((8, U), F32)],
        scratch_shapes=[pltpu.VMEM((2, zs * tn, U), BF16)] * 2,
        compiler_params=PARAMS,
        cost_estimate=cost(0),
        name="unit_grads",
    )(half, n2, n2_other, cot, up, dn, bias, normed, grads)


def local(
    tokens,
    scene_ids,
    norm1_gain,
    norm1_shift,
    qkv_weight,
    qv_bias,
    out_weight,
    out_bias,
    norm2_gain,
    norm2_shift,
    up_weight,
    up_bias,
    down_weight,
    down_bias,
    cotangent,
):
    T, D = tokens.shape
    NW = lax.axis_size("wide")
    N = lax.axis_size("narrow")
    C = out_weight.shape[0]
    hh = C // HEAD_DIM
    U = up_weight.shape[1]
    zs = N // 2
    tn = T // N
    wid = lax.axis_index("wide")
    nid = lax.axis_index("narrow")
    core = wid % 2
    ybit = nid % 2
    zgroups = [list(range(0, N, 2)), list(range(1, N, 2))]
    row = lambda v: v.reshape(1, -1)

    def swap(v, axis, bit):
        size = lax.axis_size(axis)
        return lax.ppermute(v, axis, [(i, i ^ bit) for i in range(size)])

    def wide_scatter(v):
        bit = 1
        while bit < NW:
            pairs = v.reshape((v.shape[0] // 2, 2) + v.shape[1:])
            here = (wid // bit) % 2
            send = lax.dynamic_index_in_dim(pairs, 1 - here, 1, keepdims=False)
            keep = lax.dynamic_index_in_dim(pairs, here, 1, keepdims=False)
            got = swap(send, "wide", bit)
            v = (keep.astype(F32) + got.astype(F32)).astype(v.dtype)
            bit *= 2
        return v[0]

    turn = lambda v, by: lax.ppermute(v, "narrow", [(i, (i + by) % N) for i in range(N)])

    def gather_z(v):
        blocks = [(v, 0)]
        up, down = v, v
        for k in range(1, zs // 2 + 1):
            up = turn(up, 2)
            blocks.append((up, -k))
            if 2 * k < zs:
                down = turn(down, -2)
                blocks.append((down, k))
        return blocks

    def gather_rows(v, *beside):
        blocks = gather_z(v)
        theirs = [swap(block, "narrow", 1) for block, _ in blocks]
        out, total = place(nid.reshape(1), blocks, theirs, v.shape[0] - tn)
        beside = lax.optimization_barrier((*beside, *theirs[1:-1]))[: len(beside)]
        return out.reshape(T, D), total, *beside

    def after(v, *done):
        return lax.optimization_barrier((v,) + done)[0]

    half_at = ybit.reshape(1)
    pack = pack_half(core.reshape(1), up_weight, down_weight, row(up_bias))
    near = swap(pack, "narrow", 1)
    tokens = after(tokens, pack)
    normed, q, mine = project(
        tokens, row(norm1_gain), row(norm1_shift), qkv_weight,
        row(qv_bias), scene_ids.reshape(T // 128, 128), hh,
    )

    kv = {0: mine}
    bit = 2
    while bit < NW:
        for k in list(kv):
            kv[k + bit] = swap(kv[k], "wide", bit)
        bit *= 2
    kv[1] = swap(mine, "wide", 1)

    w_near = swap(
        lax.dynamic_slice_in_dim(after(qkv_weight, mine), core * (D // 2), D // 2, 0), "narrow", 1
    )

    wo_cols = lax.dynamic_slice_in_dim(after(out_weight, mine), wid * (D // NW), D // NW, 1)
    wos = {
        0: lax.all_to_all(
            jnp.broadcast_to(wo_cols[None], (N, C, D // NW)),
            "narrow", split_axis=0, concat_axis=0, tiled=True,
        )
    }
    sums = None
    for k in range(0, NW, 2):
        if k:
            kv[k + 1] = swap(after(kv[k], sums), "wide", 1)
        sums = attend(hh, N, mine, q, [kv[k], kv[k + 1]], sums, k + 2 == NW)
        if k + 2 < NW:
            sums = sums[0]
    sends, mix32, qf = sums

    mix_half = lax.all_to_all(
        after(sends, wos[0], near), "narrow", split_axis=0, concat_axis=0, tiled=True
    )
    wos[0] = after(wos[0], sends)
    bit = 2
    while bit < NW:
        for k in list(wos):
            wos[k + bit] = swap(wos[k], "wide", bit)
        bit *= 2
    for k in list(wos):
        wos[k + 1] = swap(wos[k], "wide", 1)
    far = swap(after(near, sends), "wide", 1)
    w_far = swap(after(w_near, sends), "wide", 1)
    tok4 = tokens.reshape(zs, 2, tn, D)
    cot4 = after(cotangent, sends).reshape(zs, 2, tn, D)
    ga = before_middle(cot4, down_weight, far, near, half_at)
    direct = mm(cot4.reshape(T, D), out_weight, NT)
    mix_half = after(mix_half, direct, ga, w_near)
    a_parts, active, back, normed2, residual, sums2 = middle(
        mix_half, tok4, ga, [wos[k] for k in range(NW)], up_weight, row(up_bias), far, near,
        row(out_bias), row(norm2_gain), row(norm2_shift), half_at, wid.reshape(1),
    )
    arrived = lax.all_to_all(a_parts, "narrow", split_axis=0, concat_axis=0, tiled=True)
    z_at = (nid // 2).reshape(1)
    grad_out, ffs = after_middle(
        active, back, mix_half, cot4, down_weight, far, near, half_at, z_at, NW
    )
    grad_out = wide_scatter(grad_out)
    arrived, ffs = lax.optimization_barrier((arrived, ffs))
    exchange_z = lambda v: lax.all_to_all(
        v, "narrow", split_axis=0, concat_axis=0, tiled=True, axis_index_groups=zgroups
    )
    ffs = exchange_z(ffs)
    normed2_other = swap(after(normed2, arrived), "narrow", 1)
    do, dof = gather_grad(
        hh, arrived.reshape(zs, 2, zs, tn, C), direct.reshape(zs, 2, tn, C), mix32
    )

    dq = None
    come = {k: [] for k in range(0, NW, 2)}
    sent = []
    for k in range(NW - 2, -1, -2):
        dq, other = attend_back(hh, mine, kv[k + 1], q, qf, do, dof, dq, False)
        home = swap(other, "wide", 1)
        if k == 0:
            out_rows = output_rows(z_at, after(ffs, dq, *sent), residual, row(down_bias))
            rows_here = exchange_z(out_rows)
            dq = after(dq, out_rows, normed2_other, grad_out)
        dq, own = attend_back(hh, mine, kv[k], q, qf, do, dof, dq, k == 0)
        parts = [own, home] + come[k]
        if k:
            total = parts[0].astype(F32)
            for part in parts[1:]:
                total += part.astype(F32)
            top = 1 << (k.bit_length() - 1)
            sent = [total.astype(BF16)]
            come[k ^ top].append(swap(sent[0], "wide", top))
    grads, send, grad_sums = collect(hh, half_at, dq, parts, zs)
    other = swap(send, "narrow", 1)
    both, unit_sums = unit_grads(
        half_at, normed2, normed2_other, cot4, up_weight, down_weight, row(up_bias),
        normed, after(grads, send), NW,
    )
    part, back_all = project_back(
        grads, after(other, both, rows_here), qkv_weight, w_near, w_far, tok4, back, row(norm1_gain),
        half_at, core.reshape(1),
    )
    back_all = exchange_z(back_all)
    weights = wide_scatter(after(both, part))

    grad_out = after(grad_out, part).reshape(zs, 2, C, D // NW)
    keep = lax.dynamic_index_in_dim(grad_out, ybit, 1, keepdims=False)
    send = lax.dynamic_index_in_dim(grad_out, 1 - ybit, 1, keepdims=False)
    grad_out = (keep.astype(F32) + swap(send, "narrow", 1).astype(F32)).astype(BF16)
    rows_there = swap(after(rows_here, grad_out), "narrow", 1)
    grad_out_w = 0.0
    for k in range(zs):
        to = lax.dynamic_index_in_dim(grad_out, (nid // 2) ^ k, 0, keepdims=False)
        grad_out_w += (swap(to, "narrow", 2 * k) if k else to).astype(F32)
    vectors = vector_sums(
        hh, NW, part, tok4, sums2, cotangent, unit_sums, grad_sums, half_at, nid.reshape(1)
    )
    vectors = wide_scatter(vectors)
    back_all, vectors = lax.optimization_barrier((back_all, vectors, grad_out_w))[:2]
    token_rows = finish(
        nid.reshape(1), back_all, cotangent, vectors
    )
    grad_tokens, final, rows_there = gather_rows(token_rows, rows_there)
    output = join(half_at, rows_here, rows_there).reshape(T, D)
    size = D // NW
    grad_down_w = weights[:size].astype(F32).T
    grad_up_w = weights[size : 2 * size].astype(F32)
    grad_qkv_w = weights[2 * size :, : 3 * C].astype(F32)
    final = final[:6, : D // NW]
    up_bias_out = vectors[6, : U // NW].reshape(1, -1)
    qv_out = vectors[7, : 2 * C // NW].reshape(1, -1)
    return (
        output,
        grad_tokens,
        final[0],
        final[1],
        grad_qkv_w,
        qv_out,
        grad_out_w,
        final[4],
        final[2],
        final[3],
        grad_up_w,
        up_bias_out,
        grad_down_w,
        final[5],
    )


def solution(mesh):
    in_specs = (
        P("wide", None),
        P("wide"),
        P(),
        P(),
        P(None, "narrow"),
        P("narrow"),
        P("narrow", None),
        P(),
        P(),
        P(),
        P(None, "narrow"),
        P("narrow"),
        P("narrow", None),
        P(),
        P("wide", None),
    )
    out_specs = (
        P("wide", None),
        P("wide", None),
        P("wide"),
        P("wide"),
        P("wide", "narrow"),
        P("narrow", "wide"),
        P("narrow", "wide"),
        P("wide"),
        P("wide"),
        P("wide"),
        P("wide", "narrow"),
        P("narrow", "wide"),
        P("narrow", "wide"),
        P("wide"),
    )
    return jax.shard_map(local, mesh=mesh, in_specs=in_specs, out_specs=out_specs, check_vma=False)
```

```python
import functools

import jax
import jax.numpy as jnp
from jax import lax
from jax.experimental import pallas as pl
from jax.experimental.pallas import tpu as pltpu
from jax.sharding import PartitionSpec as P

HEAD_DIM = 64
EPSILON = 1e-05
BIG = 2.0**100
SAFE = 40.0
ONE = 2
NT = (((1,), (1,)), ((), ()))
NN = (((1,), (0,)), ((), ()))
TN = (((0,), (0,)), ((), ()))
VMEM = pl.BlockSpec(memory_space=pltpu.VMEM)
F32 = jnp.float32
BF16 = jnp.bfloat16


def limit(mib):
    return pltpu.CompilerParams(vmem_limit_bytes=mib * 1024 * 1024)


PARAMS = limit(56)


def cost(us, weight=0.0):
    return pl.CostEstimate(flops=int(us * weight * 1.15e9), bytes_accessed=0, transcendentals=0)


def mm(a, b, dims=NN):
    return lax.dot_general(a, b, dims, preferred_element_type=F32)


def slot(at, size):
    return pl.ds(pl.multiple_of(at, size), size)


def shape(dims, dtype):
    return jax.ShapeDtypeStruct(dims, dtype)


def unit_rows(values):
    centre = jnp.mean(values, axis=-1, keepdims=True)
    centred = values - centre
    spread = jnp.mean(centred * centred, axis=-1, keepdims=True)
    scale = lax.rsqrt(spread + EPSILON)
    return centred * scale, scale


def norm_back(grad, unit, scale):
    first = jnp.mean(grad, axis=-1, keepdims=True)
    second = jnp.mean(grad * unit, axis=-1, keepdims=True)
    return (grad - first - unit * second) * scale


def gelu_parts(v):
    c = 0.7978845608028654
    square = v * v
    t = jnp.tanh(c * (v + 0.044715 * (v * square)))
    value = 0.5 * v * (1.0 + t)
    slope = 0.5 * (1.0 + t) + 0.5 * v * (1.0 - t * t) * (c * (1.0 + 3 * 0.044715 * square))
    return value, slope


def split3(v):
    a = v.astype(BF16)
    rest = v - a.astype(F32)
    b = rest.astype(BF16)
    return a, b, (rest - b.astype(F32)).astype(BF16)


def id_features(ids, start, change):
    n = ids.shape[0]
    row = lax.broadcasted_iota(jnp.int32, (128, 128), 0)
    lane = lax.broadcasted_iota(jnp.int32, (128, 128), 1)
    pick = lambda v: jnp.where(lane == 0, v[0], jnp.where(lane == 1, v[1], v[2]))
    spread = [
        jnp.where(row == lane, jnp.broadcast_to(ids[c : c + 1], (128, 128)), 0.0) for c in range(n)
    ]
    own = jnp.concatenate(spread, axis=0).astype(BF16)
    moved = mm(own, pick((change[0], change[1], 0.0)).astype(BF16))
    return (moved + pick(start)[0:1]).astype(BF16)


def key_features(ids):
    return id_features(ids, (-BIG, 0.0, 1.0), (BIG, -BIG))


def query_features(ids):
    return id_features(ids, (0.0, 1.0, 0.0), (1.0, -1.0))


def project_kernel(hh, T, blk, tok, gain, shift, w, bias, ids, normed, q_out, kvx, most):
    i = pl.program_id(0)
    extra = kvx.shape[0] - hh * T

    @pl.when(i == 0)
    def _():
        most[...] = jnp.zeros_like(most)
        rows = ids[...].astype(F32)
        rows = jnp.concatenate([rows, jnp.zeros((extra - rows.shape[0], 128), F32)], axis=0)
        kvx[hh * T :, :] = rows.astype(BF16)

    unit, _ = unit_rows(tok[...].astype(F32))
    low = (unit * gain[...] + shift[...]).astype(BF16)
    normed[...] = low
    zero = jnp.zeros((1, 64), F32)
    shifts = []
    for h in range(hh):
        shifts += [bias[:, h * 128 : h * 128 + 64], zero, bias[:, h * 128 + 64 : h * 128 + 128]]
    proj = mm(low, w[...]) + jnp.concatenate(shifts, axis=1)
    for h in range(hh):
        part = proj[:, h * 192 : h * 192 + 192]
        q = jnp.concatenate([part[:, :64] * 0.125, jnp.zeros((blk, 64), F32)], axis=1)
        q_out[h] = q.astype(BF16)
        kvx[slot(h * T + i * blk, blk), :] = part[:, 64:].astype(BF16)
    row = lax.broadcasted_iota(jnp.int32, (192 * hh, 128), 0) % 192
    lane = lax.broadcasted_iota(jnp.int32, (192 * hh, 128), 1)
    is_q = (lane // 2 == lax.broadcasted_iota(jnp.int32, (192 * hh, 128), 0) // 192) & (
        lane % 2 == 1
    )
    is_k = (lane // 2 == lax.broadcasted_iota(jnp.int32, (192 * hh, 128), 0) // 192) & (
        lane % 2 == 0
    )
    pick = jnp.where(is_q & (row < 64), 1.0 / 64, 0.0)
    pick = jnp.where(is_k & (row >= 64) & (row < 128), 1.0, pick).astype(BF16)
    lengths = mm((proj * proj).astype(BF16), pick)
    most[0:1] = jnp.maximum(most[0:1], jnp.max(lengths, axis=0, keepdims=True))

    @pl.when(i == T // blk - 1)
    def _():
        row = lax.broadcasted_iota(jnp.int32, (16, 128), 0)
        odd = lax.broadcasted_iota(jnp.int32, (1, 128), 1) % 2 == 1
        tops = jnp.where(row == 0, jnp.where(odd, 0.0, most[0:1]), 0.0)
        tops = jnp.where(row == 1, jnp.where(odd, most[0:1], 0.0), tops)
        kvx[hh * T + extra - 16 :, :] = (tops * 1.05).astype(BF16)


def project(tokens, gain, shift, w, bias, ids, hh):
    T, D = tokens.shape
    blk = min(256, T)
    extra = ids.shape[0] + -ids.shape[0] % 16 + 16
    whole = lambda *dims: pl.BlockSpec(dims, lambda i: (0,) * len(dims))
    return pl.pallas_call(
        functools.partial(project_kernel, hh, T, blk),
        grid=(T // blk,),
        in_specs=[
            pl.BlockSpec((blk, D), lambda i: (i, 0)),
            whole(1, D),
            whole(1, D),
            whole(D, 192 * hh),
            whole(*bias.shape),
            whole(*ids.shape),
        ],
        out_specs=[
            pl.BlockSpec((blk, D), lambda i: (i, 0)),
            pl.BlockSpec((hh, blk, 128), lambda i: (0, i, 0)),
            whole(hh * T + extra, 128),
        ],
        out_shape=[
            shape((T, D), BF16),
            shape((hh, T, 128), BF16),
            shape((hh * T + extra, 128), BF16),
        ],
        scratch_shapes=[pltpu.VMEM((8, 128), F32)],
        compiler_params=PARAMS,
        cost_estimate=cost(7),
        name="project",
    )(tokens, gain, shift, w, bias, ids)


def scene_rows(ref, tail, count):
    return ref[tail : tail + count + -count % 16, :].astype(F32)[:count]


def counts(ids, per, out, at):
    for j in range(ids.shape[0] // per):
        out[at + j] = jnp.sum(ids[j * per : (j + 1) * per])


def meets(a, na, b, nb):
    apart = ((a == 0) & (b == nb)) | ((a == na) & (b == 0))
    return jnp.logical_not(apart)


def attend_kernel(hh, T, nb, bq, bk, first, last, mine, q_ref, *refs):
    kvs = refs[:nb]
    refs = refs[nb:]
    if not first:
        acc_in = refs[0]
        refs = refs[1:]
    if last:
        sends, mix32, feat = refs[:3]
        refs = refs[3:]
    else:
        acc_out = refs[0]
        refs = refs[1:]
    acc_sc, m_sc, v_sc, qf_sc, kf_sc, spans, qspans, tops_sc = refs
    i = pl.program_id(0)
    trows = T // 128
    tail = hh * T
    lane = lax.broadcasted_iota(jnp.int32, (bq, 128), 1)

    @pl.when(i == 0)
    def _():
        ids = scene_rows(mine, tail, trows)
        counts(ids, bq // 128, qspans, 0)
        qf_sc[...] = query_features(ids)
        tops = kvs[0][-16:, :].astype(F32)
        wide = lax.broadcasted_iota(jnp.int32, (T, 128), 1)
        for b in range(nb):
            ids = scene_rows(kvs[b], tail, trows)
            counts(ids, bk // 128, spans, b * (T // bk))
            kf_sc[b] = key_features(ids)
            tops = jnp.maximum(tops, kvs[b][-16:, :].astype(F32))
            for h in range(hh):
                kv = kvs[b][h * T : (h + 1) * T, :]
                v_sc[b, h] = jnp.where(wide < 64, jnp.ones((), BF16), kv)
        tops_sc[0] = jnp.max(mine[-16:, :].astype(F32)[1:2]) * jnp.max(tops[0:1])

    calm = tops_sc[0] < SAFE * SAFE
    if first:
        acc_sc[...] = jnp.zeros_like(acc_sc)
    else:
        acc_sc[...] = acc_in[...]
        shift = acc_in[:, :, :1]
        calm = calm & (jnp.max(jnp.abs(shift)) == 0.0)
    m_sc[...] = jnp.zeros_like(m_sc)
    qr = slot(i * bq, bq)

    def block(b, h, j):
        rows = slot(h * T + j * bk, bk)
        return jnp.concatenate([kvs[b][rows, :], kf_sc[b, slot(j * bk, bk), :]], axis=1)

    @pl.when(jnp.logical_not(calm))
    def _():
        m_sc[...] = jnp.full(m_sc.shape, -2.0 * BIG, F32)

        def step(j, carry):
            for b in range(nb):
                for h in range(hh):
                    q = jnp.concatenate([q_ref[h], qf_sc[qr, :]], axis=1)
                    s = mm(q, block(b, h, j), NT)
                    m = jnp.max(s, axis=1, keepdims=True).astype(BF16).astype(F32)
                    m_sc[h] = jnp.maximum(m_sc[h], m)
            return carry

        lax.fori_loop(0, T // bk, step, 0)
        if not first:
            for h in range(hh):
                old = jnp.broadcast_to(acc_in[h, :, :1], (bq, 128))
                new = jnp.maximum(m_sc[h], old)
                acc_sc[h] = acc_sc[h] * jnp.exp(old - new)
                m_sc[h] = new

    qs = []
    for h in range(hh):
        feature = jnp.where(lane == ONE, (-m_sc[h]).astype(BF16), qf_sc[qr, :])
        qs.append(jnp.concatenate([q_ref[h], feature], axis=1))
    for b in range(nb):
        for j in range(T // bk):

            @pl.when(meets(qspans[i], bq, spans[b * (T // bk) + j], bk))
            def _():
                for h in range(hh):
                    p = jnp.exp(mm(qs[h], block(b, h, j), NT)).astype(BF16)
                    acc_sc[h] += mm(p, v_sc[b, h, j * bk : (j + 1) * bk, :])

    if not last:
        for h in range(hh):
            acc_out[h] = jnp.where(lane == 0, m_sc[h], acc_sc[h])
        return
    parts = []
    for h in range(hh):
        acc = acc_sc[h]
        total = acc[:, 1:2]
        mix = acc / total
        mix32[h] = mix
        parts.append(mix[:, 64:])
        a, b, c = split3(-(m_sc[h] + jnp.log(total)))
        feat[h] = jnp.where(
            lane == 2, a, jnp.where(lane == 3, b, jnp.where(lane == 4, c, qf_sc[qr, :]))
        )
    whole = jnp.concatenate(parts, axis=1) if hh > 1 else parts[0]
    count, zb, tn, c = sends.shape
    halves = whole.astype(BF16).reshape(zb, 2, tn, c)
    for n in range(count):
        sends[n] = halves[:, n % 2]


def attend(hh, devices, mine, q, kvs, before, last):
    T = q.shape[1]
    nb = len(kvs)
    bq = min(512, T)
    bk = min(1024, T)
    first = before is None
    zs, tn = devices // 2, T // devices
    rows = pl.BlockSpec((hh, bq, 128), lambda i: (0, i, 0))
    whole = lambda a: pl.BlockSpec(a.shape, lambda i: (0,) * a.ndim)
    if last:
        outs = [
            shape((devices, zs, tn, hh * 64), BF16),
            shape((hh, T, 128), F32),
            shape((hh, T, 128), BF16),
        ]
        specs = [
            pl.BlockSpec((devices, zs * bq // T, tn, hh * 64), lambda i: (0, i, 0, 0)),
            rows,
            rows,
        ]
    else:
        outs = [shape((hh, T, 128), F32)]
        specs = [rows]
    return pl.pallas_call(
        functools.partial(attend_kernel, hh, T, nb, bq, bk, first, last),
        grid=(T // bq,),
        in_specs=[whole(mine), rows] + [whole(kv) for kv in kvs] + ([] if first else [rows]),
        out_specs=specs,
        out_shape=outs,
        scratch_shapes=[
            pltpu.VMEM((hh, bq, 128), F32),
            pltpu.VMEM((hh, bq, 128), F32),
            pltpu.VMEM((nb, hh, T, 128), BF16),
            pltpu.VMEM((T, 128), BF16),
            pltpu.VMEM((nb, T, 128), BF16),
            pltpu.SMEM((nb * (T // bk),), F32),
            pltpu.SMEM((T // bq,), F32),
            pltpu.SMEM((1,), F32),
        ],
        compiler_params=limit(24),
        cost_estimate=cost(8),
        name="attend",
    )(mine, q, *kvs, *(() if first else (before,)))


def pack_kernel(c_ref, up, dn, bias, out):
    half = dn.shape[0]
    D = dn.shape[1]
    for a in range(D // half):
        out[:half, a * half : (a + 1) * half] = up[a * half : (a + 1) * half, :]
    out[half : 2 * half, :] = dn[...]
    a, b, c = split3(bias[...])
    zero = jnp.zeros((1, D - 3 * half), F32)
    parts = [v.astype(F32) for v in (a, b, c)] + ([zero] if D > 3 * half else [])
    row = jnp.concatenate(parts, axis=1)
    out[2 * half :, :] = jnp.broadcast_to(row, (16, D)).astype(BF16)


def pack_half(core, up, dn, bias):
    D, U = up.shape
    half = U // 2
    return pl.pallas_call(
        pack_kernel,
        grid_spec=pltpu.PrefetchScalarGridSpec(
            num_scalar_prefetch=1,
            grid=(1,),
            in_specs=[
                pl.BlockSpec((D, half), lambda i, c: (0, c[0])),
                pl.BlockSpec((half, D), lambda i, c: (c[0], 0)),
                pl.BlockSpec((1, half), lambda i, c: (0, c[0])),
            ],
            out_specs=pl.BlockSpec((2 * half + 16, D), lambda i, c: (0, 0)),
        ),
        out_shape=shape((2 * half + 16, D), BF16),
        compiler_params=PARAMS,
        cost_estimate=cost(3),
        name="pack_half",
    )(core, up, dn, bias)


def pieces(own, far, near, half, units):
    up, dn, bias = own
    ahead = lambda v: mm(v, up[...])
    back = lambda v: mm(v, up[...], NT)
    yield slice(0, units), ahead, back, dn, bias
    for at, pack in enumerate((far, near)):
        D = pack.shape[1]
        tail = pack[2 * half :, :].astype(F32)
        bias = tail[0:1, :half] + tail[0:1, half : 2 * half] + tail[0:1, 2 * half : 3 * half]
        spans = [slice(a, a + half) for a in range(0, D, half)]

        def ahead(v, pack=pack):
            total = mm(v[:, spans[0]], pack[:half, spans[0]])
            for span in spans[1:]:
                total += mm(v[:, span], pack[:half, span])
            return total

        def back(v, pack=pack):
            return jnp.concatenate([mm(v, pack[:half, span], NT) for span in spans], axis=1)

        yield slice(units + at * half, units + (at + 1) * half), ahead, back, _Rows(
            pack, half, 2 * half
        ), bias


class _Rows:
    def __init__(self, ref, start, stop):
        self.ref, self.start, self.stop = ref, start, stop

    def __getitem__(self, at):
        return self.ref[self.start : self.stop, :]


def before_kernel(units, cot, dn_own, far, near, out):
    rows = cot.shape[0] * cot.shape[1]
    g = cot[...].reshape(rows, cot.shape[2])
    for cols, _, _, dn, _ in pieces((None, dn_own, None), far, near, units // 2, units):
        out[:, cols] = mm(g, dn[...], NT).astype(BF16)


def before_middle(cot, dn_own, far, near, half):
    zs, _, tn, D = cot.shape
    U = dn_own.shape[0]
    const = lambda a: pl.BlockSpec(a.shape, lambda i, y: (0,) * a.ndim)

    def kernel(y_ref, *refs):
        before_kernel(U, *refs)

    return pl.pallas_call(
        kernel,
        grid_spec=pltpu.PrefetchScalarGridSpec(
            num_scalar_prefetch=1,
            grid=(1,),
            in_specs=[pl.BlockSpec((zs, None, tn, D), lambda i, y: (0, y[0], 0, 0))]
            + [const(a) for a in (dn_own, far, near)],
            out_specs=pl.BlockSpec((zs * tn, 2 * U), lambda i, y: (0, 0)),
        ),
        out_shape=shape((zs * tn, 2 * U), BF16),
        compiler_params=PARAMS,
        cost_estimate=cost(3, 1.0),
        name="before_middle",
    )(half, cot, dn_own, far, near)


def middle_kernel(
    units, wid, count, mix, tok, ga, *refs,
):
    wos = refs[:count]
    middle_rest(units, wid, wos, mix, tok, ga, *refs[count:])


def middle_rest(
    units, wid, wos, mix, tok, ga, up_own, b_own, far, near, bo, g2, s2,
    a_out, active, back_out, normed2, res, sums, wo_sc,
):
    i = pl.program_id(0)

    @pl.when(i == 0)
    def _():
        sums[...] = jnp.zeros_like(sums)
        for k, part in enumerate(wos):
            wo_sc[wid ^ k] = part[...].reshape(wo_sc.shape[1:])

    wo = jnp.concatenate([wo_sc[k] for k in range(len(wos))], axis=1)
    n = mix.shape[0]
    D = tok.shape[-1]
    rows = tok.shape[0] * tok.shape[1]
    mixed = jnp.concatenate([mix[s].reshape(rows, mix.shape[-1]) for s in range(n)], axis=1)
    x = tok[...].reshape(rows, D).astype(F32)
    residual = x + mm(mixed, wo) + bo[...]
    unit, scale = unit_rows(residual)
    low = (unit * g2[...] + s2[...]).astype(BF16)
    res[...] = residual.reshape(res.shape)
    normed2[...] = low.reshape(normed2.shape)
    gn = jnp.zeros((rows, D), F32)
    for cols, ahead, back, _, bias in pieces(
        (up_own, None, b_own[...]), far, near, units // 2, units
    ):
        value, slope = gelu_parts(ahead(low) + bias)
        active[:, cols] = value.astype(BF16)
        gn += back((ga[:, cols].astype(F32) * slope).astype(BF16))
    back_low = norm_back(gn * g2[...], unit, scale).astype(BF16)
    back_out[...] = back_low.reshape(back_out.shape)
    a = mm(back_low, wo, NT).astype(BF16)
    c = a_out.shape[-1]
    for s in range(n):
        a_out[s] = a[:, s * c : (s + 1) * c].reshape(a_out.shape[1:])

    sums[0:1] += jnp.sum(gn * unit, axis=0, keepdims=True)
    sums[1:2] += jnp.sum(gn, axis=0, keepdims=True)
    sums[2:3] += jnp.sum(back_low.astype(F32), axis=0, keepdims=True)


def middle(mix, tok, ga, wos, up_own, b_own, far, near, bo, g2, s2, half, wid):
    n, zs, tn, c = mix.shape
    D = up_own.shape[0]
    U = up_own.shape[1]
    zb = zs
    const = lambda a: pl.BlockSpec(a.shape, lambda i, y, e: (0,) * a.ndim)
    rows = pl.BlockSpec((zb, tn, D), lambda i, y, e: (i, 0, 0))
    flat = pl.BlockSpec((zb * tn, 2 * U), lambda i, y, e: (i, 0))
    heads = pl.BlockSpec((n, zb, tn, c), lambda i, y, e: (0, i, 0, 0))

    def kernel(y_ref, e_ref, *refs):
        middle_kernel(U, e_ref[0], len(wos), *refs)

    return pl.pallas_call(
        kernel,
        grid_spec=pltpu.PrefetchScalarGridSpec(
            num_scalar_prefetch=2,
            grid=(zs // zb,),
            in_specs=[
                heads,
                pl.BlockSpec((zb, None, tn, D), lambda i, y, e: (i, y[0], 0, 0)),
                flat,
            ]
            + [const(a) for a in (*wos, up_own, b_own, far, near, bo, g2, s2)],
            out_specs=[heads, flat, rows, rows, rows, pl.BlockSpec((8, D), lambda i, y, e: (0, 0))],
            scratch_shapes=[pltpu.VMEM((len(wos), n * c, D // len(wos)), BF16)],
        ),
        out_shape=[
            shape((n, zs, tn, c), BF16),
            shape((zs * tn, 2 * U), BF16),
            shape((zs, tn, D), BF16),
            shape((zs, tn, D), BF16),
            shape((zs, tn, D), F32),
            shape((8, D), F32),
        ],
        compiler_params=PARAMS,
        cost_estimate=cost(12),
        name="middle",
    )(half, wid, mix, tok, ga, *wos, up_own, b_own, far, near, bo, g2, s2)


def after_kernel(units, y_ref, z_ref, active, back, mix, cot, dn_own, far, near, go, out):
    rows = active.shape[0]
    zs, tn, D = back.shape
    ff = jnp.zeros((rows, D), F32)
    for cols, _, _, dn, _ in pieces((None, dn_own, None), far, near, units // 2, units):
        ff += mm(active[:, cols], dn[...])
    out[...] = ff.astype(BF16).reshape(zs, tn, D)
    r = back[...].reshape(rows, D)
    g = jnp.where(z_ref[0] == 0, cot[...].reshape(rows, D), jnp.zeros((), BF16))
    c = mix.shape[-1]
    size = go.shape[2]
    for s in range(mix.shape[0]):
        heads = mix[s].reshape(rows, c)
        total = (mm(heads, r, TN) + mm(heads, g, TN)).astype(BF16)
        for k in range(go.shape[0]):
            go[k, s * c : (s + 1) * c, :] = total[:, k * size : (k + 1) * size]


def after_middle(active, back, mix, cot, dn_own, far, near, half, z, wides):
    n, zs, tn, c = mix.shape
    U, D = dn_own.shape
    const = lambda a: pl.BlockSpec(a.shape, lambda i, y, z: (0,) * a.ndim)
    return pl.pallas_call(
        functools.partial(after_kernel, U),
        grid_spec=pltpu.PrefetchScalarGridSpec(
            num_scalar_prefetch=2,
            grid=(1,),
            in_specs=[
                const(active),
                const(back),
                const(mix),
                pl.BlockSpec((zs, None, tn, D), lambda i, y, z: (0, y[0], 0, 0)),
            ]
            + [const(a) for a in (dn_own, far, near)],
            out_specs=[pl.BlockSpec((wides, n * c, D // wides), lambda i, y, z: (0, 0, 0))]
            + [pl.BlockSpec((zs, tn, D), lambda i, y, z: (0, 0, 0))],
        ),
        out_shape=[shape((wides, n * c, D // wides), BF16), shape((zs, tn, D), BF16)],
        compiler_params=PARAMS,
        cost_estimate=cost(6, 1.0),
        name="after_middle",
    )(half, z, active, back, mix, cot, dn_own, far, near)


def rows_kernel(z_ref, *refs):
    res, bias, out = refs[-3:]
    total = res[...] + bias[...]
    parts = refs[0]
    for k in range(parts.shape[0]):
        total += parts[k].astype(F32)
    for k in range(out.shape[0]):
        out[k] = total.astype(BF16)


def output_rows(z, parts, residual, bias):
    zs, tn, D = residual.shape
    same = lambda a: pl.BlockSpec(a.shape, lambda i, z: (0,) * a.ndim)
    return pl.pallas_call(
        rows_kernel,
        grid_spec=pltpu.PrefetchScalarGridSpec(
            num_scalar_prefetch=1,
            grid=(1,),
            in_specs=[
                same(parts),
                pl.BlockSpec((None, tn, D), lambda i, z: (z[0], 0, 0)),
                same(bias),
            ],
            out_specs=pl.BlockSpec((zs, tn, D), lambda i, z: (0, 0, 0)),
        ),
        out_shape=shape((zs, tn, D), BF16),
        compiler_params=limit(32),
        cost_estimate=cost(2),
        name="output_rows",
    )(z, parts, residual, bias)


class _Row:
    def __init__(self, ref):
        self.ref = ref
        self.shape = (ref.shape[0], 1, ref.shape[1], ref.shape[2])

    def __getitem__(self, at):
        return self.ref[at]


def gather_kernel(hh, parts, direct, mix32, do, dof):
    rows = direct.shape[0] * direct.shape[2]
    c = direct.shape[-1]
    total = direct[...].reshape(rows, c)
    for s in range(parts.shape[0]):
        total += parts[s].reshape(rows, c).astype(F32)
    low = total.astype(BF16)
    lane = lax.broadcasted_iota(jnp.int32, (rows, 128), 1)
    for h in range(hh):
        grad = jnp.concatenate(
            [jnp.zeros((rows, 64), BF16), low[:, h * 64 : h * 64 + 64]], axis=1
        )
        mix = mix32[h].reshape(rows, 128)
        delta = jnp.sum(grad.astype(F32) * mix, axis=1, keepdims=True)
        a, b, e = split3(jnp.broadcast_to(-delta, (rows, 128)))
        zero = BF16(0)
        feature = jnp.where(lane == 2, a, jnp.where(lane == 3, b, jnp.where(lane == 4, e, zero)))
        do[h] = grad.reshape(do.shape[1:])
        dof[h] = feature.reshape(dof.shape[1:])


def gather_grad(hh, parts, direct, mix32):
    zs, _, _, tn, c = parts.shape
    T = 2 * zs * tn
    m4 = mix32.reshape(hh, zs, 2, tn, 128)
    wide = pl.BlockSpec((hh, zs, None, tn, 128), lambda y: (0, 0, y, 0, 0))

    def kernel(parts, direct, mix32, do, dof):
        gather_kernel(hh, parts, _Row(direct), mix32, do, dof)

    do, dof = pl.pallas_call(
        kernel,
        grid=(2,),
        in_specs=[
            pl.BlockSpec((zs, None, zs, tn, c), lambda y: (0, y, 0, 0, 0)),
            pl.BlockSpec((zs, None, tn, c), lambda y: (0, y, 0, 0)),
            wide,
        ],
        out_specs=[wide, wide],
        out_shape=[shape((hh, zs, 2, tn, 128), BF16)] * 2,
        compiler_params=limit(32),
        cost_estimate=cost(3),
        name="gather_grad",
    )(parts, direct, m4)
    return do.reshape(hh, T, 128), dof.reshape(hh, T, 128)


def back_kernel(hh, T, bq, bk, first, last, mine, kv, q, qf, do, dof, *refs):
    if first:
        dq_out, dkv, dkv_sc, dq_sc, kf_sc, spans, qspans = refs
        dq_sc[...] = jnp.zeros_like(dq_sc)
    else:
        dq_in, dq_out, dkv, dkv_sc, dq_sc, kf_sc, spans, qspans = refs
        dq_sc[...] = dq_in[...]
    i = pl.program_id(0)
    trows = T // 128
    tail = hh * T

    @pl.when(i == 0)
    def _():
        dkv_sc[...] = jnp.zeros_like(dkv_sc)
        counts(scene_rows(mine, tail, trows), bq // 128, qspans, 0)
        ids = scene_rows(kv, tail, trows)
        counts(ids, bk // 128, spans, 0)
        kf_sc[...] = key_features(ids)

    for j in range(T // bk):

        @pl.when(meets(qspans[i], bq, spans[j], bk))
        def _():
            keys_at = slice(j * bk, (j + 1) * bk)
            kf = kf_sc[keys_at, :]
            for h in range(hh):
                keys = kv[h * T + j * bk : h * T + (j + 1) * bk, :]
                ka = jnp.concatenate([keys, kf], axis=1)
                p = jnp.exp(mm(ka, jnp.concatenate([q[h], qf[h]], axis=1), NT))
                dp = mm(ka, jnp.concatenate([do[h], dof[h]], axis=1), NT)
                ds = (p * dp).astype(BF16)
                dkv_sc[h, keys_at, :] += mm(ds, q[h]) + mm(p.astype(BF16), do[h])
                dq_sc[h] += mm(ds, keys, TN)

    if last:
        parts = [dq_sc[h][:, :64] * 0.125 for h in range(hh)]
        whole = jnp.concatenate(parts, axis=1) if hh > 1 else parts[0]
        dq_out[...] = whole.astype(BF16)
    else:
        dq_out[...] = dq_sc[...]

    @pl.when(i == T // bq - 1)
    def _():
        for h in range(hh):
            dkv[h * T : (h + 1) * T, :] = dkv_sc[h].astype(BF16)


def attend_back(hh, mine, kv, q, qf, do, dof, dq, last):
    T = q.shape[1]
    bq = min(512, T)
    bk = min(1024, T)
    first = dq is None
    rows = pl.BlockSpec((hh, bq, 128), lambda i: (0, i, 0))
    whole = lambda a: pl.BlockSpec(a.shape, lambda i: (0,) * a.ndim)
    if last:
        sums, sums_spec = shape((T, hh * 64), BF16), pl.BlockSpec((bq, hh * 64), lambda i: (i, 0))
    else:
        sums, sums_spec = shape((hh, T, 128), F32), rows
    return pl.pallas_call(
        functools.partial(back_kernel, hh, T, bq, bk, first, last),
        grid=(T // bq,),
        in_specs=[whole(mine), whole(kv)] + [rows] * (4 if first else 5),
        out_specs=[sums_spec, pl.BlockSpec((hh * T, 128), lambda i: (0, 0))],
        out_shape=[sums, shape((hh * T, 128), BF16)],
        scratch_shapes=[
            pltpu.VMEM((hh, T, 128), F32),
            pltpu.VMEM((hh, bq, 128), F32),
            pltpu.VMEM((T, 128), BF16),
            pltpu.SMEM((T // bk,), F32),
            pltpu.SMEM((T // bq,), F32),
        ],
        compiler_params=limit(32),
        cost_estimate=cost(9, 1.0),
        name="attend_back",
    )(mine, kv, q, qf, do, dof, *(() if first else (dq,)))


def collect_kernel(hh, y_ref, gq, *refs):
    parts = refs[:-3]
    grads, send, sums = refs[-3:]
    zs, _, tn, width = grads.shape
    T = 2 * zs * tn
    cols = []
    for h in range(hh):
        total = parts[0][h * T : (h + 1) * T, :].astype(F32)
        for part in parts[1:]:
            total += part[h * T : (h + 1) * T, :].astype(F32)
        low = total.astype(BF16).astype(F32)
        cols += [gq[:, h * 64 : (h + 1) * 64].astype(F32), low]
    whole = jnp.concatenate(cols, axis=1)
    row = lax.broadcasted_iota(jnp.int32, (8, width), 0)
    sums[...] = jnp.where(row == 0, jnp.sum(whole, axis=0, keepdims=True), 0.0)
    halves = whole.astype(BF16).reshape(zs, 2, tn, width)
    grads[...] = halves
    send[...] = jnp.where(y_ref[0] == 0, halves[:, 1], halves[:, 0])


def collect(hh, half, gq, parts, zs):
    T = gq.shape[0]
    tn = T // zs // 2
    width = 192 * hh
    return pl.pallas_call(
        functools.partial(collect_kernel, hh),
        in_specs=[pl.BlockSpec(memory_space=pltpu.SMEM)] + [VMEM] * (1 + len(parts)),
        out_specs=[VMEM] * 3,
        out_shape=[
            shape((zs, 2, tn, width), BF16),
            shape((zs, tn, width), BF16),
            shape((8, width), F32),
        ],
        compiler_params=limit(32),
        cost_estimate=cost(3),
        name="collect",
    )(half, gq, *parts)


def project_back(grads, other, w, w_near, w_far, tok, back, gain, half, core):
    zs, _, tn, width = grads.shape
    D = w.shape[0]
    rows = zs * tn

    def kernel(
        y_ref, c_ref, own, other, w, w_near, w_far, tok, back, gain, grad_out, out, w_sc
    ):
        w_sc[c_ref[0]] = w_near[...]
        w_sc[1 - c_ref[0]] = w_far[...]
        unit, scale = unit_rows(tok[...].reshape(rows, D).astype(F32))
        grad = mm(own[...].reshape(rows, width), w[...], NT)
        grad += mm(other[...].reshape(rows, width), w_sc[...].reshape(D, width), NT)
        grad_out[...] = grad.astype(BF16).reshape(grad_out.shape)
        total = back[...].reshape(rows, D).astype(F32) + norm_back(grad * gain[...], unit, scale)
        out[...] = total.astype(BF16).reshape(out.shape)

    const = lambda a: pl.BlockSpec(a.shape, lambda i, y, c: (0,) * a.ndim)
    own = lambda n: pl.BlockSpec((zs, None, tn, n), lambda i, y, c: (0, y[0], 0, 0))
    all_rows = pl.BlockSpec((zs, tn, D), lambda i, y, c: (0, 0, 0))
    return pl.pallas_call(
        kernel,
        grid_spec=pltpu.PrefetchScalarGridSpec(
            num_scalar_prefetch=2,
            grid=(1,),
            in_specs=[own(width), const(other), const(w), const(w_near), const(w_far), own(D)]
            + [const(back), const(gain)],
            out_specs=[all_rows, all_rows],
            scratch_shapes=[pltpu.VMEM((2, D // 2, width), BF16)],
        ),
        out_shape=[shape((zs, tn, D), BF16)] * 2,
        compiler_params=PARAMS,
        cost_estimate=cost(3, 1.0),
        name="project_back",
    )(half, core, grads, other, w, w_near, w_far, tok, back, gain)


def vector_sums(hh, wides, part, tok, sums2, cot, unit_sums, grad_sums, half, at):
    zs, tn, D = part.shape
    size = D // wides

    def kernel(y_ref, n_ref, part, tok, sums2, cot, unit_sums, grad_sums, out, sc):
        i = pl.program_id(0)
        unit, _ = unit_rows(tok[...].astype(F32))
        grad = part[...].astype(F32)

        @pl.when(i == 0)
        def _():
            sc[...] = jnp.zeros_like(sc)

        sc[0:1] += jnp.sum(grad * unit, axis=0, keepdims=True)
        sc[1:2] += jnp.sum(grad, axis=0, keepdims=True)

        @pl.when(i == zs - 1)
        def _():
            g = jnp.sum(cot[...].astype(F32), axis=0, keepdims=True)
            sc[2:4] = sums2[0:2]
            sc[4:5] = sums2[2:3] + g
            sc[5:6] = g
            pairs = []
            for h in range(hh):
                first = h * 192
                pairs += [grad_sums[0:1, first : first + 64], grad_sums[0:1, first + 128 : first + 192]]
            heads = jnp.concatenate(pairs, axis=1)
            for k in range(wides):
                out[k] = sc[:, k * size : (k + 1) * size]
                for row, v in ((6, unit_sums[0:1]), (7, heads)):
                    n = v.shape[1] // wides
                    mine = v[:, k * n : (k + 1) * n]
                    if n < size:
                        mine = jnp.concatenate([mine, jnp.zeros((1, size - n), F32)], axis=1)
                    out[k, row : row + 1] = mine

    whole = lambda a: pl.BlockSpec(a.shape, lambda i, y, n: (0,) * a.ndim)
    return pl.pallas_call(
        kernel,
        grid_spec=pltpu.PrefetchScalarGridSpec(
            num_scalar_prefetch=2,
            grid=(zs,),
            in_specs=[
                pl.BlockSpec((None, tn, D), lambda i, y, n: (i, 0, 0)),
                pl.BlockSpec((None, None, tn, D), lambda i, y, n: (i, y[0], 0, 0)),
                whole(sums2),
                pl.BlockSpec((tn, D), lambda i, y, n: (n[0], 0)),
                whole(unit_sums),
                whole(grad_sums),
            ],
            out_specs=pl.BlockSpec((wides, 8, size), lambda i, y, n: (0, 0, 0)),
            scratch_shapes=[pltpu.VMEM((8, D), F32)],
        ),
        out_shape=shape((wides, 8, size), F32),
        compiler_params=PARAMS,
        cost_estimate=cost(3, 1.0),
        name="vector_sums",
    )(half, at, part, tok, sums2, cot, unit_sums, grad_sums)


def finish_kernel(at, *refs):
    cot, vec, out = refs[-3:]
    total = cot[...].astype(F32)
    for k in range(refs[0].shape[0]):
        total += refs[0][k].astype(F32)
    tn, D = total.shape
    out[:tn, :] = total.astype(BF16)
    rows = jnp.concatenate([vec[...], jnp.zeros_like(vec)], axis=0).astype(BF16)
    out[tn:, :] = jnp.concatenate([rows, jnp.zeros((16, D - rows.shape[1]), BF16)], axis=1)


def finish(at, parts, cot, vec):
    zs, tn, D = parts.shape
    return pl.pallas_call(
        finish_kernel,
        grid_spec=pltpu.PrefetchScalarGridSpec(
            num_scalar_prefetch=1,
            grid=(1,),
            in_specs=[
                pl.BlockSpec((zs, tn, D), lambda i, n: (0, 0, 0)),
                pl.BlockSpec((tn, D), lambda i, n: (n[0], 0)),
                pl.BlockSpec(vec.shape, lambda i, n: (0, 0)),
            ],
            out_specs=pl.BlockSpec((tn + 16, D), lambda i, n: (0, 0)),
        ),
        out_shape=shape((tn + 16, D), BF16),
        compiler_params=PARAMS,
        cost_estimate=cost(2),
        name="finish",
    )(at, parts, cot, vec)


def place(nid, mine, theirs, tail):
    moves = [move for _, move in mine]
    rows, D = theirs[0].shape
    tn = rows - tail
    zs = len(moves)

    def kernel(n_ref, *refs):
        out, total = refs[-2:]
        z, y = n_ref[0] // 2, n_ref[0] % 2
        total[...] = jnp.zeros_like(total)
        for k, move in enumerate(moves):
            to = lax.rem(z + move + zs, zs)
            out[to, y] = refs[k][:tn, :]
            out[to, 1 - y] = refs[zs + k][:tn, :]
            total[...] += refs[k][tn:, :].astype(F32) + refs[zs + k][tn:, :].astype(F32)

    return pl.pallas_call(
        kernel,
        in_specs=[pl.BlockSpec(memory_space=pltpu.SMEM)] + [VMEM] * (2 * zs),
        out_specs=[VMEM] * 2,
        out_shape=[shape((zs, 2, tn, D), BF16), shape((tail, D), F32)],
        compiler_params=PARAMS,
        cost_estimate=cost(2),
        name="place",
    )(nid, *[v for v, _ in mine], *theirs)


def join(y, mine, theirs):
    zs, tn, D = mine.shape

    def kernel(y_ref, mine, theirs, out):
        out[:, y_ref[0]] = mine[...]
        out[:, 1 - y_ref[0]] = theirs[...]

    return pl.pallas_call(
        kernel,
        in_specs=[pl.BlockSpec(memory_space=pltpu.SMEM)] + [VMEM] * 2,
        out_specs=VMEM,
        out_shape=shape((zs, 2, tn, D), BF16),
        compiler_params=PARAMS,
        cost_estimate=cost(2),
        name="join",
    )(y, mine, theirs)


def units_kernel(
    y_ref, n2, n2_other, cot, up, dn, bias, normed, grads, out, sums, act_sc, grad_sc
):
    zs, _, tn, D = cot.shape
    rows = zs * tn
    U = up.shape[1]
    halves = cot[...]
    swap = y_ref[0] == 1
    g = [
        jnp.where(swap, halves[:, 1], halves[:, 0]).reshape(rows, D),
        jnp.where(swap, halves[:, 0], halves[:, 1]).reshape(rows, D),
    ]
    lows = [n2[...].reshape(rows, D), n2_other[...].reshape(rows, D)]
    total = jnp.zeros((1, U), F32)
    for k in range(2):
        value, slope = gelu_parts(mm(lows[k], up[...]) + bias[...])
        act_sc[k] = value.astype(BF16)
        grad = (mm(g[k], dn[...], NT) * slope).astype(BF16)
        grad_sc[k] = grad
        total += jnp.sum(grad.astype(F32), axis=0, keepdims=True)
    row = lax.broadcasted_iota(jnp.int32, (8, U), 0)
    sums[...] = jnp.where(row == 0, total, 0.0)
    wides = out.shape[0]
    size = D // wides
    heads = grads[...].reshape(2 * rows, grads.shape[-1])
    blank = jnp.zeros((size, U - heads.shape[1]), F32)
    for w in range(wides):
        cols = slice(w * size, (w + 1) * size)
        for at, left, right in ((0, g, act_sc), (1, lows, grad_sc)):
            part = mm(left[0][:, cols], right[0], TN) + mm(left[1][:, cols], right[1], TN)
            out[w, at * size : (at + 1) * size, :] = part.astype(BF16)
        part = jnp.concatenate([mm(normed[:, cols], heads, TN), blank], axis=1)
        out[w, 2 * size :, :] = part.astype(BF16)


def unit_grads(half, n2, n2_other, cot, up, dn, bias, normed, grads, wides):
    zs, tn, D = n2.shape
    U = up.shape[1]
    return pl.pallas_call(
        units_kernel,
        in_specs=[pl.BlockSpec(memory_space=pltpu.SMEM)] + [VMEM] * 8,
        out_specs=[VMEM] * 2,
        out_shape=[shape((wides, 3 * (D // wides), U), BF16), shape((8, U), F32)],
        scratch_shapes=[pltpu.VMEM((2, zs * tn, U), BF16)] * 2,
        compiler_params=PARAMS,
        cost_estimate=cost(0),
        name="unit_grads",
    )(half, n2, n2_other, cot, up, dn, bias, normed, grads)


def local(
    tokens,
    scene_ids,
    norm1_gain,
    norm1_shift,
    qkv_weight,
    qv_bias,
    out_weight,
    out_bias,
    norm2_gain,
    norm2_shift,
    up_weight,
    up_bias,
    down_weight,
    down_bias,
    cotangent,
):
    T, D = tokens.shape
    NW = lax.axis_size("wide")
    N = lax.axis_size("narrow")
    C = out_weight.shape[0]
    hh = C // HEAD_DIM
    U = up_weight.shape[1]
    zs = N // 2
    tn = T // N
    wid = lax.axis_index("wide")
    nid = lax.axis_index("narrow")
    core = wid % 2
    ybit = nid % 2
    zgroups = [list(range(0, N, 2)), list(range(1, N, 2))]
    row = lambda v: v.reshape(1, -1)

    def swap(v, axis, bit):
        size = lax.axis_size(axis)
        return lax.ppermute(v, axis, [(i, i ^ bit) for i in range(size)])

    def wide_scatter(v):
        bit = 1
        while bit < NW:
            pairs = v.reshape((v.shape[0] // 2, 2) + v.shape[1:])
            here = (wid // bit) % 2
            send = lax.dynamic_index_in_dim(pairs, 1 - here, 1, keepdims=False)
            keep = lax.dynamic_index_in_dim(pairs, here, 1, keepdims=False)
            got = swap(send, "wide", bit)
            v = (keep.astype(F32) + got.astype(F32)).astype(v.dtype)
            bit *= 2
        return v[0]

    turn = lambda v, by: lax.ppermute(v, "narrow", [(i, (i + by) % N) for i in range(N)])

    def gather_z(v):
        blocks = [(v, 0)]
        up, down = v, v
        for k in range(1, zs // 2 + 1):
            up = turn(up, 2)
            blocks.append((up, -k))
            if 2 * k < zs:
                down = turn(down, -2)
                blocks.append((down, k))
        return blocks

    def gather_rows(v, *beside):
        blocks = gather_z(v)
        theirs = [swap(block, "narrow", 1) for block, _ in blocks]
        out, total = place(nid.reshape(1), blocks, theirs, v.shape[0] - tn)
        beside = lax.optimization_barrier((*beside, *theirs[1:-1]))[: len(beside)]
        return out.reshape(T, D), total, *beside

    def after(v, *done):
        return lax.optimization_barrier((v,) + done)[0]

    half_at = ybit.reshape(1)
    pack = pack_half(core.reshape(1), up_weight, down_weight, row(up_bias))
    near = swap(pack, "narrow", 1)
    tokens = after(tokens, pack)
    normed, q, mine = project(
        tokens, row(norm1_gain), row(norm1_shift), qkv_weight,
        row(qv_bias), scene_ids.reshape(T // 128, 128), hh,
    )

    kv = {0: mine}
    bit = 2
    while bit < NW:
        for k in list(kv):
            kv[k + bit] = swap(kv[k], "wide", bit)
        bit *= 2
    kv[1] = swap(mine, "wide", 1)

    w_near = swap(
        lax.dynamic_slice_in_dim(after(qkv_weight, mine), core * (D // 2), D // 2, 0), "narrow", 1
    )

    wo_cols = lax.dynamic_slice_in_dim(after(out_weight, mine), wid * (D // NW), D // NW, 1)
    wos = {
        0: lax.all_to_all(
            jnp.broadcast_to(wo_cols[None], (N, C, D // NW)),
            "narrow", split_axis=0, concat_axis=0, tiled=True,
        )
    }
    sums = None
    for k in range(0, NW, 2):
        if k:
            kv[k + 1] = swap(after(kv[k], sums), "wide", 1)
        sums = attend(hh, N, mine, q, [kv[k], kv[k + 1]], sums, k + 2 == NW)
        if k + 2 < NW:
            sums = sums[0]
    sends, mix32, qf = sums

    mix_half = lax.all_to_all(
        after(sends, wos[0], near), "narrow", split_axis=0, concat_axis=0, tiled=True
    )
    wos[0] = after(wos[0], sends)
    bit = 2
    while bit < NW:
        for k in list(wos):
            wos[k + bit] = swap(wos[k], "wide", bit)
        bit *= 2
    for k in list(wos):
        wos[k + 1] = swap(wos[k], "wide", 1)
    far = swap(after(near, sends), "wide", 1)
    w_far = swap(after(w_near, sends), "wide", 1)
    tok4 = tokens.reshape(zs, 2, tn, D)
    cot4 = after(cotangent, sends).reshape(zs, 2, tn, D)
    ga = before_middle(cot4, down_weight, far, near, half_at)
    direct = mm(cot4.reshape(T, D), out_weight, NT)
    mix_half = after(mix_half, direct, ga, w_near)
    a_parts, active, back, normed2, residual, sums2 = middle(
        mix_half, tok4, ga, [wos[k] for k in range(NW)], up_weight, row(up_bias), far, near,
        row(out_bias), row(norm2_gain), row(norm2_shift), half_at, wid.reshape(1),
    )
    arrived = lax.all_to_all(a_parts, "narrow", split_axis=0, concat_axis=0, tiled=True)
    z_at = (nid // 2).reshape(1)
    grad_out, ffs = after_middle(
        active, back, mix_half, cot4, down_weight, far, near, half_at, z_at, NW
    )
    grad_out = wide_scatter(grad_out)
    arrived, ffs = lax.optimization_barrier((arrived, ffs))
    exchange_z = lambda v: lax.all_to_all(
        v, "narrow", split_axis=0, concat_axis=0, tiled=True, axis_index_groups=zgroups
    )
    ffs = exchange_z(ffs)
    normed2_other = swap(after(normed2, arrived), "narrow", 1)
    do, dof = gather_grad(
        hh, arrived.reshape(zs, 2, zs, tn, C), direct.reshape(zs, 2, tn, C), mix32
    )

    dq = None
    come = {k: [] for k in range(0, NW, 2)}
    sent = []
    for k in range(NW - 2, -1, -2):
        dq, other = attend_back(hh, mine, kv[k + 1], q, qf, do, dof, dq, False)
        home = swap(other, "wide", 1)
        if k == 0:
            out_rows = output_rows(z_at, after(ffs, dq, *sent), residual, row(down_bias))
            rows_here = exchange_z(out_rows)
            dq = after(dq, out_rows, normed2_other, grad_out)
        dq, own = attend_back(hh, mine, kv[k], q, qf, do, dof, dq, k == 0)
        parts = [own, home] + come[k]
        if k:
            total = parts[0].astype(F32)
            for part in parts[1:]:
                total += part.astype(F32)
            top = 1 << (k.bit_length() - 1)
            sent = [total.astype(BF16)]
            come[k ^ top].append(swap(sent[0], "wide", top))
    grads, send, grad_sums = collect(hh, half_at, dq, parts, zs)
    other = swap(send, "narrow", 1)
    both, unit_sums = unit_grads(
        half_at, normed2, normed2_other, cot4, up_weight, down_weight, row(up_bias),
        normed, after(grads, send), NW,
    )
    part, back_all = project_back(
        grads, after(other, both, rows_here), qkv_weight, w_near, w_far, tok4, back, row(norm1_gain),
        half_at, core.reshape(1),
    )
    back_all = exchange_z(back_all)
    weights = wide_scatter(after(both, part))

    grad_out = after(grad_out, part).reshape(zs, 2, C, D // NW)
    keep = lax.dynamic_index_in_dim(grad_out, ybit, 1, keepdims=False)
    send = lax.dynamic_index_in_dim(grad_out, 1 - ybit, 1, keepdims=False)
    grad_out = (keep.astype(F32) + swap(send, "narrow", 1).astype(F32)).astype(BF16)
    rows_there = swap(after(rows_here, grad_out), "narrow", 1)
    grad_out_w = 0.0
    for k in range(zs):
        to = lax.dynamic_index_in_dim(grad_out, (nid // 2) ^ k, 0, keepdims=False)
        grad_out_w += (swap(to, "narrow", 2 * k) if k else to).astype(F32)
    vectors = vector_sums(
        hh, NW, part, tok4, sums2, cotangent, unit_sums, grad_sums, half_at, nid.reshape(1)
    )
    vectors = wide_scatter(vectors)
    back_all, vectors = lax.optimization_barrier((back_all, vectors, grad_out_w))[:2]
    token_rows = finish(
        nid.reshape(1), back_all, cotangent, vectors
    )
    grad_tokens, final, rows_there = gather_rows(token_rows, rows_there)
    output = join(half_at, rows_here, rows_there).reshape(T, D)
    size = D // NW
    grad_down_w = weights[:size].astype(F32).T
    grad_up_w = weights[size : 2 * size].astype(F32)
    grad_qkv_w = weights[2 * size :, : 3 * C].astype(F32)
    final = final[:6, : D // NW]
    up_bias_out = vectors[6, : U // NW].reshape(1, -1)
    qv_out = vectors[7, : 2 * C // NW].reshape(1, -1)
    return (
        output,
        grad_tokens,
        final[0],
        final[1],
        grad_qkv_w,
        qv_out,
        grad_out_w,
        final[4],
        final[2],
        final[3],
        grad_up_w,
        up_bias_out,
        grad_down_w,
        final[5],
    )


def solution(mesh):
    in_specs = (
        P("wide", None),
        P("wide"),
        P(),
        P(),
        P(None, "narrow"),
        P("narrow"),
        P("narrow", None),
        P(),
        P(),
        P(),
        P(None, "narrow"),
        P("narrow"),
        P("narrow", None),
        P(),
        P("wide", None),
    )
    out_specs = (
        P("wide", None),
        P("wide", None),
        P("wide"),
        P("wide"),
        P("wide", "narrow"),
        P("narrow", "wide"),
        P("narrow", "wide"),
        P("wide"),
        P("wide"),
        P("wide"),
        P("wide", "narrow"),
        P("narrow", "wide"),
        P("narrow", "wide"),
        P("wide"),
    )
    return jax.shard_map(local, mesh=mesh, in_specs=in_specs, out_specs=out_specs, check_vma=False)
```

```python
import functools

import jax
import jax.numpy as jnp
from jax import lax
from jax.experimental import pallas as pl
from jax.experimental.pallas import tpu as pltpu
from jax.sharding import PartitionSpec as P

HEAD_DIM = 64
EPSILON = 1e-05
BIG = 2.0**100
SAFE = 40.0
ONE = 2
NT = (((1,), (1,)), ((), ()))
NN = (((1,), (0,)), ((), ()))
TN = (((0,), (0,)), ((), ()))
VMEM = pl.BlockSpec(memory_space=pltpu.VMEM)
F32 = jnp.float32
BF16 = jnp.bfloat16


def limit(mib):
    return pltpu.CompilerParams(vmem_limit_bytes=mib * 1024 * 1024)


PARAMS = limit(56)


def cost(us, weight=0.0):
    return pl.CostEstimate(flops=int(us * weight * 1.15e9), bytes_accessed=0, transcendentals=0)


def mm(a, b, dims=NN):
    return lax.dot_general(a, b, dims, preferred_element_type=F32)


def slot(at, size):
    return pl.ds(pl.multiple_of(at, size), size)


def shape(dims, dtype):
    return jax.ShapeDtypeStruct(dims, dtype)


def unit_rows(values):
    centre = jnp.mean(values, axis=-1, keepdims=True)
    centred = values - centre
    spread = jnp.mean(centred * centred, axis=-1, keepdims=True)
    scale = lax.rsqrt(spread + EPSILON)
    return centred * scale, scale


def norm_back(grad, unit, scale):
    first = jnp.mean(grad, axis=-1, keepdims=True)
    second = jnp.mean(grad * unit, axis=-1, keepdims=True)
    return (grad - first - unit * second) * scale


def gelu_parts(v):
    c = 0.7978845608028654
    square = v * v
    t = jnp.tanh(c * (v + 0.044715 * (v * square)))
    value = 0.5 * v * (1.0 + t)
    slope = 0.5 * (1.0 + t) + 0.5 * v * (1.0 - t * t) * (c * (1.0 + 3 * 0.044715 * square))
    return value, slope


def split3(v):
    a = v.astype(BF16)
    rest = v - a.astype(F32)
    b = rest.astype(BF16)
    return a, b, (rest - b.astype(F32)).astype(BF16)


def id_features(ids, start, change):
    n = ids.shape[0]
    row = lax.broadcasted_iota(jnp.int32, (128, 128), 0)
    lane = lax.broadcasted_iota(jnp.int32, (128, 128), 1)
    pick = lambda v: jnp.where(lane == 0, v[0], jnp.where(lane == 1, v[1], v[2]))
    spread = [
        jnp.where(row == lane, jnp.broadcast_to(ids[c : c + 1], (128, 128)), 0.0) for c in range(n)
    ]
    own = jnp.concatenate(spread, axis=0).astype(BF16)
    moved = mm(own, pick((change[0], change[1], 0.0)).astype(BF16))
    return (moved + pick(start)[0:1]).astype(BF16)


def key_features(ids):
    return id_features(ids, (-BIG, 0.0, 1.0), (BIG, -BIG))


def query_features(ids):
    return id_features(ids, (0.0, 1.0, 0.0), (1.0, -1.0))


def project_kernel(hh, T, blk, tok, gain, shift, w, bias, ids, normed, q_out, kvx, most):
    i = pl.program_id(0)
    extra = kvx.shape[0] - hh * T

    @pl.when(i == 0)
    def _():
        most[...] = jnp.zeros_like(most)
        rows = ids[...].astype(F32)
        rows = jnp.concatenate([rows, jnp.zeros((extra - rows.shape[0], 128), F32)], axis=0)
        kvx[hh * T :, :] = rows.astype(BF16)

    unit, _ = unit_rows(tok[...].astype(F32))
    low = (unit * gain[...] + shift[...]).astype(BF16)
    normed[...] = low
    zero = jnp.zeros((1, 64), F32)
    shifts = []
    for h in range(hh):
        shifts += [bias[:, h * 128 : h * 128 + 64], zero, bias[:, h * 128 + 64 : h * 128 + 128]]
    proj = mm(low, w[...]) + jnp.concatenate(shifts, axis=1)
    for h in range(hh):
        part = proj[:, h * 192 : h * 192 + 192]
        q = jnp.concatenate([part[:, :64] * 0.125, jnp.zeros((blk, 64), F32)], axis=1)
        q_out[h] = q.astype(BF16)
        kvx[slot(h * T + i * blk, blk), :] = part[:, 64:].astype(BF16)
    row = lax.broadcasted_iota(jnp.int32, (192 * hh, 128), 0) % 192
    lane = lax.broadcasted_iota(jnp.int32, (192 * hh, 128), 1)
    is_q = (lane // 2 == lax.broadcasted_iota(jnp.int32, (192 * hh, 128), 0) // 192) & (
        lane % 2 == 1
    )
    is_k = (lane // 2 == lax.broadcasted_iota(jnp.int32, (192 * hh, 128), 0) // 192) & (
        lane % 2 == 0
    )
    pick = jnp.where(is_q & (row < 64), 1.0 / 64, 0.0)
    pick = jnp.where(is_k & (row >= 64) & (row < 128), 1.0, pick).astype(BF16)
    lengths = mm((proj * proj).astype(BF16), pick)
    most[0:1] = jnp.maximum(most[0:1], jnp.max(lengths, axis=0, keepdims=True))

    @pl.when(i == T // blk - 1)
    def _():
        row = lax.broadcasted_iota(jnp.int32, (16, 128), 0)
        odd = lax.broadcasted_iota(jnp.int32, (1, 128), 1) % 2 == 1
        tops = jnp.where(row == 0, jnp.where(odd, 0.0, most[0:1]), 0.0)
        tops = jnp.where(row == 1, jnp.where(odd, most[0:1], 0.0), tops)
        kvx[hh * T + extra - 16 :, :] = (tops * 1.05).astype(BF16)


def project(tokens, gain, shift, w, bias, ids, hh):
    T, D = tokens.shape
    blk = min(256, T)
    extra = ids.shape[0] + -ids.shape[0] % 16 + 16
    whole = lambda *dims: pl.BlockSpec(dims, lambda i: (0,) * len(dims))
    return pl.pallas_call(
        functools.partial(project_kernel, hh, T, blk),
        grid=(T // blk,),
        in_specs=[
            pl.BlockSpec((blk, D), lambda i: (i, 0)),
            whole(1, D),
            whole(1, D),
            whole(D, 192 * hh),
            whole(*bias.shape),
            whole(*ids.shape),
        ],
        out_specs=[
            pl.BlockSpec((blk, D), lambda i: (i, 0)),
            pl.BlockSpec((hh, blk, 128), lambda i: (0, i, 0)),
            whole(hh * T + extra, 128),
        ],
        out_shape=[
            shape((T, D), BF16),
            shape((hh, T, 128), BF16),
            shape((hh * T + extra, 128), BF16),
        ],
        scratch_shapes=[pltpu.VMEM((8, 128), F32)],
        compiler_params=PARAMS,
        cost_estimate=cost(7),
        name="project",
    )(tokens, gain, shift, w, bias, ids)


def scene_rows(ref, tail, count):
    return ref[tail : tail + count + -count % 16, :].astype(F32)[:count]


def counts(ids, per, out, at):
    for j in range(ids.shape[0] // per):
        out[at + j] = jnp.sum(ids[j * per : (j + 1) * per])


def meets(a, na, b, nb):
    apart = ((a == 0) & (b == nb)) | ((a == na) & (b == 0))
    return jnp.logical_not(apart)


def attend_kernel(hh, T, nb, bq, bk, first, last, mine, q_ref, *refs):
    kvs = refs[:nb]
    refs = refs[nb:]
    if not first:
        acc_in = refs[0]
        refs = refs[1:]
    if last:
        sends, mix32, feat = refs[:3]
        refs = refs[3:]
    else:
        acc_out = refs[0]
        refs = refs[1:]
    acc_sc, m_sc, v_sc, qf_sc, kf_sc, spans, qspans, tops_sc = refs
    i = pl.program_id(0)
    trows = T // 128
    tail = hh * T
    lane = lax.broadcasted_iota(jnp.int32, (bq, 128), 1)

    @pl.when(i == 0)
    def _():
        ids = scene_rows(mine, tail, trows)
        counts(ids, bq // 128, qspans, 0)
        qf_sc[...] = query_features(ids)
        tops = kvs[0][-16:, :].astype(F32)
        wide = lax.broadcasted_iota(jnp.int32, (T, 128), 1)
        for b in range(nb):
            ids = scene_rows(kvs[b], tail, trows)
            counts(ids, bk // 128, spans, b * (T // bk))
            kf_sc[b] = key_features(ids)
            tops = jnp.maximum(tops, kvs[b][-16:, :].astype(F32))
            for h in range(hh):
                kv = kvs[b][h * T : (h + 1) * T, :]
                v_sc[b, h] = jnp.where(wide < 64, jnp.ones((), BF16), kv)
        tops_sc[0] = jnp.max(mine[-16:, :].astype(F32)[1:2]) * jnp.max(tops[0:1])

    calm = tops_sc[0] < SAFE * SAFE
    if first:
        acc_sc[...] = jnp.zeros_like(acc_sc)
    else:
        acc_sc[...] = acc_in[...]
        shift = acc_in[:, :, :1]
        calm = calm & (jnp.max(jnp.abs(shift)) == 0.0)
    m_sc[...] = jnp.zeros_like(m_sc)
    qr = slot(i * bq, bq)

    def block(b, h, j):
        rows = slot(h * T + j * bk, bk)
        return jnp.concatenate([kvs[b][rows, :], kf_sc[b, slot(j * bk, bk), :]], axis=1)

    @pl.when(jnp.logical_not(calm))
    def _():
        m_sc[...] = jnp.full(m_sc.shape, -2.0 * BIG, F32)

        def step(j, carry):
            for b in range(nb):
                for h in range(hh):
                    q = jnp.concatenate([q_ref[h], qf_sc[qr, :]], axis=1)
                    s = mm(q, block(b, h, j), NT)
                    m = jnp.max(s, axis=1, keepdims=True).astype(BF16).astype(F32)
                    m_sc[h] = jnp.maximum(m_sc[h], m)
            return carry

        lax.fori_loop(0, T // bk, step, 0)
        if not first:
            for h in range(hh):
                old = jnp.broadcast_to(acc_in[h, :, :1], (bq, 128))
                new = jnp.maximum(m_sc[h], old)
                acc_sc[h] = acc_sc[h] * jnp.exp(old - new)
                m_sc[h] = new

    qs = []
    for h in range(hh):
        feature = jnp.where(lane == ONE, (-m_sc[h]).astype(BF16), qf_sc[qr, :])
        qs.append(jnp.concatenate([q_ref[h], feature], axis=1))
    for b in range(nb):
        for j in range(T // bk):

            @pl.when(meets(qspans[i], bq, spans[b * (T // bk) + j], bk))
            def _():
                for h in range(hh):
                    p = jnp.exp(mm(qs[h], block(b, h, j), NT)).astype(BF16)
                    acc_sc[h] += mm(p, v_sc[b, h, j * bk : (j + 1) * bk, :])

    if not last:
        for h in range(hh):
            acc_out[h] = jnp.where(lane == 0, m_sc[h], acc_sc[h])
        return
    parts = []
    for h in range(hh):
        acc = acc_sc[h]
        total = acc[:, 1:2]
        mix = acc / total
        mix32[h] = mix
        parts.append(mix[:, 64:])
        a, b, c = split3(-(m_sc[h] + jnp.log(total)))
        feat[h] = jnp.where(
            lane == 2, a, jnp.where(lane == 3, b, jnp.where(lane == 4, c, qf_sc[qr, :]))
        )
    whole = jnp.concatenate(parts, axis=1) if hh > 1 else parts[0]
    count, zb, tn, c = sends.shape
    halves = whole.astype(BF16).reshape(zb, 2, tn, c)
    for n in range(count):
        sends[n] = halves[:, n % 2]


def attend(hh, devices, mine, q, kvs, before, last):
    T = q.shape[1]
    nb = len(kvs)
    bq = min(512, T)
    bk = min(1024, T)
    first = before is None
    zs, tn = devices // 2, T // devices
    rows = pl.BlockSpec((hh, bq, 128), lambda i: (0, i, 0))
    whole = lambda a: pl.BlockSpec(a.shape, lambda i: (0,) * a.ndim)
    if last:
        outs = [
            shape((devices, zs, tn, hh * 64), BF16),
            shape((hh, T, 128), F32),
            shape((hh, T, 128), BF16),
        ]
        specs = [
            pl.BlockSpec((devices, zs * bq // T, tn, hh * 64), lambda i: (0, i, 0, 0)),
            rows,
            rows,
        ]
    else:
        outs = [shape((hh, T, 128), F32)]
        specs = [rows]
    return pl.pallas_call(
        functools.partial(attend_kernel, hh, T, nb, bq, bk, first, last),
        grid=(T // bq,),
        in_specs=[whole(mine), rows] + [whole(kv) for kv in kvs] + ([] if first else [rows]),
        out_specs=specs,
        out_shape=outs,
        scratch_shapes=[
            pltpu.VMEM((hh, bq, 128), F32),
            pltpu.VMEM((hh, bq, 128), F32),
            pltpu.VMEM((nb, hh, T, 128), BF16),
            pltpu.VMEM((T, 128), BF16),
            pltpu.VMEM((nb, T, 128), BF16),
            pltpu.SMEM((nb * (T // bk),), F32),
            pltpu.SMEM((T // bq,), F32),
            pltpu.SMEM((1,), F32),
        ],
        compiler_params=limit(24),
        cost_estimate=cost(8),
        name="attend",
    )(mine, q, *kvs, *(() if first else (before,)))


def pack_kernel(c_ref, up, dn, bias, out):
    half = dn.shape[0]
    D = dn.shape[1]
    for a in range(D // half):
        out[:half, a * half : (a + 1) * half] = up[a * half : (a + 1) * half, :]
    out[half : 2 * half, :] = dn[...]
    a, b, c = split3(bias[...])
    zero = jnp.zeros((1, D - 3 * half), F32)
    parts = [v.astype(F32) for v in (a, b, c)] + ([zero] if D > 3 * half else [])
    row = jnp.concatenate(parts, axis=1)
    out[2 * half :, :] = jnp.broadcast_to(row, (16, D)).astype(BF16)


def pack_half(core, up, dn, bias):
    D, U = up.shape
    half = U // 2
    return pl.pallas_call(
        pack_kernel,
        grid_spec=pltpu.PrefetchScalarGridSpec(
            num_scalar_prefetch=1,
            grid=(1,),
            in_specs=[
                pl.BlockSpec((D, half), lambda i, c: (0, c[0])),
                pl.BlockSpec((half, D), lambda i, c: (c[0], 0)),
                pl.BlockSpec((1, half), lambda i, c: (0, c[0])),
            ],
            out_specs=pl.BlockSpec((2 * half + 16, D), lambda i, c: (0, 0)),
        ),
        out_shape=shape((2 * half + 16, D), BF16),
        compiler_params=PARAMS,
        cost_estimate=cost(3),
        name="pack_half",
    )(core, up, dn, bias)


def pieces(own, far, near, half, units):
    up, dn, bias = own
    ahead = lambda v: mm(v, up[...])
    back = lambda v: mm(v, up[...], NT)
    yield slice(0, units), ahead, back, dn, bias
    for at, pack in enumerate((far, near)):
        D = pack.shape[1]
        tail = pack[2 * half :, :].astype(F32)
        bias = tail[0:1, :half] + tail[0:1, half : 2 * half] + tail[0:1, 2 * half : 3 * half]
        spans = [slice(a, a + half) for a in range(0, D, half)]

        def ahead(v, pack=pack):
            total = mm(v[:, spans[0]], pack[:half, spans[0]])
            for span in spans[1:]:
                total += mm(v[:, span], pack[:half, span])
            return total

        def back(v, pack=pack):
            return jnp.concatenate([mm(v, pack[:half, span], NT) for span in spans], axis=1)

        yield slice(units + at * half, units + (at + 1) * half), ahead, back, _Rows(
            pack, half, 2 * half
        ), bias


class _Rows:
    def __init__(self, ref, start, stop):
        self.ref, self.start, self.stop = ref, start, stop

    def __getitem__(self, at):
        return self.ref[self.start : self.stop, :]


def before_kernel(units, cot, dn_own, far, near, out):
    rows = cot.shape[0] * cot.shape[1]
    g = cot[...].reshape(rows, cot.shape[2])
    for cols, _, _, dn, _ in pieces((None, dn_own, None), far, near, units // 2, units):
        out[:, cols] = mm(g, dn[...], NT).astype(BF16)


def before_middle(cot, dn_own, far, near, half):
    zs, _, tn, D = cot.shape
    U = dn_own.shape[0]
    const = lambda a: pl.BlockSpec(a.shape, lambda i, y: (0,) * a.ndim)

    def kernel(y_ref, *refs):
        before_kernel(U, *refs)

    return pl.pallas_call(
        kernel,
        grid_spec=pltpu.PrefetchScalarGridSpec(
            num_scalar_prefetch=1,
            grid=(1,),
            in_specs=[pl.BlockSpec((zs, None, tn, D), lambda i, y: (0, y[0], 0, 0))]
            + [const(a) for a in (dn_own, far, near)],
            out_specs=pl.BlockSpec((zs * tn, 2 * U), lambda i, y: (0, 0)),
        ),
        out_shape=shape((zs * tn, 2 * U), BF16),
        compiler_params=PARAMS,
        cost_estimate=cost(3, 1.0),
        name="before_middle",
    )(half, cot, dn_own, far, near)


def middle_kernel(
    units, wid, count, mix, tok, ga, *refs,
):
    wos = refs[:count]
    middle_rest(units, wid, wos, mix, tok, ga, *refs[count:])


def middle_rest(
    units, wid, wos, mix, tok, ga, up_own, b_own, far, near, bo, g2, s2,
    a_out, active, back_out, normed2, res, sums, wo_sc,
):
    i = pl.program_id(0)

    @pl.when(i == 0)
    def _():
        sums[...] = jnp.zeros_like(sums)
        for k, part in enumerate(wos):
            wo_sc[wid ^ k] = part[...].reshape(wo_sc.shape[1:])

    wo = jnp.concatenate([wo_sc[k] for k in range(len(wos))], axis=1)
    n = mix.shape[0]
    D = tok.shape[-1]
    rows = tok.shape[0] * tok.shape[1]
    mixed = jnp.concatenate([mix[s].reshape(rows, mix.shape[-1]) for s in range(n)], axis=1)
    x = tok[...].reshape(rows, D).astype(F32)
    residual = x + mm(mixed, wo) + bo[...]
    unit, scale = unit_rows(residual)
    low = (unit * g2[...] + s2[...]).astype(BF16)
    res[...] = residual.reshape(res.shape)
    normed2[...] = low.reshape(normed2.shape)
    gn = jnp.zeros((rows, D), F32)
    for cols, ahead, back, _, bias in pieces(
        (up_own, None, b_own[...]), far, near, units // 2, units
    ):
        value, slope = gelu_parts(ahead(low) + bias)
        active[:, cols] = value.astype(BF16)
        gn += back((ga[:, cols].astype(F32) * slope).astype(BF16))
    back_low = norm_back(gn * g2[...], unit, scale).astype(BF16)
    back_out[...] = back_low.reshape(back_out.shape)
    a = mm(back_low, wo, NT).astype(BF16)
    c = a_out.shape[-1]
    for s in range(n):
        a_out[s] = a[:, s * c : (s + 1) * c].reshape(a_out.shape[1:])

    sums[0:1] += jnp.sum(gn * unit, axis=0, keepdims=True)
    sums[1:2] += jnp.sum(gn, axis=0, keepdims=True)
    sums[2:3] += jnp.sum(back_low.astype(F32), axis=0, keepdims=True)


def middle(mix, tok, ga, wos, up_own, b_own, far, near, bo, g2, s2, half, wid):
    n, zs, tn, c = mix.shape
    D = up_own.shape[0]
    U = up_own.shape[1]
    zb = zs
    const = lambda a: pl.BlockSpec(a.shape, lambda i, y, e: (0,) * a.ndim)
    rows = pl.BlockSpec((zb, tn, D), lambda i, y, e: (i, 0, 0))
    flat = pl.BlockSpec((zb * tn, 2 * U), lambda i, y, e: (i, 0))
    heads = pl.BlockSpec((n, zb, tn, c), lambda i, y, e: (0, i, 0, 0))

    def kernel(y_ref, e_ref, *refs):
        middle_kernel(U, e_ref[0], len(wos), *refs)

    return pl.pallas_call(
        kernel,
        grid_spec=pltpu.PrefetchScalarGridSpec(
            num_scalar_prefetch=2,
            grid=(zs // zb,),
            in_specs=[
                heads,
                pl.BlockSpec((zb, None, tn, D), lambda i, y, e: (i, y[0], 0, 0)),
                flat,
            ]
            + [const(a) for a in (*wos, up_own, b_own, far, near, bo, g2, s2)],
            out_specs=[heads, flat, rows, rows, rows, pl.BlockSpec((8, D), lambda i, y, e: (0, 0))],
            scratch_shapes=[pltpu.VMEM((len(wos), n * c, D // len(wos)), BF16)],
        ),
        out_shape=[
            shape((n, zs, tn, c), BF16),
            shape((zs * tn, 2 * U), BF16),
            shape((zs, tn, D), BF16),
            shape((zs, tn, D), BF16),
            shape((zs, tn, D), F32),
            shape((8, D), F32),
        ],
        compiler_params=PARAMS,
        cost_estimate=cost(12),
        name="middle",
    )(half, wid, mix, tok, ga, *wos, up_own, b_own, far, near, bo, g2, s2)


def after_kernel(units, y_ref, z_ref, active, back, mix, cot, dn_own, far, near, go, out):
    rows = active.shape[0]
    zs, tn, D = back.shape
    ff = jnp.zeros((rows, D), F32)
    for cols, _, _, dn, _ in pieces((None, dn_own, None), far, near, units // 2, units):
        ff += mm(active[:, cols], dn[...])
    out[...] = ff.astype(BF16).reshape(zs, tn, D)
    r = back[...].reshape(rows, D)
    g = jnp.where(z_ref[0] == 0, cot[...].reshape(rows, D), jnp.zeros((), BF16))
    c = mix.shape[-1]
    size = go.shape[2]
    for s in range(mix.shape[0]):
        heads = mix[s].reshape(rows, c)
        total = (mm(heads, r, TN) + mm(heads, g, TN)).astype(BF16)
        for k in range(go.shape[0]):
            go[k, s * c : (s + 1) * c, :] = total[:, k * size : (k + 1) * size]


def after_middle(active, back, mix, cot, dn_own, far, near, half, z, wides):
    n, zs, tn, c = mix.shape
    U, D = dn_own.shape
    const = lambda a: pl.BlockSpec(a.shape, lambda i, y, z: (0,) * a.ndim)
    return pl.pallas_call(
        functools.partial(after_kernel, U),
        grid_spec=pltpu.PrefetchScalarGridSpec(
            num_scalar_prefetch=2,
            grid=(1,),
            in_specs=[
                const(active),
                const(back),
                const(mix),
                pl.BlockSpec((zs, None, tn, D), lambda i, y, z: (0, y[0], 0, 0)),
            ]
            + [const(a) for a in (dn_own, far, near)],
            out_specs=[pl.BlockSpec((wides, n * c, D // wides), lambda i, y, z: (0, 0, 0))]
            + [pl.BlockSpec((zs, tn, D), lambda i, y, z: (0, 0, 0))],
        ),
        out_shape=[shape((wides, n * c, D // wides), BF16), shape((zs, tn, D), BF16)],
        compiler_params=PARAMS,
        cost_estimate=cost(6, 1.0),
        name="after_middle",
    )(half, z, active, back, mix, cot, dn_own, far, near)


def rows_kernel(z_ref, *refs):
    res, bias, out = refs[-3:]
    total = res[...] + bias[...]
    parts = refs[0]
    for k in range(parts.shape[0]):
        total += parts[k].astype(F32)
    for k in range(out.shape[0]):
        out[k] = total.astype(BF16)


def output_rows(z, parts, residual, bias):
    zs, tn, D = residual.shape
    same = lambda a: pl.BlockSpec(a.shape, lambda i, z: (0,) * a.ndim)
    return pl.pallas_call(
        rows_kernel,
        grid_spec=pltpu.PrefetchScalarGridSpec(
            num_scalar_prefetch=1,
            grid=(1,),
            in_specs=[
                same(parts),
                pl.BlockSpec((None, tn, D), lambda i, z: (z[0], 0, 0)),
                same(bias),
            ],
            out_specs=pl.BlockSpec((zs, tn, D), lambda i, z: (0, 0, 0)),
        ),
        out_shape=shape((zs, tn, D), BF16),
        compiler_params=limit(40),
        cost_estimate=cost(2),
        name="output_rows",
    )(z, parts, residual, bias)


class _Row:
    def __init__(self, ref):
        self.ref = ref
        self.shape = (ref.shape[0], 1, ref.shape[1], ref.shape[2])

    def __getitem__(self, at):
        return self.ref[at]


def gather_kernel(hh, parts, direct, mix32, do, dof):
    rows = direct.shape[0] * direct.shape[2]
    c = direct.shape[-1]
    total = direct[...].reshape(rows, c)
    for s in range(parts.shape[0]):
        total += parts[s].reshape(rows, c).astype(F32)
    low = total.astype(BF16)
    lane = lax.broadcasted_iota(jnp.int32, (rows, 128), 1)
    for h in range(hh):
        grad = jnp.concatenate(
            [jnp.zeros((rows, 64), BF16), low[:, h * 64 : h * 64 + 64]], axis=1
        )
        mix = mix32[h].reshape(rows, 128)
        delta = jnp.sum(grad.astype(F32) * mix, axis=1, keepdims=True)
        a, b, e = split3(jnp.broadcast_to(-delta, (rows, 128)))
        zero = BF16(0)
        feature = jnp.where(lane == 2, a, jnp.where(lane == 3, b, jnp.where(lane == 4, e, zero)))
        do[h] = grad.reshape(do.shape[1:])
        dof[h] = feature.reshape(dof.shape[1:])


def gather_grad(hh, parts, direct, mix32):
    zs, _, _, tn, c = parts.shape
    T = 2 * zs * tn
    m4 = mix32.reshape(hh, zs, 2, tn, 128)
    wide = pl.BlockSpec((hh, zs, None, tn, 128), lambda y: (0, 0, y, 0, 0))

    def kernel(parts, direct, mix32, do, dof):
        gather_kernel(hh, parts, _Row(direct), mix32, do, dof)

    do, dof = pl.pallas_call(
        kernel,
        grid=(2,),
        in_specs=[
            pl.BlockSpec((zs, None, zs, tn, c), lambda y: (0, y, 0, 0, 0)),
            pl.BlockSpec((zs, None, tn, c), lambda y: (0, y, 0, 0)),
            wide,
        ],
        out_specs=[wide, wide],
        out_shape=[shape((hh, zs, 2, tn, 128), BF16)] * 2,
        compiler_params=limit(40),
        cost_estimate=cost(3),
        name="gather_grad",
    )(parts, direct, m4)
    return do.reshape(hh, T, 128), dof.reshape(hh, T, 128)


def back_kernel(hh, T, bq, bk, first, last, mine, kv, q, qf, do, dof, *refs):
    if first:
        dq_out, dkv, dkv_sc, dq_sc, kf_sc, spans, qspans = refs
        dq_sc[...] = jnp.zeros_like(dq_sc)
    else:
        dq_in, dq_out, dkv, dkv_sc, dq_sc, kf_sc, spans, qspans = refs
        dq_sc[...] = dq_in[...]
    i = pl.program_id(0)
    trows = T // 128
    tail = hh * T

    @pl.when(i == 0)
    def _():
        dkv_sc[...] = jnp.zeros_like(dkv_sc)
        counts(scene_rows(mine, tail, trows), bq // 128, qspans, 0)
        ids = scene_rows(kv, tail, trows)
        counts(ids, bk // 128, spans, 0)
        kf_sc[...] = key_features(ids)

    for j in range(T // bk):

        @pl.when(meets(qspans[i], bq, spans[j], bk))
        def _():
            keys_at = slice(j * bk, (j + 1) * bk)
            kf = kf_sc[keys_at, :]
            for h in range(hh):
                keys = kv[h * T + j * bk : h * T + (j + 1) * bk, :]
                ka = jnp.concatenate([keys, kf], axis=1)
                p = jnp.exp(mm(ka, jnp.concatenate([q[h], qf[h]], axis=1), NT))
                dp = mm(ka, jnp.concatenate([do[h], dof[h]], axis=1), NT)
                ds = (p * dp).astype(BF16)
                dkv_sc[h, keys_at, :] += mm(ds, q[h]) + mm(p.astype(BF16), do[h])
                dq_sc[h] += mm(ds, keys, TN)

    if last:
        parts = [dq_sc[h][:, :64] * 0.125 for h in range(hh)]
        whole = jnp.concatenate(parts, axis=1) if hh > 1 else parts[0]
        dq_out[...] = whole.astype(BF16)
    else:
        dq_out[...] = dq_sc[...]

    @pl.when(i == T // bq - 1)
    def _():
        for h in range(hh):
            dkv[h * T : (h + 1) * T, :] = dkv_sc[h].astype(BF16)


def attend_back(hh, mine, kv, q, qf, do, dof, dq, last):
    T = q.shape[1]
    bq = min(512, T)
    bk = min(1024, T)
    first = dq is None
    rows = pl.BlockSpec((hh, bq, 128), lambda i: (0, i, 0))
    whole = lambda a: pl.BlockSpec(a.shape, lambda i: (0,) * a.ndim)
    if last:
        sums, sums_spec = shape((T, hh * 64), BF16), pl.BlockSpec((bq, hh * 64), lambda i: (i, 0))
    else:
        sums, sums_spec = shape((hh, T, 128), F32), rows
    return pl.pallas_call(
        functools.partial(back_kernel, hh, T, bq, bk, first, last),
        grid=(T // bq,),
        in_specs=[whole(mine), whole(kv)] + [rows] * (4 if first else 5),
        out_specs=[sums_spec, pl.BlockSpec((hh * T, 128), lambda i: (0, 0))],
        out_shape=[sums, shape((hh * T, 128), BF16)],
        scratch_shapes=[
            pltpu.VMEM((hh, T, 128), F32),
            pltpu.VMEM((hh, bq, 128), F32),
            pltpu.VMEM((T, 128), BF16),
            pltpu.SMEM((T // bk,), F32),
            pltpu.SMEM((T // bq,), F32),
        ],
        compiler_params=limit(40),
        cost_estimate=cost(9, 1.0),
        name="attend_back",
    )(mine, kv, q, qf, do, dof, *(() if first else (dq,)))


def collect_kernel(hh, y_ref, gq, *refs):
    parts = refs[:-3]
    grads, send, sums = refs[-3:]
    zs, _, tn, width = grads.shape
    T = 2 * zs * tn
    cols = []
    for h in range(hh):
        total = parts[0][h * T : (h + 1) * T, :].astype(F32)
        for part in parts[1:]:
            total += part[h * T : (h + 1) * T, :].astype(F32)
        low = total.astype(BF16).astype(F32)
        cols += [gq[:, h * 64 : (h + 1) * 64].astype(F32), low]
    whole = jnp.concatenate(cols, axis=1)
    row = lax.broadcasted_iota(jnp.int32, (8, width), 0)
    sums[...] = jnp.where(row == 0, jnp.sum(whole, axis=0, keepdims=True), 0.0)
    halves = whole.astype(BF16).reshape(zs, 2, tn, width)
    grads[...] = halves
    send[...] = jnp.where(y_ref[0] == 0, halves[:, 1], halves[:, 0])


def collect(hh, half, gq, parts, zs):
    T = gq.shape[0]
    tn = T // zs // 2
    width = 192 * hh
    return pl.pallas_call(
        functools.partial(collect_kernel, hh),
        in_specs=[pl.BlockSpec(memory_space=pltpu.SMEM)] + [VMEM] * (1 + len(parts)),
        out_specs=[VMEM] * 3,
        out_shape=[
            shape((zs, 2, tn, width), BF16),
            shape((zs, tn, width), BF16),
            shape((8, width), F32),
        ],
        compiler_params=limit(40),
        cost_estimate=cost(3),
        name="collect",
    )(half, gq, *parts)


def project_back(grads, other, w, w_near, w_far, tok, back, gain, half, core):
    zs, _, tn, width = grads.shape
    D = w.shape[0]
    rows = zs * tn

    def kernel(
        y_ref, c_ref, own, other, w, w_near, w_far, tok, back, gain, grad_out, out, w_sc
    ):
        w_sc[c_ref[0]] = w_near[...]
        w_sc[1 - c_ref[0]] = w_far[...]
        unit, scale = unit_rows(tok[...].reshape(rows, D).astype(F32))
        grad = mm(own[...].reshape(rows, width), w[...], NT)
        grad += mm(other[...].reshape(rows, width), w_sc[...].reshape(D, width), NT)
        grad_out[...] = grad.astype(BF16).reshape(grad_out.shape)
        total = back[...].reshape(rows, D).astype(F32) + norm_back(grad * gain[...], unit, scale)
        out[...] = total.astype(BF16).reshape(out.shape)

    const = lambda a: pl.BlockSpec(a.shape, lambda i, y, c: (0,) * a.ndim)
    own = lambda n: pl.BlockSpec((zs, None, tn, n), lambda i, y, c: (0, y[0], 0, 0))
    all_rows = pl.BlockSpec((zs, tn, D), lambda i, y, c: (0, 0, 0))
    return pl.pallas_call(
        kernel,
        grid_spec=pltpu.PrefetchScalarGridSpec(
            num_scalar_prefetch=2,
            grid=(1,),
            in_specs=[own(width), const(other), const(w), const(w_near), const(w_far), own(D)]
            + [const(back), const(gain)],
            out_specs=[all_rows, all_rows],
            scratch_shapes=[pltpu.VMEM((2, D // 2, width), BF16)],
        ),
        out_shape=[shape((zs, tn, D), BF16)] * 2,
        compiler_params=PARAMS,
        cost_estimate=cost(3, 1.0),
        name="project_back",
    )(half, core, grads, other, w, w_near, w_far, tok, back, gain)


def vector_sums(hh, wides, part, tok, sums2, cot, unit_sums, grad_sums, half, at):
    zs, tn, D = part.shape
    size = D // wides

    def kernel(y_ref, n_ref, part, tok, sums2, cot, unit_sums, grad_sums, out, sc):
        i = pl.program_id(0)
        unit, _ = unit_rows(tok[...].astype(F32))
        grad = part[...].astype(F32)

        @pl.when(i == 0)
        def _():
            sc[...] = jnp.zeros_like(sc)

        sc[0:1] += jnp.sum(grad * unit, axis=0, keepdims=True)
        sc[1:2] += jnp.sum(grad, axis=0, keepdims=True)

        @pl.when(i == zs - 1)
        def _():
            g = jnp.sum(cot[...].astype(F32), axis=0, keepdims=True)
            sc[2:4] = sums2[0:2]
            sc[4:5] = sums2[2:3] + g
            sc[5:6] = g
            pairs = []
            for h in range(hh):
                first = h * 192
                pairs += [grad_sums[0:1, first : first + 64], grad_sums[0:1, first + 128 : first + 192]]
            heads = jnp.concatenate(pairs, axis=1)
            for k in range(wides):
                out[k] = sc[:, k * size : (k + 1) * size]
                for row, v in ((6, unit_sums[0:1]), (7, heads)):
                    n = v.shape[1] // wides
                    mine = v[:, k * n : (k + 1) * n]
                    if n < size:
                        mine = jnp.concatenate([mine, jnp.zeros((1, size - n), F32)], axis=1)
                    out[k, row : row + 1] = mine

    whole = lambda a: pl.BlockSpec(a.shape, lambda i, y, n: (0,) * a.ndim)
    return pl.pallas_call(
        kernel,
        grid_spec=pltpu.PrefetchScalarGridSpec(
            num_scalar_prefetch=2,
            grid=(zs,),
            in_specs=[
                pl.BlockSpec((None, tn, D), lambda i, y, n: (i, 0, 0)),
                pl.BlockSpec((None, None, tn, D), lambda i, y, n: (i, y[0], 0, 0)),
                whole(sums2),
                pl.BlockSpec((tn, D), lambda i, y, n: (n[0], 0)),
                whole(unit_sums),
                whole(grad_sums),
            ],
            out_specs=pl.BlockSpec((wides, 8, size), lambda i, y, n: (0, 0, 0)),
            scratch_shapes=[pltpu.VMEM((8, D), F32)],
        ),
        out_shape=shape((wides, 8, size), F32),
        compiler_params=PARAMS,
        cost_estimate=cost(3, 1.0),
        name="vector_sums",
    )(half, at, part, tok, sums2, cot, unit_sums, grad_sums)


def finish_kernel(at, *refs):
    cot, vec, out = refs[-3:]
    total = cot[...].astype(F32)
    for k in range(refs[0].shape[0]):
        total += refs[0][k].astype(F32)
    tn, D = total.shape
    out[:tn, :] = total.astype(BF16)
    rows = jnp.concatenate([vec[...], jnp.zeros_like(vec)], axis=0).astype(BF16)
    out[tn:, :] = jnp.concatenate([rows, jnp.zeros((16, D - rows.shape[1]), BF16)], axis=1)


def finish(at, parts, cot, vec):
    zs, tn, D = parts.shape
    return pl.pallas_call(
        finish_kernel,
        grid_spec=pltpu.PrefetchScalarGridSpec(
            num_scalar_prefetch=1,
            grid=(1,),
            in_specs=[
                pl.BlockSpec((zs, tn, D), lambda i, n: (0, 0, 0)),
                pl.BlockSpec((tn, D), lambda i, n: (n[0], 0)),
                pl.BlockSpec(vec.shape, lambda i, n: (0, 0)),
            ],
            out_specs=pl.BlockSpec((tn + 16, D), lambda i, n: (0, 0)),
        ),
        out_shape=shape((tn + 16, D), BF16),
        compiler_params=PARAMS,
        cost_estimate=cost(2),
        name="finish",
    )(at, parts, cot, vec)


def place(nid, mine, theirs, tail):
    moves = [move for _, move in mine]
    rows, D = theirs[0].shape
    tn = rows - tail
    zs = len(moves)

    def kernel(n_ref, *refs):
        out, total = refs[-2:]
        z, y = n_ref[0] // 2, n_ref[0] % 2
        total[...] = jnp.zeros_like(total)
        for k, move in enumerate(moves):
            to = lax.rem(z + move + zs, zs)
            out[to, y] = refs[k][:tn, :]
            out[to, 1 - y] = refs[zs + k][:tn, :]
            total[...] += refs[k][tn:, :].astype(F32) + refs[zs + k][tn:, :].astype(F32)

    return pl.pallas_call(
        kernel,
        in_specs=[pl.BlockSpec(memory_space=pltpu.SMEM)] + [VMEM] * (2 * zs),
        out_specs=[VMEM] * 2,
        out_shape=[shape((zs, 2, tn, D), BF16), shape((tail, D), F32)],
        compiler_params=PARAMS,
        cost_estimate=cost(2),
        name="place",
    )(nid, *[v for v, _ in mine], *theirs)


def join(y, mine, theirs):
    zs, tn, D = mine.shape

    def kernel(y_ref, mine, theirs, out):
        out[:, y_ref[0]] = mine[...]
        out[:, 1 - y_ref[0]] = theirs[...]

    return pl.pallas_call(
        kernel,
        in_specs=[pl.BlockSpec(memory_space=pltpu.SMEM)] + [VMEM] * 2,
        out_specs=VMEM,
        out_shape=shape((zs, 2, tn, D), BF16),
        compiler_params=PARAMS,
        cost_estimate=cost(2),
        name="join",
    )(y, mine, theirs)


def units_kernel(
    y_ref, n2, n2_other, cot, up, dn, bias, normed, grads, out, sums, act_sc, grad_sc
):
    zs, _, tn, D = cot.shape
    rows = zs * tn
    U = up.shape[1]
    halves = cot[...]
    swap = y_ref[0] == 1
    g = [
        jnp.where(swap, halves[:, 1], halves[:, 0]).reshape(rows, D),
        jnp.where(swap, halves[:, 0], halves[:, 1]).reshape(rows, D),
    ]
    lows = [n2[...].reshape(rows, D), n2_other[...].reshape(rows, D)]
    total = jnp.zeros((1, U), F32)
    for k in range(2):
        value, slope = gelu_parts(mm(lows[k], up[...]) + bias[...])
        act_sc[k] = value.astype(BF16)
        grad = (mm(g[k], dn[...], NT) * slope).astype(BF16)
        grad_sc[k] = grad
        total += jnp.sum(grad.astype(F32), axis=0, keepdims=True)
    row = lax.broadcasted_iota(jnp.int32, (8, U), 0)
    sums[...] = jnp.where(row == 0, total, 0.0)
    wides = out.shape[0]
    size = D // wides
    heads = grads[...].reshape(2 * rows, grads.shape[-1])
    blank = jnp.zeros((size, U - heads.shape[1]), F32)
    for w in range(wides):
        cols = slice(w * size, (w + 1) * size)
        for at, left, right in ((0, g, act_sc), (1, lows, grad_sc)):
            part = mm(left[0][:, cols], right[0], TN) + mm(left[1][:, cols], right[1], TN)
            out[w, at * size : (at + 1) * size, :] = part.astype(BF16)
        part = jnp.concatenate([mm(normed[:, cols], heads, TN), blank], axis=1)
        out[w, 2 * size :, :] = part.astype(BF16)


def unit_grads(half, n2, n2_other, cot, up, dn, bias, normed, grads, wides):
    zs, tn, D = n2.shape
    U = up.shape[1]
    return pl.pallas_call(
        units_kernel,
        in_specs=[pl.BlockSpec(memory_space=pltpu.SMEM)] + [VMEM] * 8,
        out_specs=[VMEM] * 2,
        out_shape=[shape((wides, 3 * (D // wides), U), BF16), shape((8, U), F32)],
        scratch_shapes=[pltpu.VMEM((2, zs * tn, U), BF16)] * 2,
        compiler_params=PARAMS,
        cost_estimate=cost(0),
        name="unit_grads",
    )(half, n2, n2_other, cot, up, dn, bias, normed, grads)


def local(
    tokens,
    scene_ids,
    norm1_gain,
    norm1_shift,
    qkv_weight,
    qv_bias,
    out_weight,
    out_bias,
    norm2_gain,
    norm2_shift,
    up_weight,
    up_bias,
    down_weight,
    down_bias,
    cotangent,
):
    T, D = tokens.shape
    NW = lax.axis_size("wide")
    N = lax.axis_size("narrow")
    C = out_weight.shape[0]
    hh = C // HEAD_DIM
    U = up_weight.shape[1]
    zs = N // 2
    tn = T // N
    wid = lax.axis_index("wide")
    nid = lax.axis_index("narrow")
    core = wid % 2
    ybit = nid % 2
    zgroups = [list(range(0, N, 2)), list(range(1, N, 2))]
    row = lambda v: v.reshape(1, -1)

    def swap(v, axis, bit):
        size = lax.axis_size(axis)
        return lax.ppermute(v, axis, [(i, i ^ bit) for i in range(size)])

    def wide_scatter(v):
        bit = 1
        while bit < NW:
            pairs = v.reshape((v.shape[0] // 2, 2) + v.shape[1:])
            here = (wid // bit) % 2
            send = lax.dynamic_index_in_dim(pairs, 1 - here, 1, keepdims=False)
            keep = lax.dynamic_index_in_dim(pairs, here, 1, keepdims=False)
            got = swap(send, "wide", bit)
            v = (keep.astype(F32) + got.astype(F32)).astype(v.dtype)
            bit *= 2
        return v[0]

    turn = lambda v, by: lax.ppermute(v, "narrow", [(i, (i + by) % N) for i in range(N)])

    def gather_z(v):
        blocks = [(v, 0)]
        up, down = v, v
        for k in range(1, zs // 2 + 1):
            up = turn(up, 2)
            blocks.append((up, -k))
            if 2 * k < zs:
                down = turn(down, -2)
                blocks.append((down, k))
        return blocks

    def gather_rows(v, *beside):
        blocks = gather_z(v)
        theirs = [swap(block, "narrow", 1) for block, _ in blocks]
        out, total = place(nid.reshape(1), blocks, theirs, v.shape[0] - tn)
        beside = lax.optimization_barrier((*beside, *theirs[1:-1]))[: len(beside)]
        return out.reshape(T, D), total, *beside

    def after(v, *done):
        return lax.optimization_barrier((v,) + done)[0]

    half_at = ybit.reshape(1)
    pack = pack_half(core.reshape(1), up_weight, down_weight, row(up_bias))
    near = swap(pack, "narrow", 1)
    tokens = after(tokens, pack)
    normed, q, mine = project(
        tokens, row(norm1_gain), row(norm1_shift), qkv_weight,
        row(qv_bias), scene_ids.reshape(T // 128, 128), hh,
    )

    kv = {0: mine}
    bit = 2
    while bit < NW:
        for k in list(kv):
            kv[k + bit] = swap(kv[k], "wide", bit)
        bit *= 2
    kv[1] = swap(mine, "wide", 1)

    w_near = swap(
        lax.dynamic_slice_in_dim(after(qkv_weight, mine), core * (D // 2), D // 2, 0), "narrow", 1
    )

    wo_cols = lax.dynamic_slice_in_dim(after(out_weight, mine), wid * (D // NW), D // NW, 1)
    wos = {
        0: lax.all_to_all(
            jnp.broadcast_to(wo_cols[None], (N, C, D // NW)),
            "narrow", split_axis=0, concat_axis=0, tiled=True,
        )
    }
    sums = None
    for k in range(0, NW, 2):
        if k:
            kv[k + 1] = swap(after(kv[k], sums), "wide", 1)
        sums = attend(hh, N, mine, q, [kv[k], kv[k + 1]], sums, k + 2 == NW)
        if k + 2 < NW:
            sums = sums[0]
    sends, mix32, qf = sums

    mix_half = lax.all_to_all(
        after(sends, wos[0], near), "narrow", split_axis=0, concat_axis=0, tiled=True
    )
    wos[0] = after(wos[0], sends)
    bit = 2
    while bit < NW:
        for k in list(wos):
            wos[k + bit] = swap(wos[k], "wide", bit)
        bit *= 2
    for k in list(wos):
        wos[k + 1] = swap(wos[k], "wide", 1)
    far = swap(after(near, sends), "wide", 1)
    w_far = swap(after(w_near, sends), "wide", 1)
    tok4 = tokens.reshape(zs, 2, tn, D)
    cot4 = after(cotangent, sends).reshape(zs, 2, tn, D)
    ga = before_middle(cot4, down_weight, far, near, half_at)
    direct = mm(cot4.reshape(T, D), out_weight, NT)
    mix_half = after(mix_half, direct, ga, w_near)
    a_parts, active, back, normed2, residual, sums2 = middle(
        mix_half, tok4, ga, [wos[k] for k in range(NW)], up_weight, row(up_bias), far, near,
        row(out_bias), row(norm2_gain), row(norm2_shift), half_at, wid.reshape(1),
    )
    arrived = lax.all_to_all(a_parts, "narrow", split_axis=0, concat_axis=0, tiled=True)
    z_at = (nid // 2).reshape(1)
    grad_out, ffs = after_middle(
        active, back, mix_half, cot4, down_weight, far, near, half_at, z_at, NW
    )
    grad_out = wide_scatter(grad_out)
    arrived, ffs = lax.optimization_barrier((arrived, ffs))
    exchange_z = lambda v: lax.all_to_all(
        v, "narrow", split_axis=0, concat_axis=0, tiled=True, axis_index_groups=zgroups
    )
    ffs = exchange_z(ffs)
    normed2_other = swap(after(normed2, arrived), "narrow", 1)
    do, dof = gather_grad(
        hh, arrived.reshape(zs, 2, zs, tn, C), direct.reshape(zs, 2, tn, C), mix32
    )

    dq = None
    come = {k: [] for k in range(0, NW, 2)}
    sent = []
    for k in range(NW - 2, -1, -2):
        dq, other = attend_back(hh, mine, kv[k + 1], q, qf, do, dof, dq, False)
        home = swap(other, "wide", 1)
        if k == 0:
            out_rows = output_rows(z_at, after(ffs, dq, *sent), residual, row(down_bias))
            rows_here = exchange_z(out_rows)
            dq = after(dq, out_rows, normed2_other, grad_out)
        dq, own = attend_back(hh, mine, kv[k], q, qf, do, dof, dq, k == 0)
        parts = [own, home] + come[k]
        if k:
            total = parts[0].astype(F32)
            for part in parts[1:]:
                total += part.astype(F32)
            top = 1 << (k.bit_length() - 1)
            sent = [total.astype(BF16)]
            come[k ^ top].append(swap(sent[0], "wide", top))
    grads, send, grad_sums = collect(hh, half_at, dq, parts, zs)
    other = swap(send, "narrow", 1)
    both, unit_sums = unit_grads(
        half_at, normed2, normed2_other, cot4, up_weight, down_weight, row(up_bias),
        normed, after(grads, send), NW,
    )
    part, back_all = project_back(
        grads, after(other, both, rows_here), qkv_weight, w_near, w_far, tok4, back, row(norm1_gain),
        half_at, core.reshape(1),
    )
    back_all = exchange_z(back_all)
    weights = wide_scatter(after(both, part))

    grad_out = after(grad_out, part).reshape(zs, 2, C, D // NW)
    keep = lax.dynamic_index_in_dim(grad_out, ybit, 1, keepdims=False)
    send = lax.dynamic_index_in_dim(grad_out, 1 - ybit, 1, keepdims=False)
    grad_out = (keep.astype(F32) + swap(send, "narrow", 1).astype(F32)).astype(BF16)
    rows_there = swap(after(rows_here, grad_out), "narrow", 1)
    grad_out_w = 0.0
    for k in range(zs):
        to = lax.dynamic_index_in_dim(grad_out, (nid // 2) ^ k, 0, keepdims=False)
        grad_out_w += (swap(to, "narrow", 2 * k) if k else to).astype(F32)
    vectors = vector_sums(
        hh, NW, part, tok4, sums2, cotangent, unit_sums, grad_sums, half_at, nid.reshape(1)
    )
    vectors = wide_scatter(vectors)
    back_all, vectors = lax.optimization_barrier((back_all, vectors, grad_out_w))[:2]
    token_rows = finish(
        nid.reshape(1), back_all, cotangent, vectors
    )
    grad_tokens, final, rows_there = gather_rows(token_rows, rows_there)
    output = join(half_at, rows_here, rows_there).reshape(T, D)
    size = D // NW
    grad_down_w = weights[:size].astype(F32).T
    grad_up_w = weights[size : 2 * size].astype(F32)
    grad_qkv_w = weights[2 * size :, : 3 * C].astype(F32)
    final = final[:6, : D // NW]
    up_bias_out = vectors[6, : U // NW].reshape(1, -1)
    qv_out = vectors[7, : 2 * C // NW].reshape(1, -1)
    return (
        output,
        grad_tokens,
        final[0],
        final[1],
        grad_qkv_w,
        qv_out,
        grad_out_w,
        final[4],
        final[2],
        final[3],
        grad_up_w,
        up_bias_out,
        grad_down_w,
        final[5],
    )


def solution(mesh):
    in_specs = (
        P("wide", None),
        P("wide"),
        P(),
        P(),
        P(None, "narrow"),
        P("narrow"),
        P("narrow", None),
        P(),
        P(),
        P(),
        P(None, "narrow"),
        P("narrow"),
        P("narrow", None),
        P(),
        P("wide", None),
    )
    out_specs = (
        P("wide", None),
        P("wide", None),
        P("wide"),
        P("wide"),
        P("wide", "narrow"),
        P("narrow", "wide"),
        P("narrow", "wide"),
        P("wide"),
        P("wide"),
        P("wide"),
        P("wide", "narrow"),
        P("narrow", "wide"),
        P("narrow", "wide"),
        P("wide"),
    )
    return jax.shard_map(local, mesh=mesh, in_specs=in_specs, out_specs=out_specs, check_vma=False)
```
